32 devices in a mesh: frame: 8 (over z, x), head: 4 (over y, core).
Axes of the slice: x: 2, y: 2, z: 4, core: 2. Of those that a mesh axis runs over, the one named last changes fastest.
Arguments:
- features: bfloat16 [8, 96, 256, 1536], P(None, 'frame', None, 'head'), may hold values from -6 to 6
- lengths: int32 [8, 96], P(None, 'frame'), may hold values from 64 to 256, as said below
- loss_mask: int32 [8, 96, 256], P(None, 'frame'), may hold values from 0 to 1, as said below
- sq_weight: float32 [5, 1536, 1536], P(None, 'frame', 'head')
- sq_first: float32 [5, 1536, 1536], P(None, 'frame', 'head'), may hold values from -5.340576e-05 to 5.340576e-05
- sq_second: float32 [5, 1536, 1536], P(None, 'frame', 'head'), may hold values from 5.3897747e-11 to 2.1559099e-10
- ffn_weight: float32 [2, 1536, 6144], P(None, 'frame', 'head'), may hold values from -0.15625 to 0.15625
- ffn_first: float32 [2, 1536, 6144], P(None, 'frame', 'head'), may hold values from -5.340576e-05 to 5.340576e-05
- ffn_second: float32 [2, 1536, 6144], P(None, 'frame', 'head'), may hold values from 5.3897747e-11 to 2.1559099e-10
- left_bases: float32 [7, 32, 48, 48], P(None, 'frame'), may hold values from -1 to 1, as said below
- right_sq: float32 [5, 12, 128, 128], P(None, 'head'), may hold values from -1 to 1, as said below
- right_ffn: float32 [2, 48, 128, 128], P(None, 'head'), may hold values from -1 to 1, as said below
- latents: float32 [64, 1536], replicated, may hold values from -6 to 6
- lat_first: float32 [64, 1536], replicated, may hold values from -5.340576e-05 to 5.340576e-05
- lat_second: float32 [64, 1536], replicated, may hold values from 3.3686092e-12 to 1.3474437e-11
- time_embed: float32 [96, 1536], P('frame', 'head'), may hold values from -3 to 3
- time_first: float32 [96, 1536], P('frame', 'head'), may hold values from -5.340576e-05 to 5.340576e-05
- time_second: float32 [96, 1536], P('frame', 'head'), may hold values from 5.3897747e-11 to 2.1559099e-10
- gains: float32 [4, 1536], replicated, may hold values from 0.3 to 2.5
- gain_first: float32 [4, 1536], P(None, 'head'), may hold values from -5.340576e-05 to 5.340576e-05
- gain_second: float32 [4, 1536], P(None, 'head'), may hold values from 5.3897747e-11 to 2.1559099e-10
Outputs:
- loss_sum: float32 [], replicated
- masked_count: float32 [], replicated
- grad_norm: float32 [], replicated
- sq_new: float32 [5, 1536, 1536], P(None, 'frame', 'head')
- sq_first_new: float32 [5, 1536, 1536], P(None, 'frame', 'head')
- sq_second_new: float32 [5, 1536, 1536], P(None, 'frame', 'head')
- sq_low: bfloat16 [5, 1536, 1536], P(None, 'frame', 'head')
- ffn_new: float32 [2, 1536, 6144], P(None, 'frame', 'head')
- ffn_first_new: float32 [2, 1536, 6144], P(None, 'frame', 'head')
- ffn_second_new: float32 [2, 1536, 6144], P(None, 'frame', 'head')
- ffn_low: bfloat16 [2, 1536, 6144], P(None, 'frame', 'head')
- lat_new: float32 [64, 1536], replicated
- lat_first_new: float32 [64, 1536], replicated
- lat_second_new: float32 [64, 1536], replicated
- time_new: float32 [96, 1536], P('frame', 'head')
- time_first_new: float32 [96, 1536], P('frame', 'head')
- time_second_new: float32 [96, 1536], P('frame', 'head')
- gain_new: float32 [4, 1536], P(None, 'head')
- gain_first_new: float32 [4, 1536], P(None, 'head')
- gain_second_new: float32 [4, 1536], P(None, 'head')
The draws below stay inside these ranges and needn't reach their ends.
Inputs may be any that keep to these rules, and one draw needn't show every extreme that they name: `lengths`: some frame has all 256 patches as keys. `loss_mask`: the first patch of every frame counts. `left_bases`: every block is an orthogonal matrix. `right_sq`: every block is an orthogonal matrix. `right_ffn`: every block is an orthogonal matrix.
All inputs are finite; a program needn't handle non-finite values.
Results may differ from the reference program's by a relative error of at most 0.015.
Values may be sent and summed in bfloat16 or wider, within the bound.
No kernel may reach another device: no remote copies, remote signals or barrier semaphores. Data moves between devices by JAX's collectives and lax.ppermute only.
A program may use at most 1 GiB of HBM per device.

```python
import math
import jax
import jax.numpy as jnp
from jax import lax

D = 1536
HEADS = 16
HEAD_SIZE = 96
FF = 6144
LATENTS = 64
PATCH = 256
FRAMES = 96
VIDEOS = 8
BL = 48
BR = 128
STEP = 5
NPARAMS = 30922752


def householder(key, lead, size):
    vectors = jax.random.normal(key, lead + (size,), jnp.float32)
    identity = jnp.eye(size, dtype=jnp.float32)
    return identity - 2.0 * vectors[..., :, None] * vectors[..., None, :] / jnp.sum(vectors * vectors, -1)[..., None, None]


def draw_left_bases(key, part):
    key = jax.random.fold_in(key, 11)
    return householder(key, (7, D // BL), BL)


def draw_right_sq(key, part):
    key = jax.random.fold_in(key, 12)
    return householder(key, (5, D // BR), BR)


def draw_right_ffn(key, part):
    key = jax.random.fold_in(key, 13)
    return householder(key, (2, FF // BR), BR)


def draw_lengths(key, part):
    key = jax.random.fold_in(key, 14)
    key_one, key_two = jax.random.split(key)
    drawn = jax.random.randint(key_one, (VIDEOS, FRAMES), PATCH // 4, PATCH + PATCH // 2)
    place = jax.random.randint(key_two, (), 0, FRAMES)
    return jnp.minimum(drawn, PATCH).at[0, place].set(PATCH).astype(jnp.int32)


def draw_loss_mask(key, part):
    key = jax.random.fold_in(key, 15)
    frame_ids = lax.broadcasted_iota(jnp.int32, (VIDEOS, FRAMES, PATCH), 1)
    patch_ids = lax.broadcasted_iota(jnp.int32, (VIDEOS, FRAMES, PATCH), 2)
    thresh = 250 + 500 * frame_ids // max(FRAMES - 1, 1)
    rolled = jax.random.randint(key, (VIDEOS, FRAMES, PATCH), 0, 1000)
    return ((rolled < thresh) | (patch_ids == 0)).astype(jnp.int32)


def draw_gains(key, part):
    key = jax.random.fold_in(key, 16)
    ramped = lax.broadcasted_iota(jnp.float32, (4, D), 1) / (D - 1)
    return (0.6 + 1.2 * ramped) * jax.random.uniform(key, (4, D), jnp.float32, 0.85, 1.15)


def draw_sq_weight(key, part):
    key = jax.random.fold_in(key, 17)
    out_scale = ((FRAMES * PATCH + LATENTS) / 64.0) ** 0.5
    scales = jnp.array([1.0, 1.0, 1.0, out_scale, 1.0], jnp.float32) * D ** (-0.5)
    sample = jax.random.normal(key, (5, D, D), jnp.float32)
    return sample * scales[:, None, None]


def levels(stream_key, dims, cuts, smallest, largest):
    factor_of, own = 1.0, jax.random.fold_in(stream_key, 6)
    for dim, parts in cuts:
        heights = jnp.exp(jax.random.uniform(jax.random.fold_in(own, dim), (parts,), jnp.float32, smallest / len(cuts), largest / len(cuts)))
        factor_of = factor_of * jnp.repeat(heights, dims[dim] // parts).reshape([-1 if axis == dim else 1 for axis in range(len(dims))])
    return factor_of


def normal_values(own_key, shape, deviation, reach, cuts=(), kind=jnp.bfloat16):
    factor_of = levels(own_key, shape, cuts, -0.22, 0.18) if cuts else 1.0
    values = jax.random.normal(own_key, shape, jnp.float32) * deviation * factor_of
    return jnp.minimum(jnp.maximum(values, -reach), reach).astype(kind)


def setup_inputs(seed: int = 0) -> dict:
    key_list = jax.random.split(jax.random.key(seed), 22)
    features = normal_values(key_list[0], (VIDEOS, FRAMES, PATCH, D), 1.0, 6.0, ((1, 8), (3, 4)))
    lengths = draw_lengths(jax.random.fold_in(key_list[21], 71), 0)
    loss_mask = draw_loss_mask(jax.random.fold_in(key_list[21], 71), 0)
    sq_weight = draw_sq_weight(jax.random.fold_in(key_list[21], 71), 0)
    sq_first = normal_values(key_list[4], (5, D, D), ((400 * NPARAMS) ** -0.5), 5.340576171875e-05, ((1, 8), (2, 4)), jnp.float32)
    sq_second = jnp.clip(jnp.exp(math.log(2.1559098950518774e-10) - 1.3862944 * jax.random.uniform(key_list[5], (5, D, D), jnp.float32) ** levels(key_list[5], (5, D, D), ((1, 8), (2, 4)), -0.2, 0.2)), 5.3897747376296934e-11, 2.1559098950518774e-10)
    ffn_weight = normal_values(key_list[6], (2, D, FF), D ** -0.5, 0.15625, ((1, 8), (2, 4)), jnp.float32)
    ffn_first = normal_values(key_list[7], (2, D, FF), ((400 * NPARAMS) ** -0.5), 5.340576171875e-05, ((1, 8), (2, 4)), jnp.float32)
    ffn_second = jnp.clip(jnp.exp(math.log(2.1559098950518774e-10) - 1.3862944 * jax.random.uniform(key_list[8], (2, D, FF), jnp.float32) ** levels(key_list[8], (2, D, FF), ((1, 8), (2, 4)), -0.2, 0.2)), 5.3897747376296934e-11, 2.1559098950518774e-10)
    left_bases = draw_left_bases(jax.random.fold_in(key_list[21], 71), 0)
    right_sq = draw_right_sq(jax.random.fold_in(key_list[21], 71), 0)
    right_ffn = draw_right_ffn(jax.random.fold_in(key_list[21], 71), 0)
    latents = normal_values(key_list[12], (LATENTS, D), 1.0, 6.0, (), jnp.float32)
    lat_first = normal_values(key_list[13], (LATENTS, D), ((400 * NPARAMS) ** -0.5), 5.340576171875e-05, (), jnp.float32)
    lat_second = jnp.clip(jnp.exp(jax.random.uniform(key_list[14], (LATENTS, D), jnp.float32, math.log(3.3686092110185584e-12), math.log(1.3474436844074233e-11))), 3.3686092110185584e-12, 1.3474436844074233e-11)
    time_embed = normal_values(key_list[15], (FRAMES, D), 0.5, 3.0, ((0, 8), (1, 4)), jnp.float32)
    time_first = normal_values(key_list[16], (FRAMES, D), ((400 * NPARAMS) ** -0.5), 5.340576171875e-05, ((0, 8), (1, 4)), jnp.float32)
    time_second = jnp.clip(jnp.exp(math.log(2.1559098950518774e-10) - 1.3862944 * jax.random.uniform(key_list[17], (FRAMES, D), jnp.float32) ** levels(key_list[17], (FRAMES, D), ((0, 8), (1, 4)), -0.2, 0.2)), 5.3897747376296934e-11, 2.1559098950518774e-10)
    gains = draw_gains(jax.random.fold_in(key_list[21], 71), 0)
    gain_first = normal_values(key_list[19], (4, D), ((400 * NPARAMS) ** -0.5), 5.340576171875e-05, ((1, 4),), jnp.float32)
    gain_second = jnp.clip(jnp.exp(math.log(2.1559098950518774e-10) - 1.3862944 * jax.random.uniform(key_list[20], (4, D), jnp.float32) ** levels(key_list[20], (4, D), ((1, 4),), -0.2, 0.2)), 5.3897747376296934e-11, 2.1559098950518774e-10)
    return {"features": features, "lengths": lengths, "loss_mask": loss_mask, "sq_weight": sq_weight, "sq_first": sq_first, "sq_second": sq_second, "ffn_weight": ffn_weight, "ffn_first": ffn_first, "ffn_second": ffn_second, "left_bases": left_bases, "right_sq": right_sq, "right_ffn": right_ffn, "latents": latents, "lat_first": lat_first, "lat_second": lat_second, "time_embed": time_embed, "time_first": time_first, "time_second": time_second, "gains": gains, "gain_first": gain_first, "gain_second": gain_second}


@jax.custom_vjp
def low(v):
    return lax.optimization_barrier(v.astype(jnp.bfloat16)).astype(jnp.float32)

@jax.custom_vjp
def low_back(v):
    return v

def low_keep(v):
    return (low(v), None)

def low_pass(kept, grad):
    return (grad,)

def back_keep(v):
    return (v, None)

def back_low(kept, grad):
    return (low(grad),)
low.defvjp(low_keep, low_pass)
low_back.defvjp(back_keep, back_low)
HIGH_ACCURACY = lax.Precision.HIGHEST
clip_max = 0.05
beta_one = 0.5
beta_two = 0.6
adam_eps = 1e-08

def round_both(v):
    return low(low_back(v))

def hdot(a, b):
    return jnp.dot(a, b, precision=HIGH_ACCURACY)

def layer_norm(v, norm_gain):
    cent = v - lax.optimization_barrier(jnp.mean(v, -1, keepdims=True))
    return cent * lax.rsqrt(lax.optimization_barrier(jnp.mean(cent * cent, -1, keepdims=True)) + 1e-05) * norm_gain

def forward(sq_weight, ffn_weight, latents, time_embed, gains, features, lengths, loss_mask):
    w_query, w_key, w_value, w_outt, w_dec = [low(sq_weight[slab]) for slab in range(5)]
    w_up, w_downt = (low(ffn_weight[0]), low(ffn_weight[1]))
    inv_root = HEAD_SIZE ** (-0.5)
    normed_lat = low(layer_norm(latents, gains[1]))
    query = round_both(hdot(normed_lat, w_query)).reshape(LATENTS, HEADS, HEAD_SIZE)
    latent_key = round_both(hdot(normed_lat, w_key))
    latent_value = round_both(hdot(normed_lat, w_value))

    def one_video(carry, video_inputs):
        patch_feat, frame_lens, count_mask = video_inputs
        feat_float = patch_feat.astype(jnp.float32)
        summed = low(feat_float + time_embed[:, None, :]).reshape(-1, D)
        normalized_input = low(layer_norm(summed, gains[0]))
        key_x = round_both(hdot(normalized_input, w_key))
        val_x = round_both(hdot(normalized_input, w_value))
        valid_key = (lax.broadcasted_iota(jnp.int32, (FRAMES, PATCH), 1) < frame_lens[:, None]).reshape(-1)
        keep = jnp.concatenate([valid_key, jnp.ones((LATENTS,), bool)])
        keys_all = jnp.concatenate([key_x, latent_key]).reshape(-1, HEADS, HEAD_SIZE)
        vals_all = jnp.concatenate([val_x, latent_value]).reshape(-1, HEADS, HEAD_SIZE)
        scores = jnp.einsum('lhd,nhd->hln', query, keys_all, precision=HIGH_ACCURACY) * inv_root
        probs = jax.nn.softmax(jnp.where(keep[None, None, :], scores, -1e+30), -1)
        attn = jnp.einsum('hln,nhd->lhd', probs, vals_all, precision=HIGH_ACCURACY).reshape(LATENTS, D)
        z_one = latents + low_back(hdot(low(attn), w_outt.T))
        pre = low_back(hdot(low(layer_norm(z_one, gains[2])), w_up))
        z_two = z_one + low_back(hdot(low(jax.nn.gelu(pre)), w_downt.T))
        final = low(layer_norm(z_two, gains[3]))
        dec_query = round_both(hdot(final, w_query)).reshape(LATENTS, HEADS, HEAD_SIZE)
        dec_value = round_both(hdot(final, w_dec)).reshape(LATENTS, HEADS, HEAD_SIZE)
        dscores = jnp.einsum('nhd,lhd->nhl', key_x.reshape(-1, HEADS, HEAD_SIZE), dec_query, precision=HIGH_ACCURACY) * inv_root
        dprobs = jax.nn.softmax(dscores, -1)
        pred = jnp.einsum('nhl,lhd->nhd', dprobs, dec_value, precision=HIGH_ACCURACY).reshape(FRAMES, PATCH, D)
        error_pred = pred - feat_float
        return (carry + jnp.sum(count_mask.astype(jnp.float32)[..., None] * error_pred * error_pred), None)
    loss_sum, _ = lax.scan(jax.checkpoint(one_video), jnp.zeros((), jnp.float32), (features, lengths, loss_mask))
    return loss_sum

def rotate(gradient_tensor, left_basis, right_basis, inverse):
    slabs, row_count, col_count = gradient_tensor.shape
    bl = left_basis.shape[-1]
    br = right_basis.shape[-1]
    blocks = gradient_tensor.reshape(slabs, row_count // bl, bl, col_count // br, br)
    if inverse:
        out = jnp.einsum('maij,majcl,mckl->maick', left_basis, blocks, right_basis, precision=HIGH_ACCURACY)
    else:
        out = jnp.einsum('maij,maick,mckl->majcl', left_basis, blocks, right_basis, precision=HIGH_ACCURACY)
    return out.reshape(slabs, row_count, col_count)

def adam_moments(gradient_tensor, moment_one, moment_two):
    moment_one = beta_one * moment_one + (1.0 - beta_one) * gradient_tensor
    moment_two = beta_two * moment_two + (1.0 - beta_two) * gradient_tensor * gradient_tensor
    adam_step = moment_one / (1.0 - beta_one ** STEP) / (jnp.sqrt(moment_two / (1.0 - beta_two ** STEP)) + adam_eps)
    return (moment_one, moment_two, adam_step)

def soap_update(weight, gradient_tensor, moment_one, moment_two, left_basis, right_basis, rates):
    moment_one, moment_two, adam_step = adam_moments(rotate(gradient_tensor, left_basis, right_basis, False), moment_one, moment_two)
    updated = weight - rates[:, None, None] * (rotate(adam_step, left_basis, right_basis, True) + 0.01 * weight)
    return (updated, moment_one, moment_two, updated.astype(jnp.bfloat16))

def adamw_update(weight, gradient_tensor, moment_one, moment_two, decay):
    moment_one, moment_two, adam_step = adam_moments(gradient_tensor, moment_one, moment_two)
    return (weight - 0.3 * (adam_step + decay * weight), moment_one, moment_two)

def reference(features, lengths, loss_mask, sq_weight, sq_first, sq_second, ffn_weight, ffn_first, ffn_second, left_bases, right_sq, right_ffn, latents, lat_first, lat_second, time_embed, time_first, time_second, gains, gain_first, gain_second):

    def loss_of(sq_w, ffn_w, lat_w, time_w, gain_w):
        return forward(sq_w, ffn_w, lat_w, time_w, gain_w, features, lengths, loss_mask)
    loss_sum, back = jax.vjp(loss_of, sq_weight, ffn_weight, latents, time_embed, gains)
    grads = back(jnp.ones((), jnp.float32))
    masked_count = jnp.sum(loss_mask.astype(jnp.float32))
    squares = sum((jnp.sum(item * item) for item in grads))
    grad_norm = jnp.sqrt(squares) / masked_count
    factor = jnp.minimum(1.0, clip_max / grad_norm) / masked_count
    g_sq, g_ffn, g_lat, g_time, g_gain = [item * factor for item in grads]
    out_rate = ((FRAMES * PATCH + LATENTS) / 64.0) ** 0.5
    sq_rates = jnp.array([1.0, 1.0, 1.0, out_rate, 1.0], jnp.float32) * 0.02
    ffn_rates = jnp.array([0.02, 0.02], jnp.float32)
    sq_out = soap_update(sq_weight, g_sq, sq_first, sq_second, left_bases[:5], right_sq, sq_rates)
    ffn_out = soap_update(ffn_weight, g_ffn, ffn_first, ffn_second, left_bases[5:], right_ffn, ffn_rates)
    lat_out = adamw_update(latents, g_lat, lat_first, lat_second, 0.01)
    time_out = adamw_update(time_embed, g_time, time_first, time_second, 0.01)
    gain_out = adamw_update(gains, g_gain, gain_first, gain_second, 0.0)
    return (loss_sum, masked_count, grad_norm, sq_out[0], sq_out[1], sq_out[2], sq_out[3], ffn_out[0], ffn_out[1], ffn_out[2], ffn_out[3], lat_out[0], lat_out[1], lat_out[2], time_out[0], time_out[1], time_out[2], gain_out[0], gain_out[1], gain_out[2])
```

```python
import functools

import jax
import jax.numpy as jnp
from jax import lax
from jax.experimental import pallas as pl
from jax.experimental.pallas import tpu as pltpu
from jax.sharding import PartitionSpec as P

HEAD_SIZE = 96
LATENTS = 64
PATCH = 256
FRAMES = 96
STEP = 5
GROUP = 4
EXTRA = 128
TAIL = 16
VMEM_BYTES = 58 * 1024 * 1024

HIGH_ACCURACY = lax.Precision.HIGHEST
clip_max = 0.05
beta_one = 0.5
beta_two = 0.6
adam_eps = 1e-08
f32 = jnp.float32
bf16 = jnp.bfloat16


def nn(a, b):
    return lax.dot_general(a, b, (((1,), (0,)), ((), ())), preferred_element_type=f32)


def nt(a, b):
    return lax.dot_general(a, b, (((1,), (1,)), ((), ())), preferred_element_type=f32)


def tn(a, b):
    return lax.dot_general(a, b, (((0,), (0,)), ((), ())), preferred_element_type=f32)


def normalize_rows(v):
    cent = v - jnp.mean(v, -1, keepdims=True)
    rstd = lax.rsqrt(jnp.mean(cent * cent, -1, keepdims=True) + 1e-05)
    return (cent * rstd, rstd)


def norm_reverse(dy, xhat, rstd, gain):
    scaled = dy * gain
    first = jnp.mean(scaled, -1, keepdims=True)
    second = jnp.mean(scaled * xhat, -1, keepdims=True)
    return rstd * (scaled - first - xhat * second)


def rotate(grad, left, right, inverse):
    slabs, rows, cols = grad.shape
    bl = left.shape[-1]
    br = right.shape[-1]
    blocks = grad.reshape(slabs, rows // bl, bl, cols // br, br)
    if inverse:
        out = jnp.einsum("maij,majcl,mckl->maick", left, blocks, right, precision=HIGH_ACCURACY)
    else:
        out = jnp.einsum("maij,maick,mckl->majcl", left, blocks, right, precision=HIGH_ACCURACY)
    return out.reshape(slabs, rows, cols)


def adam_moments(grad, one, two):
    one = beta_one * one + (1.0 - beta_one) * grad
    two = beta_two * two + (1.0 - beta_two) * grad * grad
    step = one / (1.0 - beta_one**STEP) / (jnp.sqrt(two / (1.0 - beta_two**STEP)) + adam_eps)
    return (one, two, step)


def soap_update(weight, grad, one, two, left, right, rates):
    one, two, step = adam_moments(rotate(grad, left, right, False), one, two)
    updated = weight - rates[:, None, None] * (rotate(step, left, right, True) + 0.01 * weight)
    return (updated, one, two, updated.astype(bf16))


def adamw_update(weight, grad, one, two, decay):
    one, two, step = adam_moments(grad, one, two)
    return (weight - 0.3 * (step + decay * weight), one, two)


def swap(x, axis, bit):
    size = lax.axis_size(axis)
    return lax.ppermute(x, axis, [(i, i ^ bit) for i in range(size)])


def sum_over(x, axis):
    bit = 1
    while bit < lax.axis_size(axis):
        x = x + swap(x, axis, bit)
        bit *= 2
    return x


def sum_head(x):
    x = x + swap(x, "head", 1)
    x = lax.reduce_precision(x, 8, 7)
    return x + swap(x.astype(bf16), "head", 2).astype(f32)


def split_three(x):
    high = lax.reduce_precision(x, 8, 7)
    rest = x - high
    mid = lax.reduce_precision(rest, 8, 7)
    return jnp.concatenate([high, mid, rest - mid], -1).astype(bf16)


def join_three(x):
    n = x.shape[-1] // 3
    x = x.astype(f32)
    return x[..., :n] + x[..., n : 2 * n] + x[..., 2 * n :]


def head_of_lane(rows, cols):
    return lax.broadcasted_iota(jnp.int32, (rows, cols), 1) // HEAD_SIZE


def spread(x):
    owner = head_of_lane(*x.shape)
    x = x.astype(f32)
    return jnp.concatenate([jnp.where(owner == j, x, 0.0) for j in range(GROUP)], 0).astype(bf16)


def collect(r):
    rows = r.shape[0] // GROUP
    owner = head_of_lane(rows, r.shape[1])
    out = jnp.where(owner == 0, r[:rows], 0.0)
    for j in range(1, GROUP):
        out = out + jnp.where(owner == j, r[j * rows : (j + 1) * rows], 0.0)
    return out


def whole(shape):
    return pl.BlockSpec(shape, lambda *_: (0,) * len(shape), pipeline_mode=pl.Buffered(1))


def kernel_absorb(scale, x_ref, w_ref, out_ref):
    out_ref[...] = (nt(spread(x_ref[...]), w_ref[...]) * scale).astype(bf16)


def absorb(x, w, scale):
    depth, width = w.shape
    cols = GROUP * HEAD_SIZE
    groups = width // cols
    rows = GROUP * LATENTS
    return pl.pallas_call(
        functools.partial(kernel_absorb, scale),
        grid=(groups,),
        in_specs=[
            pl.BlockSpec((LATENTS, cols), lambda g: (0, g)),
            pl.BlockSpec((depth, cols), lambda g: (0, g)),
        ],
        out_specs=pl.BlockSpec((rows, depth), lambda g: (g, 0)),
        out_shape=jax.ShapeDtypeStruct((groups * rows, depth), bf16),
        compiler_params=pltpu.CompilerParams(vmem_limit_bytes=VMEM_BYTES),
        name="absorb",
    )(x, w)


def kernel_read(
    nf, place, own, ra, rb, rc, time_ref, g0, qw, wv, xn_in, e_in, px_in, st_in, o_in,
    xn_o, e_o, px_o, st_o, o_o, xs, acc, run,
):
    del xn_in, e_in, px_in, st_in, o_in
    i = pl.program_id(0)
    tokens, depth = xs.shape
    cols = own.shape[1]
    heads_rows = GROUP * LATENTS
    groups = qw.shape[0] // heads_rows

    @pl.when(i == 0)
    def _():
        acc[...] = jnp.zeros_like(acc)
        run[0] = jnp.full(run.shape[1:], -1e30, f32)
        run[1] = jnp.zeros(run.shape[1:], f32)
        st_o[...] = jnp.zeros_like(st_o)

    for k, part in enumerate((own, ra, rb, rc)):
        off = pl.multiple_of((place[0] ^ k) * cols, 128)
        for f in range(nf):
            rows = slice(f * PATCH, (f + 1) * PATCH)
            moved = part[rows, :].astype(f32) + time_ref[pl.ds(i * nf + f, 1), pl.ds(off, cols)]
            xs[rows, pl.ds(off, cols)] = moved.astype(bf16)
    x = xs[...].astype(f32)
    cent = x - jnp.sum(x, -1, keepdims=True) * (1.0 / depth)
    rstd = lax.rsqrt(jnp.sum(cent * cent, -1, keepdims=True) * (1.0 / depth) + 1e-05)
    xn_o[:, :depth] = (cent * rstd * g0[...]).astype(bf16)
    lane = lax.broadcasted_iota(jnp.int32, (tokens, EXTRA), 1)
    frame = lax.broadcasted_iota(jnp.int32, (tokens, EXTRA), 0) // PATCH + i * nf
    xn_o[:, depth:] = jnp.where(lane == frame, rstd, 0.0).astype(bf16)
    key = lax.broadcasted_iota(jnp.int32, (1, tokens), 1)
    limit = place[1 + i * nf]
    for f in range(1, nf):
        limit = jnp.where(key >= f * PATCH, f * PATCH + place[1 + i * nf + f], limit)
    valid = key < limit
    block = lax.broadcasted_iota(jnp.int32, (heads_rows, 128), 1)
    last = i == pl.num_programs(0) - 1
    for g in range(groups):
        rows = slice(g * heads_rows, (g + 1) * heads_rows)
        scores = jnp.where(valid, nt(qw[rows, :], xn_o[:, :depth]), -1e30)
        old = run[0, rows, :]
        new = jnp.maximum(old, jnp.max(scores, -1, keepdims=True))
        expo = jnp.exp(scores - new[:, :1])
        shrink = jnp.exp(old - new)
        total = run[1, rows, :] * shrink + jnp.sum(expo, -1, keepdims=True)
        run[0, rows, :] = new
        run[1, rows, :] = total
        low = expo.astype(bf16)
        e_o[rows, :] = low
        stats = jnp.where(block == i, new, st_o[rows, :])
        stats = jnp.where(last & (block == 126), new, stats)
        st_o[rows, :] = jnp.where(last & (block == 127), total, stats)
        acc[rows, :] = acc[rows, :] * shrink[:, :1] + nn(low, xn_o[...])

    @pl.when(last)
    def _():
        for g in range(groups):
            rows = slice(g * heads_rows, (g + 1) * heads_rows)
            wide = slice(g * cols, (g + 1) * cols)
            held = acc[rows, :].astype(bf16)
            px_o[rows, :] = held
            mixed = nn(held[:, :depth], wv[:, wide]) / run[1, rows, :1]
            o_o[:, wide] = collect(mixed)


def read_pass(j, prev, feat, got, time_full, gain, lens, qw, wv, h, videos_dev):
    count, tokens_video, cols = feat.shape
    depth = wv.shape[0]
    frames_dev = tokens_video // PATCH
    nf = 2 if frames_dev % 2 == 0 else 1
    tokens = nf * PATCH
    blocks = frames_dev // nf
    rows = qw.shape[0]
    place = jnp.concatenate([h[None], lens]).astype(jnp.int32)
    feat2 = feat.reshape(count * tokens_video, cols)
    shapes = (
        jax.ShapeDtypeStruct((videos_dev * tokens_video, depth + EXTRA), bf16),
        jax.ShapeDtypeStruct((videos_dev * rows, tokens_video), bf16),
        jax.ShapeDtypeStruct((videos_dev * rows, depth + EXTRA), bf16),
        jax.ShapeDtypeStruct((videos_dev * rows, 128), f32),
        jax.ShapeDtypeStruct((videos_dev * LATENTS, depth), f32),
    )
    aliases = {}
    if prev is None:
        prev = [jnp.zeros((8, 128), s.dtype) for s in shapes]
    else:
        aliases = {9 + n: n for n in range(5)}
    anyspec = pl.BlockSpec(memory_space=pl.ANY)
    return pl.pallas_call(
        functools.partial(kernel_read, nf),
        grid_spec=pltpu.PrefetchScalarGridSpec(
            num_scalar_prefetch=1,
            grid=(blocks,),
            in_specs=[
                pl.BlockSpec((tokens, cols), lambda i, p: ((p[0] * videos_dev + j) * blocks + i, 0)),
                pl.BlockSpec((tokens, cols), lambda i, p: (i, 0)),
                pl.BlockSpec((tokens, cols), lambda i, p: (i, 0)),
                pl.BlockSpec((tokens, cols), lambda i, p: (i, 0)),
                whole(time_full.shape),
                whole(gain.shape),
                whole(qw.shape),
                whole(wv.shape),
                anyspec, anyspec, anyspec, anyspec, anyspec,
            ],
            out_specs=[
                pl.BlockSpec((tokens, depth + EXTRA), lambda i, p: (j * blocks + i, 0)),
                pl.BlockSpec((rows, tokens), lambda i, p: (j, i)),
                pl.BlockSpec((rows, depth + EXTRA), lambda i, p: (j, 0), pipeline_mode=pl.Buffered(1)),
                pl.BlockSpec((rows, 128), lambda i, p: (j, 0), pipeline_mode=pl.Buffered(1)),
                pl.BlockSpec((LATENTS, depth), lambda i, p: (j, 0), pipeline_mode=pl.Buffered(1)),
            ],
            scratch_shapes=[
                pltpu.VMEM((tokens, depth), bf16),
                pltpu.VMEM((rows, depth + EXTRA), f32),
                pltpu.VMEM((2, rows, 128), f32),
            ],
        ),
        out_shape=shapes,
        input_output_aliases=aliases,
        compiler_params=pltpu.CompilerParams(vmem_limit_bytes=VMEM_BYTES),
        cost_estimate=pl.CostEstimate(
            flops=4 * rows * tokens_video * depth,
            bytes_accessed=tokens_video * depth * 8,
            transcendentals=rows * tokens_video,
        ),
        name="read_pass",
    )(place, feat2, *got, time_full, gain, qw, wv, *prev)


def kernel_decode(
    nf, scale, place, xn, own, ra, rb, rc, msk, dq, dv, wk,
    ddq_o, ddv_o, dx_o, side_o, loss_o, dqw, dvd, sc, zs, acc, dacc, loss,
):
    i = pl.program_id(0)
    tokens = xn.shape[0]
    depth = wk.shape[0]
    cols = own.shape[1]
    heads_rows = GROUP * LATENTS
    groups = dqw.shape[0] // heads_rows
    total_rows = dqw.shape[0]

    @pl.when(i == 0)
    def _():
        acc[...] = jnp.zeros_like(acc)
        dacc[...] = jnp.zeros_like(dacc)
        loss[...] = jnp.zeros_like(loss)
        for g in range(groups):
            rows = slice(g * heads_rows, (g + 1) * heads_rows)
            wide = slice(g * cols, (g + 1) * cols)
            dqw[rows, :] = (nt(spread(dq[:, wide]), wk[:, wide]) * scale).astype(bf16)
            dvd[g] = spread(dv[:, wide])

    sc[...] = nt(dqw[...], xn[:, :depth]).reshape(groups, heads_rows, tokens)
    counts = msk[...]
    second = jnp.zeros((1, tokens), f32)
    for k, part in enumerate((own, ra, rb, rc)):
        g = place[0] ^ k
        s = sc[g].reshape(GROUP, LATENTS, tokens)
        a = jnp.exp(s - jnp.max(s, 1, keepdims=True))
        a = a / jnp.sum(a, 1, keepdims=True)
        low = a.reshape(heads_rows, tokens).astype(bf16)
        error = tn(low, dvd[g]) - part[...].astype(f32)
        kept = counts * error
        loss[...] += jnp.sum((kept * error).reshape(tokens // 8, 8, cols), 0)
        dp = (2.0 * kept).astype(bf16)
        dacc[g] += nn(low, dp)
        da = nt(dvd[g], dp).reshape(GROUP, LATENTS, tokens)
        z = a * (da - jnp.sum(a * da, 1, keepdims=True))
        second = second + jnp.sum((z * s).reshape(heads_rows, tokens), 0, keepdims=True)
        zs[pl.ds(pl.multiple_of(g * heads_rows, heads_rows), heads_rows), :] = z.reshape(
            heads_rows, tokens
        ).astype(bf16)
    zs[pl.ds(total_rows, TAIL), :] = tail_rows(nf, i, second, xn, depth)
    acc[...] += nn(zs[...], xn[...])

    @pl.when(i == pl.num_programs(0) - 1)
    def _():
        gain = jnp.zeros((8, depth), f32)
        for g in range(groups):
            rows = slice(g * heads_rows, (g + 1) * heads_rows)
            wide = slice(g * cols, (g + 1) * cols)
            held = acc[rows, :depth]
            low = held.astype(bf16)
            dx_o[rows, :] = low
            ddq_o[:, wide] = collect(nn(low, wk[:, wide])) * scale
            ddv_o[:, wide] = collect(dacc[g])
            gain = gain + jnp.sum(
                (held * dqw[rows, :].astype(f32)).reshape(heads_rows // 8, 8, depth), 0
            )
        side_o[0:TAIL, :] = tn(acc[:total_rows, depth:].astype(bf16), dqw[...])[:TAIL]
        side_o[TAIL : 2 * TAIL, :] = acc[total_rows:, :depth]
        side_o[2 * TAIL :, :] = gain
        loss_o[...] = loss[...]


def tail_rows(nf, i, second, xn, depth):
    tokens = xn.shape[0]
    rstd = nt(jnp.ones((TAIL, EXTRA), bf16), xn[:, depth:])
    row = lax.broadcasted_iota(jnp.int32, (TAIL, tokens), 0)
    frame = lax.broadcasted_iota(jnp.int32, (TAIL, tokens), 1) // PATCH + i * nf
    return jnp.where(row == frame, rstd * second * (1.0 / depth), 0.0).astype(bf16)


def decode_pass(j, xn_all, feat, got, counts, dq_all, dv_all, wk, h, scale, videos_dev):
    count, tokens_video, cols = feat.shape
    depth = wk.shape[0]
    frames_dev = tokens_video // PATCH
    nf = 2 if frames_dev % 2 == 0 else 1
    tokens = nf * PATCH
    blocks = frames_dev // nf
    groups = depth // cols
    heads_rows = GROUP * LATENTS
    rows = groups * heads_rows
    feat2 = feat.reshape(count * tokens_video, cols)
    return pl.pallas_call(
        functools.partial(kernel_decode, nf, scale),
        grid_spec=pltpu.PrefetchScalarGridSpec(
            num_scalar_prefetch=1,
            grid=(blocks,),
            in_specs=[
                pl.BlockSpec((tokens, depth + EXTRA), lambda i, p: (j * blocks + i, 0)),
                pl.BlockSpec((tokens, cols), lambda i, p: ((p[0] * videos_dev + j) * blocks + i, 0)),
                pl.BlockSpec((tokens, cols), lambda i, p: (i, 0)),
                pl.BlockSpec((tokens, cols), lambda i, p: (i, 0)),
                pl.BlockSpec((tokens, cols), lambda i, p: (i, 0)),
                pl.BlockSpec((tokens, 1), lambda i, p: (j * blocks + i, 0)),
                pl.BlockSpec((LATENTS, depth), lambda i, p: (j, 0), pipeline_mode=pl.Buffered(1)),
                pl.BlockSpec((LATENTS, depth), lambda i, p: (j, 0), pipeline_mode=pl.Buffered(1)),
                whole(wk.shape),
            ],
            out_specs=[
                whole((LATENTS, depth)),
                whole((LATENTS, depth)),
                whole((rows, depth)),
                whole((2 * TAIL + 8, depth)),
                whole((8, cols)),
            ],
            scratch_shapes=[
                pltpu.VMEM((rows, depth), bf16),
                pltpu.VMEM((groups, heads_rows, cols), bf16),
                pltpu.VMEM((groups, heads_rows, tokens), f32),
                pltpu.VMEM((rows + TAIL, tokens), bf16),
                pltpu.VMEM((rows + TAIL, depth + EXTRA), f32),
                pltpu.VMEM((groups, heads_rows, cols), f32),
                pltpu.VMEM((8, cols), f32),
            ],
        ),
        out_shape=(
            jax.ShapeDtypeStruct((LATENTS, depth), f32),
            jax.ShapeDtypeStruct((LATENTS, depth), f32),
            jax.ShapeDtypeStruct((rows, depth), bf16),
            jax.ShapeDtypeStruct((2 * TAIL + 8, depth), f32),
            jax.ShapeDtypeStruct((8, cols), f32),
        ),
        compiler_params=pltpu.CompilerParams(vmem_limit_bytes=VMEM_BYTES),
        cost_estimate=pl.CostEstimate(
            flops=6 * rows * tokens_video * depth,
            bytes_accessed=tokens_video * depth * 4,
            transcendentals=rows * tokens_video,
        ),
        name="decode_pass",
    )(jnp.full((1,), h, jnp.int32), xn_all, feat2, *got, counts, dq_all, dv_all, wk)


def kernel_value(do, wv, px, st, ld, ow_o, dwv_o, side_o, acc):
    g = pl.program_id(0)
    v = pl.program_id(1)
    depth = wv.shape[0]

    @pl.when((g == 0) & (v == 0))
    def _():
        side_o[...] = jnp.zeros_like(side_o)

    diag = spread(do[...])
    ow = nt(diag, wv[...]).astype(bf16)
    ow_o[...] = ow
    norm = px[...].astype(f32) * jnp.exp(st[:, 126:127] - ld[:, 0:1])
    low = norm.astype(bf16)
    part = tn(diag, low[:, :depth])

    @pl.when(v == 0)
    def _():
        acc[...] = part

    @pl.when(v > 0)
    def _():
        acc[...] += part

    dwv_o[...] = acc[...].astype(bf16)
    side_o[0:TAIL, :] += tn(low[:, depth:], ow)[:TAIL]
    rows = ow.shape[0]
    side_o[TAIL:, :] += jnp.sum((ow.astype(f32) * norm[:, :depth]).reshape(rows // 8, 8, depth), 0)


def value_pass(do_all, wv, px_all, st_all, ld, videos_dev):
    depth = wv.shape[0]
    cols = GROUP * HEAD_SIZE
    groups = depth // cols
    rows = GROUP * LATENTS
    return pl.pallas_call(
        kernel_value,
        grid=(groups, videos_dev),
        in_specs=[
            pl.BlockSpec((LATENTS, cols), lambda g, v: (v, g)),
            pl.BlockSpec((depth, cols), lambda g, v: (0, g)),
            pl.BlockSpec((rows, depth + EXTRA), lambda g, v: (v * groups + g, 0)),
            pl.BlockSpec((rows, 128), lambda g, v: (v * groups + g, 0)),
            pl.BlockSpec((rows, 128), lambda g, v: (v * groups + g, 0)),
        ],
        out_specs=[
            pl.BlockSpec((rows, depth), lambda g, v: (v * groups + g, 0)),
            pl.BlockSpec((cols, depth), lambda g, v: (g, 0)),
            pl.BlockSpec((TAIL + 8, depth), lambda g, v: (0, 0)),
        ],
        out_shape=(
            jax.ShapeDtypeStruct((videos_dev * groups * rows, depth), bf16),
            jax.ShapeDtypeStruct((depth, depth), bf16),
            jax.ShapeDtypeStruct((TAIL + 8, depth), f32),
        ),
        scratch_shapes=[pltpu.VMEM((cols, depth), f32)],
        compiler_params=pltpu.CompilerParams(vmem_limit_bytes=VMEM_BYTES),
        name="value_pass",
    )(do_all, wv, px_all, st_all, ld)


def kernel_back(nf, scale, videos_dev, xn, e, st, ld, ow, qw, q, wk, *rest):
    dqs = rest[:videos_dev]
    dxs = rest[videos_dev : 2 * videos_dev]
    dq_o, dwk_o, side_o, zs, acc = rest[2 * videos_dev :]
    v = pl.program_id(0)
    i = pl.program_id(1)
    tokens = xn.shape[0]
    depth = wk.shape[0]
    heads_rows = GROUP * LATENTS
    total_rows = qw.shape[0]
    groups = total_rows // heads_rows
    cols = GROUP * HEAD_SIZE

    @pl.when((v == 0) & (i == 0))
    def _():
        acc[...] = jnp.zeros_like(acc)

    second = jnp.zeros((1, tokens), f32)
    block = lax.broadcasted_iota(jnp.int32, (heads_rows, 128), 1)
    for g in range(groups):
        rows = slice(g * heads_rows, (g + 1) * heads_rows)
        peak = jnp.sum(jnp.where(block == i, st[rows, :], 0.0), -1, keepdims=True)
        lse = ld[rows, 0:1]
        dp = nt(ow[rows, :], xn[:, :depth])
        expo = e[rows, :].astype(f32)
        prob = expo * jnp.exp(peak - lse)
        z = prob * (dp - ld[rows, 1:2])
        score = jnp.log(jnp.maximum(expo, 1e-37)) + peak
        second = second + jnp.sum(z * score + prob * dp, 0, keepdims=True)
        zs[rows, :] = z.astype(bf16)
    zs[total_rows:, :] = tail_rows(nf, i, second, xn, depth)
    acc[...] += nn(zs[...], xn[...])

    @pl.when((v == videos_dev - 1) & (i == pl.num_programs(1) - 1))
    def _():
        gain = jnp.zeros((8, depth), f32)
        for g in range(groups):
            rows = slice(g * heads_rows, (g + 1) * heads_rows)
            wide = slice(g * cols, (g + 1) * cols)
            held = acc[rows, :depth]
            low = held.astype(bf16)
            dq_o[:, wide] = collect(nn(low, wk[:, wide])) * scale
            grad = tn(spread(q[:, wide]), low)
            for one, dx in zip(dqs, dxs):
                grad = grad + tn(spread(one[:, wide]), dx[rows, :])
            dwk_o[wide, :] = (grad * scale).astype(bf16)
            gain = gain + jnp.sum(
                (held * qw[rows, :].astype(f32)).reshape(heads_rows // 8, 8, depth), 0
            )
        side_o[0:TAIL, :] = tn(acc[:total_rows, depth:].astype(bf16), qw[...])[:TAIL]
        side_o[TAIL : 2 * TAIL, :] = acc[total_rows:, :depth]
        side_o[2 * TAIL :, :] = gain


def back_pass(xn_all, e_all, st_all, ld, ow, qw, q_all, wk, dq_all, dxs, scale, videos_dev):
    depth = wk.shape[0]
    tokens_video = e_all.shape[1]
    frames_dev = tokens_video // PATCH
    nf = 2 if frames_dev % 2 == 0 else 1
    tokens = nf * PATCH
    blocks = frames_dev // nf
    rows = qw.shape[0]
    dqs = [dq_all[v * LATENTS : (v + 1) * LATENTS] for v in range(videos_dev)]
    return pl.pallas_call(
        functools.partial(kernel_back, nf, scale, videos_dev),
        grid=(videos_dev, blocks),
        in_specs=[
            pl.BlockSpec((tokens, depth + EXTRA), lambda v, i: (v * blocks + i, 0)),
            pl.BlockSpec((rows, tokens), lambda v, i: (v, i)),
            pl.BlockSpec((rows, 128), lambda v, i: (v, 0)),
            pl.BlockSpec((rows, 128), lambda v, i: (v, 0)),
            pl.BlockSpec((rows, depth), lambda v, i: (v, 0)),
            whole(qw.shape),
            whole(q_all.shape),
            whole(wk.shape),
        ]
        + [whole(a.shape) for a in dqs]
        + [whole(a.shape) for a in dxs],
        out_specs=[
            whole((LATENTS, depth)),
            whole((depth, depth)),
            whole((2 * TAIL + 8, depth)),
        ],
        out_shape=(
            jax.ShapeDtypeStruct((LATENTS, depth), f32),
            jax.ShapeDtypeStruct((depth, depth), bf16),
            jax.ShapeDtypeStruct((2 * TAIL + 8, depth), f32),
        ),
        scratch_shapes=[
            pltpu.VMEM((rows + TAIL, tokens), bf16),
            pltpu.VMEM((rows + TAIL, depth + EXTRA), f32),
        ],
        compiler_params=pltpu.CompilerParams(vmem_limit_bytes=VMEM_BYTES),
        cost_estimate=pl.CostEstimate(
            flops=4 * videos_dev * rows * tokens_video * depth,
            bytes_accessed=videos_dev * tokens_video * depth * 4,
            transcendentals=videos_dev * rows * tokens_video,
        ),
        name="back_pass",
    )(xn_all, e_all, st_all, ld, ow, qw, q_all, wk, *dqs, *dxs)


def scatter_head(x):
    me = lax.axis_index("head")
    core, side = (me & 1, me >> 1)
    x = x.reshape((2, 2) + x.shape[1:])
    away = lax.dynamic_index_in_dim(x, 1 - core, 1, False)
    near = lax.dynamic_index_in_dim(x, core, 1, False)
    x = near.astype(f32) + swap(away, "head", 1).astype(f32)
    away = lax.dynamic_index_in_dim(x, 1 - side, 0, False)
    near = lax.dynamic_index_in_dim(x, side, 0, False)
    return near, swap(away.astype(bf16), "head", 2)


def per_device(
    features, lengths, loss_mask, sq_weight, sq_first, sq_second, ffn_weight, ffn_first,
    ffn_second, left_bases, right_sq, right_ffn, latents, lat_first, lat_second, time_embed,
    time_first, time_second, gains, gain_first, gain_second,
):
    videos, frames_dev, patches, cols = features.shape
    lat_count, depth = latents.shape
    heads_dev = cols // HEAD_SIZE
    head_size = lax.axis_size("head")
    frame_size = lax.axis_size("frame")
    videos_dev = videos // head_size
    rows_dev = sq_weight.shape[1]
    scale = HEAD_SIZE ** (-0.5)
    f = lax.axis_index("frame")
    h = lax.axis_index("head")
    first_frame = (f == 0).astype(f32)
    first_head = (h == 0).astype(f32)
    share = videos_dev * lat_count // frame_size
    tokens_video = frames_dev * patches

    with jax.named_scope("exchange"):
        feat = features.reshape(videos, tokens_video, cols)
        got = [
            [
                swap(lax.dynamic_index_in_dim(feat, videos_dev * (h ^ k) + j, 0, False), "head", k)
                for k in range(1, head_size)
            ]
            for j in range(videos_dev)
        ]

    with jax.named_scope("weights"):
        sq_low = sq_weight.astype(bf16)
        kv_rows = lax.all_gather(sq_low[1:3], "head", axis=2, tiled=True)
        w_key = lax.all_gather(kv_rows[0], "frame", axis=0, tiled=True)
        w_value = lax.all_gather(kv_rows[1], "frame", axis=0, tiled=True)
        w_query, w_outt, w_dec = (
            lax.all_gather(sq_low[n], "frame", axis=0, tiled=True) for n in (0, 3, 4)
        )
        ffn_low = ffn_weight.astype(bf16)
        w_up, w_downt = (
            lax.all_gather(ffn_low[n], "frame", axis=0, tiled=True) for n in (0, 1)
        )
        time_full = lax.all_gather(time_embed, "head", axis=1, tiled=True)

    with jax.named_scope("latent_keys"):
        zhat_zero, zrstd_zero = normalize_rows(latents)
        normed_lat = (zhat_zero * gains[1]).astype(bf16)
        query = nn(normed_lat, w_query).astype(bf16)
        q_all = lax.all_gather(query, "head", axis=1, tiled=True)
        w_key_own = lax.dynamic_slice_in_dim(w_key, h * cols, cols, 1)
        w_value_own = lax.dynamic_slice_in_dim(w_value, h * cols, cols, 1)
        lat_key = nn(normed_lat, w_key_own).astype(bf16).reshape(lat_count, heads_dev, HEAD_SIZE)
        lat_value = nn(normed_lat, w_value_own).astype(bf16).reshape(lat_count, heads_dev, HEAD_SIZE)
        qw = absorb(q_all, w_key, scale)

    with jax.named_scope("read"):
        own_lens = lax.dynamic_slice_in_dim(lengths, h * videos_dev, videos_dev, 0)
        state = None
        for j in range(videos_dev):
            state = read_pass(
                j, state, feat, got[j], time_full, gains[0:1], own_lens[j], qw, w_value, h, videos_dev
            )
        xn_all, e_all, px_all, st_all, o_all = state

    with jax.named_scope("combine"):
        heads = depth // HEAD_SIZE
        lse_local = (
            (st_all[:, 126] + jnp.log(st_all[:, 127]))
            .reshape(videos_dev, heads, lat_count)
            .transpose(0, 2, 1)
            .reshape(videos_dev * lat_count, heads)
        )
        pay = jnp.concatenate(
            [o_all.astype(bf16), split_three(lse_local)], 1
        ).reshape(frame_size, share, depth + 3 * heads)
        pay = lax.all_to_all(pay, "frame", 0, 0, tiled=True)
        lse_each = join_three(pay[..., depth:])
        o_each = pay[..., :depth].astype(f32).reshape(frame_size, share, heads, HEAD_SIZE)
        top = jnp.max(lse_each, 0)
        weight = jnp.exp(lse_each - top)
        total = jnp.sum(weight, 0)
        o_tok = jnp.sum(o_each * weight[..., None], 0) / total[..., None]
        lse_tok = top + jnp.log(total)
        o_heads = o_tok.reshape(share, head_size, cols).transpose(1, 0, 2).astype(bf16)
        l_heads = split_three(lse_tok.reshape(share, head_size, heads_dev).transpose(1, 0, 2))
        pay = lax.all_to_all(jnp.concatenate([o_heads, l_heads], 2), "head", 0, 0, tiled=True)
        lse_tok = join_three(pay[..., cols:])
        o_tok = pay[..., :cols].astype(f32).reshape(head_size, share, heads_dev, HEAD_SIZE)
        first_row = lax.rem(f * share, lat_count)
        q_rows = lax.dynamic_slice_in_dim(query, first_row, share, 0).reshape(
            share, heads_dev, HEAD_SIZE
        )
        lat_scores = (
            jnp.einsum("rnd,jnd->rnj", q_rows, lat_key, preferred_element_type=f32) * scale
        )
        lse = jnp.logaddexp(lse_tok, jax.nn.logsumexp(lat_scores, -1)[None])
        lat_prob = jnp.exp(lat_scores[None] - lse[..., None])
        attn = o_tok * jnp.exp(lse_tok - lse)[..., None] + jnp.einsum(
            "srnj,jnd->srnd", lat_prob, lat_value.astype(f32), precision=HIGH_ACCURACY
        )
        rows = head_size * share
        attn_low = attn.reshape(rows, cols).astype(bf16)

    with jax.named_scope("latent_forward"):
        lat_rows = jnp.tile(lax.dynamic_slice_in_dim(latents, first_row, share, 0), (head_size, 1))
        z_one = lat_rows + sum_head(nt(attn_low, w_outt))
        z1hat, z1rstd = normalize_rows(z_one)
        ffn_in = (z1hat * gains[2]).astype(bf16)
        pre = nn(ffn_in, w_up)
        hidden = jax.nn.gelu(pre).astype(bf16)
        z_two = z_one + sum_head(nt(hidden, w_downt))
        z2hat, z2rstd = normalize_rows(z_two)
        final = (z2hat * gains[3]).astype(bf16)
        dec = jnp.concatenate([nn(final, w_query), nn(final, w_dec)], 1).astype(bf16)

    def to_tokens(x):
        x = lax.all_to_all(x.reshape(head_size, share, -1), "head", 0, 0, tiled=True)
        x = x.transpose(1, 0, 2)
        x = jnp.broadcast_to(x[None], (frame_size,) + x.shape)
        x = lax.all_to_all(x, "frame", 0, 0, tiled=True)
        return x.reshape(videos_dev * lat_count, head_size, -1)

    with jax.named_scope("decode"):
        dec_all = to_tokens(dec)
        dq_all = dec_all[..., :cols].reshape(videos_dev * lat_count, depth)
        dv_all = dec_all[..., cols:].reshape(videos_dev * lat_count, depth)
        own_mask = lax.dynamic_slice_in_dim(loss_mask, h * videos_dev, videos_dev, 0).astype(f32)
        counts = own_mask.reshape(videos_dev * tokens_video, 1)
        decoded = [
            decode_pass(
                j, xn_all, feat, got[j], counts, dq_all, dv_all, w_key, h, scale, videos_dev
            )
            for j in range(videos_dev)
        ]
        loss_part = sum(jnp.sum(d[4]) for d in decoded)
        count_part = jnp.sum(own_mask)
        dec_side = sum(d[3] for d in decoded)

    with jax.named_scope("latent_backward"):
        ddec = jnp.concatenate(
            [
                jnp.concatenate([d[n] for d in decoded], 0).reshape(frame_size, share, head_size, cols)
                for n in (0, 1)
            ],
            3,
        ).astype(bf16)
        ddec = lax.all_to_all(
            ddec.reshape(frame_size, share, -1), "frame", 0, 0, tiled=True
        ).astype(f32)
        ddec = jnp.sum(ddec, 0).astype(bf16).reshape(share, head_size, 2 * cols).transpose(1, 0, 2)
        ddec = lax.all_to_all(ddec, "head", 0, 0, tiled=True).reshape(rows, 2 * cols)
        ddq_low, ddv_low = (ddec[:, :cols], ddec[:, cols:])
        dfinal = sum_head(nt(ddq_low, w_query) + nt(ddv_low, w_dec))
        dz_two = norm_reverse(dfinal, z2hat, z2rstd, gains[3])
        dz2_low = dz_two.astype(bf16)
        _, gelu_back = jax.vjp(jax.nn.gelu, pre)
        dpre = gelu_back(nn(dz2_low, w_downt))[0].astype(bf16)
        dffn_in = sum_head(nt(dpre, w_up))
        dz_one = dz_two + norm_reverse(dffn_in, z1hat, z1rstd, gains[2])
        dz1_low = dz_one.astype(bf16)
        dattn = nn(dz1_low, w_outt).astype(bf16)
        dattn_heads = dattn.astype(f32).reshape(head_size, share, heads_dev, HEAD_SIZE)
        delta = jnp.sum(dattn_heads * attn, -1)
        pay = jnp.concatenate(
            [
                dattn,
                split_three(lse.reshape(rows, heads_dev)),
                split_three(delta.reshape(rows, heads_dev)),
            ],
            1,
        )
        pay = to_tokens(pay)
        do_all = pay[..., :cols].reshape(videos_dev * lat_count, depth)

        def by_head(x):
            x = join_three(x).reshape(videos_dev, lat_count, heads)
            return x.transpose(0, 2, 1).reshape(videos_dev * heads * lat_count, 1)

        ld = jnp.concatenate(
            [
                by_head(pay[..., cols : cols + 3 * heads_dev]),
                by_head(pay[..., cols + 3 * heads_dev :]),
            ],
            1,
        )
        ld = jnp.pad(ld, ((0, 0), (0, 126)))

    with jax.named_scope("latent_pairs"):
        lat_value_f = lat_value.astype(f32)
        lat_dprob = jnp.einsum("srnd,jnd->srnj", dattn_heads, lat_value_f, precision=HIGH_ACCURACY)
        lat_dscore = lat_prob * (lat_dprob - delta[..., None]) * scale
        dq_lat = jnp.einsum(
            "srnj,jnd->rnd", lat_dscore, lat_key.astype(f32), precision=HIGH_ACCURACY
        ).reshape(share, cols)
        dk_lat = jnp.einsum(
            "srnj,rnd->jnd", lat_dscore, q_rows.astype(f32), precision=HIGH_ACCURACY
        ).reshape(lat_count, cols)
        dv_lat = jnp.einsum(
            "srnj,srnd->jnd", lat_prob, dattn_heads, precision=HIGH_ACCURACY
        ).reshape(lat_count, cols)
        dk_lat_low = dk_lat.astype(bf16)
        dv_lat_low = dv_lat.astype(bf16)
        dzn_pairs = nt(dk_lat_low, w_key_own) + nt(dv_lat_low, w_value_own)

    with jax.named_scope("value"):
        ow, dwv_t, value_side = value_pass(do_all, w_value, px_all, st_all, ld, videos_dev)

    with jax.named_scope("back"):
        dq_part, dwk_t, back_side = back_pass(
            xn_all, e_all, st_all, ld, ow, qw, q_all, w_key, dq_all,
            [d[2] for d in decoded], scale, videos_dev,
        )

    with jax.named_scope("row_gradients"):
        all_rows = frame_size * rows
        wide = lax.all_gather(
            jnp.concatenate([hidden, dpre, attn_low, ddq_low, ddv_low], 1), "frame", axis=0, tiled=True
        )
        hid = hidden.shape[1]
        narrow = jnp.concatenate(
            [a.reshape(rows, frame_size, rows_dev) for a in (ffn_in, dz2_low, dz1_low, final)], 2
        ).transpose(1, 0, 2)
        narrow = lax.all_to_all(narrow, "frame", 0, 0, tiled=True).reshape(all_rows, 4 * rows_dev)
        ffn_in_own, dz2_own, dz1_own, final_own = (
            narrow[:, n * rows_dev : (n + 1) * rows_dev] for n in range(4)
        )
        grad_up = tn(ffn_in_own, wide[:, hid : 2 * hid])
        grad_downt = tn(dz2_own, wide[:, :hid])
        grad_outt = tn(dz1_own, wide[:, 2 * hid : 2 * hid + cols])
        grad_query = tn(final_own, wide[:, 2 * hid + cols : 2 * hid + 2 * cols])
        grad_dec = tn(final_own, wide[:, 2 * hid + 2 * cols :])

    with jax.named_scope("patch_gradients"):
        side = dec_side + back_side
        pulled = side[:TAIL] + value_side[:TAIL]
        pulled = pulled * gains[0]
        time_part = (
            pulled
            - jnp.mean(pulled, -1, keepdims=True)
            - side[TAIL : 2 * TAIL] / gains[0]
        )
        gain0 = jnp.sum(side[2 * TAIL :] + value_side[TAIL:], 0, keepdims=True) / gains[0]
        pack = jnp.concatenate(
            [dq_part, time_part, gain0, jnp.zeros((7, depth), f32)], 0
        )
        pack = pack.reshape(-1, head_size, cols).transpose(1, 0, 2)
        near, far = scatter_head(pack)
        pack = near + far.astype(f32)
        time_own = pack[lat_count : lat_count + frames_dev]
        dq_pad = lax.dynamic_update_slice_in_dim(
            jnp.zeros((lat_count, cols), f32), dq_lat, first_row, 0
        )
        pack = jnp.concatenate([pack[:lat_count] + dq_pad, pack[lat_count + TAIL :]], 0)
        pack = sum_over(pack, "frame")
        dquery = pack[:lat_count].astype(bf16)
        gain0_own = pack[lat_count]
        dzn_query = sum_head(nt(dquery, w_query))
        lat_direct = lax.dynamic_update_slice_in_dim(
            jnp.zeros((lat_count, depth), f32),
            jnp.sum(dz_one.reshape(head_size, share, depth), 0),
            first_row,
            0,
        )
        row_part = jnp.concatenate(
            [lat_direct, jnp.sum(dffn_in * z1hat, 0)[None], jnp.sum(dfinal * z2hat, 0)[None]], 0
        )
        row_sum, dzn_pairs = lax.psum((row_part * first_head, dzn_pairs), ("frame", "head"))
        dzn = dzn_query + dzn_pairs
        grad_gain1 = jnp.sum(dzn * zhat_zero, 0)
        lat_grad = row_sum[:lat_count] + norm_reverse(dzn, zhat_zero, zrstd_zero, gains[1])
        gain_rest = jnp.stack([grad_gain1, row_sum[lat_count], row_sum[lat_count + 1]])
        gain_grad = jnp.concatenate(
            [gain0_own[None], lax.dynamic_slice_in_dim(gain_rest, h * cols, cols, 1)], 0
        )
        normed_own = lax.dynamic_slice_in_dim(normed_lat, f * rows_dev, rows_dev, 1)
        grad_query = grad_query + tn(normed_own, dquery)

    with jax.named_scope("key_value_gradients"):
        grads = []
        for grad, lat_low in ((dwk_t, dk_lat_low), (dwv_t, dv_lat_low)):
            near, far = scatter_head(grad.reshape(head_size, cols, depth))
            grad = near + far.astype(f32) + tn(lat_low, normed_lat)
            grads.append(grad.astype(bf16))
        both = jnp.concatenate(grads, 0).T
        both = lax.psum_scatter(both, "frame", scatter_dimension=0, tiled=True).astype(f32)
        grad_key, grad_value = (both[:, :cols], both[:, cols:])

    with jax.named_scope("update"):
        sq_grad = jnp.stack([grad_query, grad_key, grad_value, grad_outt, grad_dec])
        ffn_grad = jnp.stack([grad_up, grad_downt])
        squares = (
            jnp.sum(sq_grad * sq_grad) + jnp.sum(ffn_grad * ffn_grad) + jnp.sum(time_own * time_own)
        )
        squares = (
            squares
            + first_frame * first_head * jnp.sum(lat_grad * lat_grad)
            + first_frame * jnp.sum(gain_grad * gain_grad)
        )
        sums = jnp.pad(jnp.stack([loss_part, count_part, squares])[None], ((0, 7), (0, 125)))
        sums = sum_over(sum_over(sums, "head"), "frame")
        loss_sum, masked_count, squares = (sums[0, 0], sums[0, 1], sums[0, 2])
        grad_norm = jnp.sqrt(squares) / masked_count
        factor = jnp.minimum(1.0, clip_max / grad_norm) / masked_count
        out_rate = ((FRAMES * PATCH + LATENTS) / 64.0) ** 0.5
        sq_rates = jnp.array([1.0, 1.0, 1.0, out_rate, 1.0], f32) * 0.02
        ffn_rates = jnp.array([0.02, 0.02], f32)
        sq_out = soap_update(
            sq_weight, sq_grad * factor, sq_first, sq_second, left_bases[:5], right_sq, sq_rates
        )
        ffn_out = soap_update(
            ffn_weight, ffn_grad * factor, ffn_first, ffn_second, left_bases[5:], right_ffn, ffn_rates
        )
        lat_out = adamw_update(latents, lat_grad * factor, lat_first, lat_second, 0.01)
        time_out = adamw_update(time_embed, time_own * factor, time_first, time_second, 0.01)
        gain_own = lax.dynamic_slice_in_dim(gains, h * cols, cols, 1)
        gain_out = adamw_update(gain_own, gain_grad * factor, gain_first, gain_second, 0.0)
    return (loss_sum, masked_count, grad_norm, *sq_out, *ffn_out, *lat_out, *time_out, *gain_out)


def solution(mesh):
    matrix = P(None, "frame", "head")
    frame_rows = P("frame", "head")
    by_head = P(None, "head")
    placed = (
        P(None, "frame", None, "head"),
        P(None, "frame"),
        P(None, "frame", None),
        matrix, matrix, matrix, matrix, matrix, matrix,
        P(None, "frame", None, None),
        P(None, "head", None, None),
        P(None, "head", None, None),
        P(), P(), P(),
        frame_rows, frame_rows, frame_rows,
        P(), by_head, by_head,
    )
    outs = (
        P(), P(), P(),
        matrix, matrix, matrix, matrix, matrix, matrix, matrix, matrix,
        P(), P(), P(),
        frame_rows, frame_rows, frame_rows,
        by_head, by_head, by_head,
    )
    return jax.shard_map(per_device, mesh=mesh, in_specs=placed, out_specs=outs, check_vma=False)
```

```python
import functools

import jax
import jax.numpy as jnp
from jax import lax
from jax.experimental import pallas as pl
from jax.experimental.pallas import tpu as pltpu
from jax.sharding import PartitionSpec as P

HEAD_SIZE = 96
LATENTS = 64
PATCH = 256
FRAMES = 96
STEP = 5
GROUP = 4
EXTRA = 128
TAIL = 16
VMEM_BYTES = 62 * 1024 * 1024

HIGH_ACCURACY = lax.Precision.HIGHEST
clip_max = 0.05
beta_one = 0.5
beta_two = 0.6
adam_eps = 1e-08
BRIEF = pl.CostEstimate(flops=1, bytes_accessed=1, transcendentals=0)
f32 = jnp.float32
bf16 = jnp.bfloat16


def nn(a, b):
    return lax.dot_general(a, b, (((1,), (0,)), ((), ())), preferred_element_type=f32)


def nt(a, b):
    return lax.dot_general(a, b, (((1,), (1,)), ((), ())), preferred_element_type=f32)


def tn(a, b):
    return lax.dot_general(a, b, (((0,), (0,)), ((), ())), preferred_element_type=f32)


def normalize_rows(v):
    cent = v - jnp.mean(v, -1, keepdims=True)
    rstd = lax.rsqrt(jnp.mean(cent * cent, -1, keepdims=True) + 1e-05)
    return (cent * rstd, rstd)


def norm_reverse(dy, xhat, rstd, gain):
    scaled = dy * gain
    first = jnp.mean(scaled, -1, keepdims=True)
    second = jnp.mean(scaled * xhat, -1, keepdims=True)
    return rstd * (scaled - first - xhat * second)


def adam_moments(grad, one, two):
    one = beta_one * one + (1.0 - beta_one) * grad
    two = beta_two * two + (1.0 - beta_two) * grad * grad
    step = one / (1.0 - beta_one**STEP) / (jnp.sqrt(two / (1.0 - beta_two**STEP)) + adam_eps)
    return (one, two, step)


def adamw_update(weight, grad, one, two, decay):
    one, two, step = adam_moments(grad, one, two)
    return (weight - 0.3 * (step + decay * weight), one, two)


def swap(x, axis, bit):
    size = lax.axis_size(axis)
    return lax.ppermute(x, axis, [(i, i ^ bit) for i in range(size)])


def sum_over(x, axis):
    bit = 1
    while bit < lax.axis_size(axis):
        x = x + swap(x, axis, bit)
        bit *= 2
    return x


def sum_rounded(x, axis):
    bit = 1
    while bit < lax.axis_size(axis):
        x = lax.reduce_precision(x, 8, 7)
        x = x + swap(x.astype(bf16), axis, bit).astype(f32)
        bit *= 2
    return x


def sum_head(x):
    x = x + swap(x, "head", 1)
    x = lax.reduce_precision(x, 8, 7)
    return x + swap(x.astype(bf16), "head", 2).astype(f32)


def gather_head(x, axis):
    me = lax.axis_index("head")
    bit = 1
    while bit < lax.axis_size("head"):
        away = swap(x, "head", bit)
        mine_first = (me & bit) == 0
        x = jnp.concatenate(
            [jnp.where(mine_first, x, away), jnp.where(mine_first, away, x)], axis
        )
        bit *= 2
    return x


def zero_of(x):
    return (x[(0,) * x.ndim].astype(f32) * 0.0).astype(jnp.int32)


def after(x, *deps):
    return lax.optimization_barrier((x, *deps))[0]


def split_three(x):
    high = lax.reduce_precision(x, 8, 7)
    rest = x - high
    mid = lax.reduce_precision(rest, 8, 7)
    return jnp.concatenate([high, mid, rest - mid], -1).astype(bf16)


def join_three(x):
    n = x.shape[-1] // 3
    x = x.astype(f32)
    return x[..., :n] + x[..., n : 2 * n] + x[..., 2 * n :]


def head_of_lane(rows, cols):
    return lax.broadcasted_iota(jnp.int32, (rows, cols), 1) // HEAD_SIZE


def spread(x):
    owner = head_of_lane(*x.shape)
    x = x.astype(f32)
    return jnp.concatenate([jnp.where(owner == j, x, 0.0) for j in range(GROUP)], 0).astype(bf16)


def collect(r):
    rows = r.shape[0] // GROUP
    owner = head_of_lane(rows, r.shape[1])
    out = jnp.where(owner == 0, r[:rows], 0.0)
    for j in range(1, GROUP):
        out = out + jnp.where(owner == j, r[j * rows : (j + 1) * rows], 0.0)
    return out


def whole(shape):
    return pl.BlockSpec(shape, lambda *_: (0,) * len(shape), pipeline_mode=pl.Buffered(1))


def kernel_absorb(scale, x_ref, w_ref, out_ref):
    out_ref[...] = (nt(spread(x_ref[...]), w_ref[...]) * scale).astype(bf16)


def absorb(x, w, scale):
    depth, width = w.shape
    cols = GROUP * HEAD_SIZE
    groups = width // cols
    rows = GROUP * LATENTS
    return pl.pallas_call(
        functools.partial(kernel_absorb, scale),
        grid=(groups,),
        in_specs=[
            pl.BlockSpec((LATENTS, cols), lambda g: (0, g)),
            pl.BlockSpec((depth, cols), lambda g: (0, g)),
        ],
        out_specs=pl.BlockSpec((rows, depth), lambda g: (g, 0)),
        out_shape=jax.ShapeDtypeStruct((groups * rows, depth), bf16),
        compiler_params=pltpu.CompilerParams(vmem_limit_bytes=VMEM_BYTES),
        cost_estimate=BRIEF,
        name="absorb",
    )(x, w)


def kernel_pick(place, a, b, c, far_o, near_o):
    del place
    far_o[0] = a[...]
    far_o[1] = b[...]
    near_o[...] = c[...]


def pick(feat, place, j, c, videos_dev):
    count, tokens_video, cols = feat.shape
    frames_dev = tokens_video // PATCH
    cuts, nf = chunks_of(frames_dev)
    step = nf * PATCH
    blocks = cuts[c] // nf
    start = (j * frames_dev + sum(cuts[:c])) // nf
    tokens = cuts[c] * PATCH
    feat2 = feat.reshape(count * tokens_video, cols)

    def spot(k):
        return lambda i, p: ((p[0] ^ k) * (videos_dev * frames_dev // nf) + start + i, 0)

    return pl.pallas_call(
        kernel_pick,
        grid_spec=pltpu.PrefetchScalarGridSpec(
            num_scalar_prefetch=1,
            grid=(blocks,),
            in_specs=[pl.BlockSpec((step, cols), spot(k)) for k in (2, 3, 1)],
            out_specs=[
                pl.BlockSpec((2, step, cols), lambda i, p: (0, i, 0)),
                pl.BlockSpec((step, cols), lambda i, p: (i, 0)),
            ],
        ),
        out_shape=[
            jax.ShapeDtypeStruct((2, tokens, cols), bf16),
            jax.ShapeDtypeStruct((tokens, cols), bf16),
        ],
        compiler_params=pltpu.CompilerParams(vmem_limit_bytes=VMEM_BYTES),
        cost_estimate=BRIEF,
        name="pick",
    )(place[None], feat2, feat2, feat2)


def kernel_gate(*refs):
    del refs


def gate(x, *deps):
    anyspec = pl.BlockSpec(memory_space=pl.ANY)
    return pl.pallas_call(
        kernel_gate,
        in_specs=[anyspec] * (1 + len(deps)),
        out_specs=anyspec,
        out_shape=jax.ShapeDtypeStruct(x.shape, x.dtype),
        input_output_aliases={0: 0},
        cost_estimate=BRIEF,
        name="gate",
    )(x, *deps)


def frames_a_block(frames):
    return 2 if frames % 2 == 0 else 1


def chunks_of(frames):
    if frames % 6 == 0:
        return (frames // 3 * 2, frames // 3), frames // 3
    return (frames,), 1


def kernel_read(
    nf, first, place, own, ra, rb, rc, time_ref, g0, qw, wv, xn_in, ft_in, e_in, px_in, st_in, o_in, dep,
    xn_o, ft_o, e_o, px_o, st_o, o_o, token_o, xs, acc, run,
):
    del xn_in, ft_in, e_in, px_in, st_in, o_in, dep
    i = pl.program_id(0)
    tokens, depth = xs.shape
    cols = own.shape[1]
    heads_rows = GROUP * LATENTS
    groups = qw.shape[0] // heads_rows

    @pl.when(i == 0)
    def _():
        acc[...] = jnp.zeros_like(acc)
        run[0] = jnp.full(run.shape[1:], -1e30, f32)
        run[1] = jnp.zeros(run.shape[1:], f32)
        st_o[...] = jnp.zeros_like(st_o)

    for k, part in enumerate((own, ra, rb, rc)):
        off = pl.multiple_of((place[0] ^ k) * cols, 128)
        for f in range(nf):
            rows = slice(f * PATCH, (f + 1) * PATCH)
            raw = part[rows, :]
            ft_o[rows, pl.ds(off, cols)] = raw
            row = first + i * nf + f
            moved = raw.astype(f32) + time_ref[pl.ds(row, 1), pl.ds(off, cols)]
            xs[rows, pl.ds(off, cols)] = moved.astype(bf16)
    x = xs[...].astype(f32)
    cent = x - jnp.sum(x, -1, keepdims=True) * (1.0 / depth)
    rstd = lax.rsqrt(jnp.sum(cent * cent, -1, keepdims=True) * (1.0 / depth) + 1e-05)
    xn_o[:, :depth] = (cent * rstd * g0[...]).astype(bf16)
    lane = lax.broadcasted_iota(jnp.int32, (tokens, EXTRA), 1)
    frame = lax.broadcasted_iota(jnp.int32, (tokens, EXTRA), 0) // PATCH + first + i * nf
    xn_o[:, depth:] = jnp.where(lane == frame, rstd, 0.0).astype(bf16)
    key = lax.broadcasted_iota(jnp.int32, (1, tokens), 1)
    limit = place[1 + first + i * nf]
    for f in range(1, nf):
        limit = jnp.where(key >= f * PATCH, f * PATCH + place[1 + first + i * nf + f], limit)
    valid = key < limit
    block = lax.broadcasted_iota(jnp.int32, (heads_rows, 128), 1)
    last = i == pl.num_programs(0) - 1
    for g in range(groups):
        rows = slice(g * heads_rows, (g + 1) * heads_rows)
        scores = jnp.where(valid, nt(qw[rows, :], xn_o[:, :depth]), -1e30)
        old = run[0, rows, :]
        new = jnp.maximum(old, jnp.max(scores, -1, keepdims=True))
        expo = jnp.exp(scores - new[:, :1])
        shrink = jnp.exp(old - new)
        total = run[1, rows, :] * shrink + jnp.sum(expo, -1, keepdims=True)
        run[0, rows, :] = new
        run[1, rows, :] = total
        low = expo.astype(bf16)
        e_o[rows, :] = low
        stats = jnp.where(block == i, new, st_o[rows, :])
        stats = jnp.where(last & (block == 126), new, stats)
        st_o[rows, :] = jnp.where(last & (block == 127), total, stats)
        acc[rows, :] = acc[rows, :] * shrink[:, :1] + nn(low, xn_o[...])

    @pl.when(last)
    def _():
        for g in range(groups):
            rows = slice(g * heads_rows, (g + 1) * heads_rows)
            wide = slice(g * cols, (g + 1) * cols)
            held = acc[rows, :].astype(bf16)
            px_o[rows, :] = held
            mixed = nn(held[:, :depth], wv[:, wide]) * (1.0 / run[1, rows, :1])
            o_o[:, wide] = collect(mixed)
        token_o[...] = run[1, 0:8, :]


def read_pass(j, c, prev, feat, got, time_full, gain, lens, qw, wv, dep, h, videos_dev):
    count, tokens_video, cols = feat.shape
    depth = wv.shape[0]
    frames_dev = tokens_video // PATCH
    cuts, nf = chunks_of(frames_dev)
    chunks = len(cuts)
    frames = cuts[c]
    before = sum(cuts[:c])
    tokens = nf * PATCH
    blocks = frames // nf
    start = (j * frames_dev + before) // nf
    rows = qw.shape[0]
    part = j * chunks + c
    parts = videos_dev * chunks
    place = jnp.concatenate([h[None], lens]).astype(jnp.int32)
    feat2 = feat.reshape(count * tokens_video, cols)
    shapes = (
        jax.ShapeDtypeStruct((videos_dev * tokens_video, depth + EXTRA), bf16),
        jax.ShapeDtypeStruct((videos_dev * tokens_video, depth), bf16),
        jax.ShapeDtypeStruct((videos_dev * rows, tokens_video), bf16),
        jax.ShapeDtypeStruct((parts * rows, depth + EXTRA), bf16),
        jax.ShapeDtypeStruct((parts * rows, 128), f32),
        jax.ShapeDtypeStruct((parts * LATENTS, depth), f32),
    )
    aliases = {}
    if prev is None:
        prev = [jnp.zeros((16, 128), s.dtype) for s in shapes]
    else:
        aliases = {9 + n: n for n in range(6)}
    anyspec = pl.BlockSpec(memory_space=pl.ANY)
    one = pl.Buffered(1)
    return pl.pallas_call(
        functools.partial(kernel_read, nf, before),
        grid_spec=pltpu.PrefetchScalarGridSpec(
            num_scalar_prefetch=1,
            grid=(blocks,),
            in_specs=[
                pl.BlockSpec(
                    (tokens, cols),
                    lambda i, p: (p[0] * (videos_dev * frames_dev // nf) + start + i, 0),
                ),
                pl.BlockSpec((tokens, cols), lambda i, p: (i, 0)),
                pl.BlockSpec((tokens, cols), lambda i, p: (i, 0)),
                pl.BlockSpec((tokens, cols), lambda i, p: (i, 0)),
                whole(time_full.shape),
                whole(gain.shape),
                whole(qw.shape),
                whole(wv.shape),
            ]
            + [anyspec] * 7,
            out_specs=[
                pl.BlockSpec((tokens, depth + EXTRA), lambda i, p: (start + i, 0)),
                pl.BlockSpec((tokens, depth), lambda i, p: (start + i, 0)),
                pl.BlockSpec((rows, tokens), lambda i, p: (j, before // nf + i)),
                pl.BlockSpec((rows, depth + EXTRA), lambda i, p: (part, 0), pipeline_mode=one),
                pl.BlockSpec((rows, 128), lambda i, p: (part, 0), pipeline_mode=one),
                pl.BlockSpec((LATENTS, depth), lambda i, p: (part, 0), pipeline_mode=one),
                whole((8, 128)),
            ],
            scratch_shapes=[
                pltpu.VMEM((tokens, depth), bf16),
                pltpu.VMEM((rows, depth + EXTRA), f32),
                pltpu.VMEM((2, rows, 128), f32),
            ],
        ),
        out_shape=(*shapes, jax.ShapeDtypeStruct((8, 128), f32)),
        input_output_aliases=aliases,
        compiler_params=pltpu.CompilerParams(vmem_limit_bytes=VMEM_BYTES),
        cost_estimate=pl.CostEstimate(
            flops=rows * frames * PATCH * depth // 2,
            bytes_accessed=frames * PATCH * depth,
            transcendentals=rows * frames * PATCH,
        ),
        name="read_pass",
    )(place, feat2, *got, time_full, gain, qw, wv, *prev, dep)


def kernel_decode(
    nf, scale, xn, feat, msk, dq, dv, wk,
    ddq_o, ddv_o, dx_o, side_o, loss_o, dqw, dvd, sc, zs, acc, dacc, loss,
):
    i = pl.program_id(0)
    tokens = xn.shape[0]
    depth = wk.shape[0]
    heads_rows = GROUP * LATENTS
    total_rows = dqw.shape[0]
    groups = total_rows // heads_rows
    cols = depth // groups

    @pl.when(i == 0)
    def _():
        acc[...] = jnp.zeros_like(acc)
        dacc[...] = jnp.zeros_like(dacc)
        loss[...] = jnp.zeros_like(loss)
        for g in range(groups):
            rows = slice(g * heads_rows, (g + 1) * heads_rows)
            wide = slice(g * cols, (g + 1) * cols)
            dqw[rows, :] = (nt(spread(dq[:, wide]), wk[:, wide]) * scale).astype(bf16)
            dvd[g] = spread(dv[:, wide])

    sc[...] = nt(dqw[...], xn[:, :depth])
    counts = msk[...]
    second = jnp.zeros((1, tokens), f32)
    for g in range(groups):
        rows = slice(g * heads_rows, (g + 1) * heads_rows)
        wide = slice(g * cols, (g + 1) * cols)
        s = sc[rows, :].reshape(GROUP, LATENTS, tokens)
        a = jnp.exp(s - jnp.max(s, 1, keepdims=True))
        a = a * (1.0 / jnp.sum(a, 1, keepdims=True))
        low = a.reshape(heads_rows, tokens).astype(bf16)
        error = tn(low, dvd[g]) - feat[:, wide].astype(f32)
        kept = counts * error
        loss[...] += jnp.sum((kept * error).reshape(tokens // 8, 8, cols), 0)
        dp = (2.0 * kept).astype(bf16)
        dacc[g] += nn(low, dp)
        da = nt(dvd[g], dp).reshape(GROUP, LATENTS, tokens)
        z = a * (da - jnp.sum(a * da, 1, keepdims=True))
        second = second + jnp.sum((z * s).reshape(heads_rows, tokens), 0, keepdims=True)
        zs[rows, :] = z.reshape(heads_rows, tokens).astype(bf16)
    zs[total_rows:, :] = tail_rows(nf, i, second, xn, depth)
    acc[...] += nn(zs[...], xn[...])

    @pl.when(i == pl.num_programs(0) - 1)
    def _():
        gain = jnp.zeros((8, depth), f32)
        for g in range(groups):
            rows = slice(g * heads_rows, (g + 1) * heads_rows)
            wide = slice(g * cols, (g + 1) * cols)
            held = acc[rows, :depth]
            low = held.astype(bf16)
            dx_o[rows, :] = low
            ddq_o[:, wide] = collect(nn(low, wk[:, wide])) * scale
            ddv_o[:, wide] = collect(dacc[g])
            gain = gain + jnp.sum(
                (held * dqw[rows, :].astype(f32)).reshape(heads_rows // 8, 8, depth), 0
            )
        side_o[0:TAIL, :] = tn(acc[:total_rows, depth:].astype(bf16), dqw[...])[:TAIL]
        side_o[TAIL : 2 * TAIL, :] = acc[total_rows:, :depth]
        side_o[2 * TAIL :, :] = gain
        loss_o[...] = loss[...]


def tail_rows(nf, i, second, xn, depth):
    tokens = xn.shape[0]
    rstd = nt(jnp.ones((TAIL, EXTRA), bf16), xn[:, depth:])
    row = lax.broadcasted_iota(jnp.int32, (TAIL, tokens), 0)
    frame = lax.broadcasted_iota(jnp.int32, (TAIL, tokens), 1) // PATCH + i * nf
    return jnp.where(row == frame, rstd * second * (1.0 / depth), 0.0).astype(bf16)


def decode_pass(j, xn_all, ft_all, counts, dq_all, dv_all, wk, scale, videos_dev):
    depth = wk.shape[0]
    tokens_video = xn_all.shape[0] // videos_dev
    cols = GROUP * HEAD_SIZE
    frames_dev = tokens_video // PATCH
    nf = frames_a_block(frames_dev)
    tokens = nf * PATCH
    blocks = frames_dev // nf
    groups = depth // cols
    heads_rows = GROUP * LATENTS
    rows = groups * heads_rows
    one = pl.Buffered(1)
    return pl.pallas_call(
        functools.partial(kernel_decode, nf, scale),
        grid=(blocks,),
        in_specs=[
            pl.BlockSpec((tokens, depth + EXTRA), lambda i: (j * blocks + i, 0)),
            pl.BlockSpec((tokens, depth), lambda i: (j * blocks + i, 0)),
            pl.BlockSpec((tokens, 1), lambda i: (j * blocks + i, 0)),
            pl.BlockSpec((LATENTS, depth), lambda i: (j, 0), pipeline_mode=one),
            pl.BlockSpec((LATENTS, depth), lambda i: (j, 0), pipeline_mode=one),
            whole(wk.shape),
        ],
        out_specs=[
            whole((LATENTS, depth)),
            whole((LATENTS, depth)),
            whole((rows, depth)),
            whole((2 * TAIL + 8, depth)),
            whole((8, cols)),
        ],
        scratch_shapes=[
            pltpu.VMEM((rows, depth), bf16),
            pltpu.VMEM((groups, heads_rows, cols), bf16),
            pltpu.VMEM((rows, tokens), f32),
            pltpu.VMEM((rows + TAIL, tokens), bf16),
            pltpu.VMEM((rows + TAIL, depth + EXTRA), f32),
            pltpu.VMEM((groups, heads_rows, cols), f32),
            pltpu.VMEM((8, cols), f32),
        ],
        out_shape=(
            jax.ShapeDtypeStruct((LATENTS, depth), f32),
            jax.ShapeDtypeStruct((LATENTS, depth), f32),
            jax.ShapeDtypeStruct((rows, depth), bf16),
            jax.ShapeDtypeStruct((2 * TAIL + 8, depth), f32),
            jax.ShapeDtypeStruct((8, cols), f32),
        ),
        compiler_params=pltpu.CompilerParams(vmem_limit_bytes=VMEM_BYTES),
        cost_estimate=pl.CostEstimate(
            flops=6 * rows * tokens_video * depth,
            bytes_accessed=tokens_video * depth * 4,
            transcendentals=rows * tokens_video,
        ),
        name="decode_pass",
    )(xn_all, ft_all, counts, dq_all, dv_all, wk)


def head_column(ld, first):
    lane = lax.broadcasted_iota(jnp.int32, ld.shape, 1)
    return jnp.concatenate(
        [jnp.sum(jnp.where(lane == first + j, ld, 0.0), -1, keepdims=True) for j in range(GROUP)], 0
    )


def kernel_value(chunks, place, do, wv, ld, *rest):
    pxs = rest[:chunks]
    sts = rest[chunks : 2 * chunks]
    ow_o, near_o, away_o, side_o, acc = rest[2 * chunks :]
    k = pl.program_id(0)
    v = pl.program_id(1)
    depth = wv.shape[0]

    @pl.when((k == 0) & (v == 0))
    def _():
        side_o[...] = jnp.zeros_like(side_o)

    diag = spread(do[...])
    ow = nt(diag, wv[...]).astype(bf16)
    ow_o[...] = ow
    norm = 0.0
    lse = head_column(ld[...], (place[0] ^ k) * GROUP)
    for px, st in zip(pxs, sts):
        norm = norm + px[...].astype(f32) * jnp.exp(st[:, 126:127] - lse)
    low = norm.astype(bf16)
    part = tn(diag, low[:, :depth])

    @pl.when(v == 0)
    def _():
        acc[...] = part

    @pl.when(v > 0)
    def _():
        acc[...] += part

    @pl.when(k & 1 == 0)
    def _():
        near_o[0] = acc[...].astype(bf16)

    @pl.when(k & 1 == 1)
    def _():
        away_o[0] = acc[...].astype(bf16)

    side_o[0:TAIL, :] += tn(low[:, depth:], ow)[:TAIL]
    rows = ow.shape[0]
    side_o[TAIL:, :] += jnp.sum((ow.astype(f32) * norm[:, :depth]).reshape(rows // 8, 8, depth), 0)


def value_pass(do_all, wv, px_all, st_all, ld, h, videos_dev):
    depth = wv.shape[0]
    cols = GROUP * HEAD_SIZE
    groups = depth // cols
    rows = GROUP * LATENTS
    chunks = px_all.shape[0] // (videos_dev * groups * rows)

    def spot(c):
        return lambda k, v, p: ((v * chunks + c) * groups + (p[0] ^ k), 0)

    return pl.pallas_call(
        functools.partial(kernel_value, chunks),
        grid_spec=pltpu.PrefetchScalarGridSpec(
            num_scalar_prefetch=1,
            grid=(groups, videos_dev),
            in_specs=[
                pl.BlockSpec((LATENTS, cols), lambda k, v, p: (v, p[0] ^ k)),
                pl.BlockSpec((depth, cols), lambda k, v, p: (0, p[0] ^ k)),
                pl.BlockSpec((LATENTS, 128), lambda k, v, p: (v, 0)),
            ]
            + [pl.BlockSpec((rows, depth + EXTRA), spot(c)) for c in range(chunks)]
            + [pl.BlockSpec((rows, 128), spot(c)) for c in range(chunks)],
            out_specs=[
                pl.BlockSpec((rows, depth), lambda k, v, p: (v * groups + (p[0] ^ k), 0)),
                pl.BlockSpec((1, cols, depth), lambda k, v, p: (k >> 1, 0, 0)),
                pl.BlockSpec((1, cols, depth), lambda k, v, p: (k >> 1, 0, 0)),
                pl.BlockSpec((TAIL + 8, depth), lambda k, v, p: (0, 0)),
            ],
            scratch_shapes=[pltpu.VMEM((cols, depth), f32)],
        ),
        out_shape=(
            jax.ShapeDtypeStruct((videos_dev * groups * rows, depth), bf16),
            jax.ShapeDtypeStruct((groups // 2, cols, depth), bf16),
            jax.ShapeDtypeStruct((groups // 2, cols, depth), bf16),
            jax.ShapeDtypeStruct((TAIL + 8, depth), f32),
        ),
        compiler_params=pltpu.CompilerParams(vmem_limit_bytes=VMEM_BYTES),
        cost_estimate=BRIEF,
        name="value_pass",
    )(jnp.full((1,), h, jnp.int32), do_all, wv, ld, *[px_all] * chunks, *[st_all] * chunks)


def kernel_back(
    nf, per_chunk, per_read, scale, videos_dev, final, place, xn, e, st, ld, ow, qw, q, wk, *rest
):
    dqs = rest[:videos_dev]
    dxs = rest[videos_dev : 2 * videos_dev]
    rest = rest[2 * videos_dev :]
    if final:
        g0, side_a, side_b, dq_o, near_o, away_o, pack_o, zs, acc, pack = rest
    else:
        dq_o, near_o, away_o, side_o, zs, acc = rest
    v = pl.program_id(0)
    i = pl.program_id(1)
    tokens = xn.shape[0]
    depth = wk.shape[0]
    heads_rows = GROUP * LATENTS
    total_rows = qw.shape[0]
    groups = total_rows // heads_rows
    cols = GROUP * HEAD_SIZE

    @pl.when((v == 0) & (i == 0))
    def _():
        acc[...] = jnp.zeros_like(acc)

    second = jnp.zeros((1, tokens), f32)
    block = lax.broadcasted_iota(jnp.int32, (heads_rows, 128), 1)
    heads_total = depth // HEAD_SIZE
    base = (place[0] >> 1 if final else (place[0] >> 1) ^ 1) * groups
    for g in range(groups):
        rows = slice(g * heads_rows, (g + 1) * heads_rows)
        spot = lax.rem(i, per_chunk) // per_read
        peak = jnp.sum(jnp.where(block == spot, st[rows, :], 0.0), -1, keepdims=True)
        lse = head_column(ld[...], (base + g) * GROUP)
        delta = head_column(ld[...], (heads_total // GROUP + base + g) * GROUP)
        dp = nt(ow[rows, :], xn[:, :depth])
        expo = e[rows, :].astype(f32)
        prob = expo * jnp.exp(peak - lse)
        z = prob * (dp - delta)
        score = jnp.log(jnp.maximum(expo, 1e-37)) + peak
        second = second + jnp.sum(z * score + prob * dp, 0, keepdims=True)
        zs[rows, :] = z.astype(bf16)
    zs[total_rows:, :] = tail_rows(nf, i, second, xn, depth)
    acc[...] += nn(zs[...], xn[...])

    @pl.when((v == videos_dev - 1) & (i == pl.num_programs(1) - 1))
    def _():
        gain = jnp.zeros((8, depth), f32)
        for k in range(groups):
            g = (place[0] & 1) ^ k
            rows = pl.ds(pl.multiple_of(g * heads_rows, heads_rows), heads_rows)
            wide = pl.ds(pl.multiple_of(g * cols, 128), cols)
            low = acc[rows, :depth].astype(bf16)
            dq_o[k] = collect(nn(low, wk[:, wide])) * scale
            grad = tn(spread(q[:, wide]), low)
            for one, dx in zip(dqs, dxs):
                grad = grad + tn(spread(one[:, wide]), dx[rows, :])
            target = away_o if k & 1 else near_o
            target[...] = (grad * scale).astype(bf16)
        for g in range(groups):
            rows = slice(g * heads_rows, (g + 1) * heads_rows)
            gain = gain + jnp.sum(
                (acc[rows, :depth] * qw[rows, :].astype(f32)).reshape(heads_rows // 8, 8, depth), 0
            )
        pulled = tn(acc[:total_rows, depth:].astype(bf16), qw[...])[:TAIL]
        moved = acc[total_rows:, :depth]
        if final:
            pulled = (pulled + side_a[0:TAIL, :] + side_b[0:TAIL, :]) * g0[...]
            moved = moved + side_a[TAIL : 2 * TAIL, :] + side_b[TAIL : 2 * TAIL, :]
            moved = moved * (1.0 / g0[...])
            gain = gain + side_a[2 * TAIL :, :] + side_b[2 * TAIL :, :]
            mean = jnp.sum(pulled, -1, keepdims=True) * (1.0 / depth)
            pack[0:TAIL, :] = pulled - mean - moved
            pack[TAIL:, :] = gain * (1.0 / g0[...])
            for k in range(pack_o.shape[0]):
                wide = pl.ds(pl.multiple_of((place[0] ^ k) * cols, 128), cols)
                pack_o[(k & 1) * 2 + (k >> 1)] = pack[:, wide]
        else:
            side_o[0:TAIL, :] = pulled
            side_o[TAIL : 2 * TAIL, :] = moved
            side_o[2 * TAIL :, :] = gain


def back_pass(
    far, xn_all, e_all, st_all, ld, ow, qw, q_all, wk, dq_all, dxs, sides, gain, scale, h, videos_dev
):
    depth = wk.shape[0]
    tokens_video = e_all.shape[1]
    frames_dev = tokens_video // PATCH
    cuts, read_nf = chunks_of(frames_dev)
    chunks = len(cuts)
    nf = frames_a_block(read_nf)
    tokens = nf * PATCH
    blocks = frames_dev // nf
    per_chunk = cuts[0] // nf
    rows = qw.shape[0] // 2
    cols = GROUP * HEAD_SIZE
    groups = depth // cols
    packed = TAIL + 8
    final = not far
    one = pl.Buffered(1)

    def y(p):
        return (p[0] >> 1) ^ 1 if far else p[0] >> 1

    outs = [
        jax.ShapeDtypeStruct((2, LATENTS, cols), f32),
        jax.ShapeDtypeStruct((cols, depth), bf16),
        jax.ShapeDtypeStruct((cols, depth), bf16),
    ]
    scratch = [
        pltpu.VMEM((rows + TAIL, tokens), bf16),
        pltpu.VMEM((rows + TAIL, depth + EXTRA), f32),
    ]
    extra = []
    if final:
        extra = [gain, *sides]
        outs.append(jax.ShapeDtypeStruct((groups, packed, cols), f32))
        scratch.append(pltpu.VMEM((packed, depth), f32))
    else:
        outs.append(jax.ShapeDtypeStruct((2 * TAIL + 8, depth), f32))
    return pl.pallas_call(
        functools.partial(
            kernel_back, nf, per_chunk, read_nf // nf, scale, videos_dev, final
        ),
        grid_spec=pltpu.PrefetchScalarGridSpec(
            num_scalar_prefetch=1,
            grid=(videos_dev, blocks),
            in_specs=[
                pl.BlockSpec((tokens, depth + EXTRA), lambda v, i, p: (v * blocks + i, 0)),
                pl.BlockSpec((rows, tokens), lambda v, i, p: (v * 2 + y(p), i)),
                pl.BlockSpec(
                    (rows, 128), lambda v, i, p: ((v * chunks + i // per_chunk) * 2 + y(p), 0)
                ),
                pl.BlockSpec((LATENTS, 128), lambda v, i, p: (v, 0)),
                pl.BlockSpec((rows, depth), lambda v, i, p: (v * 2 + y(p), 0)),
                pl.BlockSpec((rows, depth), lambda v, i, p: (y(p), 0), pipeline_mode=one),
                pl.BlockSpec((LATENTS, 2 * cols), lambda v, i, p: (0, y(p)), pipeline_mode=one),
                pl.BlockSpec((depth, 2 * cols), lambda v, i, p: (0, y(p)), pipeline_mode=one),
            ]
            + [
                pl.BlockSpec((LATENTS, 2 * cols), lambda v, i, p, n=n: (n, y(p)), pipeline_mode=one)
                for n in range(videos_dev)
            ]
            + [
                pl.BlockSpec((rows, depth), lambda v, i, p: (y(p), 0), pipeline_mode=one)
                for _ in dxs
            ]
            + [whole(a.shape) for a in extra],
            out_specs=[whole(a.shape) for a in outs],
            scratch_shapes=scratch,
        ),
        out_shape=outs,
        compiler_params=pltpu.CompilerParams(vmem_limit_bytes=VMEM_BYTES),
        cost_estimate=pl.CostEstimate(
            flops=4 * videos_dev * rows * tokens_video * depth,
            bytes_accessed=videos_dev * tokens_video * depth * 4,
            transcendentals=videos_dev * rows * tokens_video,
        ),
        name="back_far" if far else "back_near",
    )(
        jnp.full((1,), h, jnp.int32), xn_all, e_all, st_all, ld, ow, qw, q_all, wk,
        *[dq_all] * videos_dev, *dxs, *extra,
    )


def halves(x):
    high = x.astype(bf16)
    return high, (x - high.astype(f32)).astype(bf16)


def precise(a, b, dims):
    dims = ((dims[0], dims[1]), ((), ()))
    ah, al = halves(a)
    bh, bl = halves(b)
    out = lax.dot_general(ah, bh, dims, preferred_element_type=f32)
    out = out + lax.dot_general(ah, bl, dims, preferred_element_type=f32)
    return out + lax.dot_general(al, bh, dims, preferred_element_type=f32)


def turn_body(g, left, right, out, total):
    @pl.when(pl.program_id(0) == 0)
    def _():
        total[...] = jnp.zeros_like(total)

    rows, cols = g.shape
    square = g * g
    part = square[:, :128]
    for c in range(1, cols // 128):
        part = part + square[:, c * 128 : (c + 1) * 128]
    total[...] += jnp.sum(part.reshape(rows // 8, 8, 128), 0)
    turned = precise(left[0], g, ((0,), (0,)))
    for c in range(cols // 128):
        wide = slice(c * 128, (c + 1) * 128)
        out[:, wide] = precise(turned[:, wide], right[0, c], ((1,), (0,)))


def kernel_turn(grad, left, right, out, total):
    turn_body(grad[...].astype(f32), left, right, out, total)


def kernel_turn_product(a, b, left, right, out, total):
    frames, _, rows, own = a.shape
    turn_body(tn(a[...].reshape(frames * rows, own), b[...]), left, right, out, total)


def kernel_turn_sum(a, b, c, d, left, right, out, total):
    frames, _, rows, own = a.shape
    grad = tn(a[...].reshape(frames * rows, own), b[...]) + tn(c[...], d[...])
    turn_body(grad, left, right, out, total)


def turn(slab, slot, operands, rows, cols, left, right):
    step = 3 * 128
    if len(operands) == 1:
        body = kernel_turn
        specs = [pl.BlockSpec((rows, step), lambda i: (0, i))]
        arrays = operands
    else:
        a, which, b, first = operands[:4]
        body = kernel_turn_product
        specs = [
            pl.BlockSpec((a.shape[0], 1) + a.shape[2:], lambda i: (0, which, 0, 0)),
            pl.BlockSpec((b.shape[0], step), lambda i: (0, first // step + i)),
        ]
        arrays = [a, b]
        if len(operands) > 4:
            body = kernel_turn_sum
            c, d = operands[4:]
            specs += [
                pl.BlockSpec(c.shape, lambda i: (0, 0)),
                pl.BlockSpec((d.shape[0], step), lambda i: (0, i)),
            ]
            arrays += [c, d]
    return pl.pallas_call(
        body,
        grid=(cols // step,),
        in_specs=specs
        + [
            pl.BlockSpec((1, rows, rows), lambda i: (slab, 0, 0)),
            pl.BlockSpec((1, 3, 128, 128), lambda i: (slot, i, 0, 0)),
        ],
        out_specs=[
            pl.BlockSpec((rows, step), lambda i: (0, i)),
            pl.BlockSpec((8, 128), lambda i: (0, 0)),
        ],
        out_shape=(
            jax.ShapeDtypeStruct((rows, cols), f32),
            jax.ShapeDtypeStruct((8, 128), f32),
        ),
        compiler_params=pltpu.CompilerParams(vmem_limit_bytes=VMEM_BYTES),
        cost_estimate=BRIEF,
        name="turn",
    )(*arrays, left, right)


def kernel_update(rates, factor, weight, one, two, left, right, *rest):
    turned = rest[: len(rates)]
    new_o, one_o, two_o, low_o = rest[len(rates) :]
    slab = pl.program_id(0)
    g = turned[0][...]
    rate = jnp.float32(rates[0])
    for n in range(1, len(rates)):
        g = jnp.where(slab == n, turned[n][...], g)
        rate = jnp.where(slab == n, jnp.float32(rates[n]), rate)
    first, second, step = adam_moments(g * factor[0], one[0], two[0])
    one_o[0] = first
    two_o[0] = second
    cols = step.shape[1]
    back = jnp.concatenate(
        [
            precise(step[:, c * 128 : (c + 1) * 128], right[0, c], ((1,), (1,)))
            for c in range(cols // 128)
        ],
        1,
    )
    back = precise(left[0], back, ((1,), (0,)))
    held = weight[0]
    new = held - rate * (back + 0.01 * held)
    new_o[0] = new
    low_o[0] = new.astype(bf16)


def update(factor, weight, one, two, first_slab, left, right, turned, rates):
    slabs, rows, cols = weight.shape
    step = 6 * 128 if cols % (6 * 128) == 0 else 3 * 128
    tile = pl.BlockSpec((1, rows, step), lambda s, i: (s, 0, i))
    own = [
        pl.BlockSpec((rows, step), lambda s, i, n=n: (0, jnp.where(s == n, i, 0)))
        for n in range(slabs)
    ]
    return pl.pallas_call(
        functools.partial(kernel_update, rates),
        grid=(slabs, cols // step),
        in_specs=[
            pl.BlockSpec(memory_space=pltpu.SMEM),
            tile,
            tile,
            tile,
            pl.BlockSpec((1, rows, rows), lambda s, i: (first_slab + s, 0, 0)),
            pl.BlockSpec((1, step // 128, 128, 128), lambda s, i: (s, i, 0, 0)),
        ]
        + own,
        out_specs=[tile] * 4,
        out_shape=[jax.ShapeDtypeStruct(weight.shape, f32)] * 3
        + [jax.ShapeDtypeStruct(weight.shape, bf16)],
        compiler_params=pltpu.CompilerParams(vmem_limit_bytes=VMEM_BYTES),
        cost_estimate=BRIEF,
        name="update",
    )(factor, weight, one, two, left, right, *turned)


def sum_near(near, away):
    near = near.astype(f32) + swap(away, "head", 1).astype(f32)
    return near[0] + swap(near[1].astype(bf16), "head", 2).astype(f32)


def to_frames(x):
    f = lax.axis_index("frame")
    out = []
    for d in range(x.shape[0]):
        piece = lax.dynamic_index_in_dim(x, f ^ d, 0, False)
        out.append(swap(piece, "frame", d) if d else piece)
    return jnp.stack(out)


def scatter_deep(x):
    mine = lax.axis_index("frame") >> 1
    total = lax.dynamic_index_in_dim(x, mine, 0, False)
    low = x.astype(bf16)
    for d in range(1, x.shape[0]):
        send = lax.dynamic_index_in_dim(low, mine ^ d, 0, False)
        total = total + swap(send, "frame", 2 * d).astype(f32)
    return total


def per_device(
    features, lengths, loss_mask, sq_weight, sq_first, sq_second, ffn_weight, ffn_first,
    ffn_second, left_bases, right_sq, right_ffn, latents, lat_first, lat_second, time_embed,
    time_first, time_second, gains, gain_first, gain_second,
):
    videos, frames_dev, patches, cols = features.shape
    lat_count, depth = latents.shape
    heads_dev = cols // HEAD_SIZE
    head_size = lax.axis_size("head")
    frame_size = lax.axis_size("frame")
    videos_dev = videos // head_size
    rows_dev = sq_weight.shape[1]
    scale = HEAD_SIZE ** (-0.5)
    f = lax.axis_index("frame")
    h = lax.axis_index("head")
    first_frame = (f == 0).astype(f32)
    first_head = (h == 0).astype(f32)
    share = videos_dev * lat_count // frame_size
    tokens_video = frames_dev * patches

    chunks = len(chunks_of(frames_dev)[0])
    feat = features.reshape(videos, tokens_video, cols)

    with jax.named_scope("weights"):
        sq_low = sq_weight.astype(bf16)
        ffn_low = ffn_weight.astype(bf16)
        zhat_zero, zrstd_zero = normalize_rows(latents)
        normed_lat = (zhat_zero * gains[1]).astype(bf16)
        normed_own = lax.dynamic_slice_in_dim(normed_lat, f * rows_dev, rows_dev, 1)
        kv_own = jnp.concatenate([sq_low[1], sq_low[2]], 1)
        kv_far = swap(kv_own, "head", 2)
        low_side = (h & 2) == 0
        kv_rows = jnp.concatenate(
            [jnp.where(low_side, kv_own, kv_far), jnp.where(low_side, kv_far, kv_own)], 1
        )
        away, near = zip(
            *[pick(feat, h, j, c, videos_dev) for j in range(videos_dev) for c in range(chunks)]
        )
        slabs, blocks_dev, bl, _ = left_bases.shape
        left = (
            left_bases[:, :, :, None, :] * jnp.eye(blocks_dev, dtype=f32)[None, :, None, :, None]
        ).reshape(slabs, rows_dev, rows_dev)
        opening = gate(away[0], kv_far)
        query = nn(normed_own, sq_low[0])
        bit = 1
        while bit < frame_size:
            query = query + swap(query, "frame", bit)
            if bit == 1:
                held = sum((zero_of(n) for n in near[1:]), zero_of(opening))
                query = query + held.astype(f32)
            bit *= 2
        query = query.astype(bf16)
        even_core = (h & 1) == 0
        q_all = gather_head(query, 1)
        time_full = gather_head(time_embed, 1)

    with jax.named_scope("exchange"):
        crossed = [swap(opening, "head", 2)]
        waiting = [opening] + [gate(n, crossed[0], q_all, time_full) for n in away[1:2]]

    with jax.named_scope("weights"):
        kv_half = lax.all_gather(kv_rows, "frame", axis=0, tiled=True)
        kv_half = kv_half + (zero_of(waiting[-1]) + zero_of(left)).astype(bf16)
        kv_away = swap(kv_half, "head", 1)
        even = jnp.where(even_core, kv_half, kv_away)
        odd = jnp.where(even_core, kv_away, kv_half)
        w_key, w_value = (
            jnp.concatenate(
                [
                    side[:, at : at + cols]
                    for at in (n * cols, (n + 2) * cols)
                    for side in (even, odd)
                ],
                1,
            )
            for n in (0, 1)
        )
        rest = lax.all_gather(
            after(
                jnp.concatenate([sq_low[0], sq_low[3], sq_low[4], ffn_low[0], ffn_low[1]], 1), kv_half
            ),
            "frame",
            axis=0,
            tiled=True,
        )
        w_query, w_outt, w_dec = (rest[:, n * cols : (n + 1) * cols] for n in range(3))
        hid = ffn_low.shape[2]
        w_up = rest[:, 3 * cols : 3 * cols + hid]
        w_downt = rest[:, 3 * cols + hid :]
        w_key_own = jnp.where(low_side, kv_half[:, :cols], kv_half[:, 2 * cols : 3 * cols])
        w_value_own = jnp.where(low_side, kv_half[:, cols : 2 * cols], kv_half[:, 3 * cols :])

    with jax.named_scope("latent_keys"):
        lat_key = nn(normed_lat, w_key_own).astype(bf16).reshape(lat_count, heads_dev, HEAD_SIZE)
        lat_value = nn(normed_lat, w_value_own).astype(bf16).reshape(lat_count, heads_dev, HEAD_SIZE)
        qw = absorb(q_all, w_key, scale)

    with jax.named_scope("read"):
        own_lens = lax.dynamic_slice_in_dim(lengths, h * videos_dev, videos_dev, 0)
        state = None
        parts = videos_dev * chunks
        token = qw
        for n in range(parts):
            j, c = divmod(n, chunks)
            passed = crossed[n][1] if n < 2 else gate(crossed[n][1], token)
            got = [swap(near[n], "head", 1), crossed[n].reshape(-1, cols), swap(passed, "head", 1)]
            if n + 1 < parts:
                crossed.append(swap(waiting[n + 1], "head", 2))
            if n + 2 < parts and n % 2 == 0:
                waiting.append(gate(away[n + 2], crossed[n + 1], token))
            *state, token = read_pass(
                j, c, state, feat, got, time_full, gains[0:1], own_lens[j], qw, w_value,
                waiting[-1], h, videos_dev,
            )
            if n + 2 < parts and n % 2 == 1:
                waiting.append(gate(away[n + 2], crossed[n + 1], token))
        xn_all, ft_all, e_all, px_all, st_all, o_all = state

    with jax.named_scope("combine"):
        heads = depth // HEAD_SIZE
        lse_parts = (
            (st_all[:, 126] + jnp.log(st_all[:, 127]))
            .reshape(videos_dev, chunks, heads, lat_count)
            .transpose(1, 0, 3, 2)
            .reshape(chunks, videos_dev * lat_count, heads)
        )
        o_parts = o_all.reshape(videos_dev, chunks, lat_count, heads, HEAD_SIZE)
        o_parts = o_parts.transpose(1, 0, 2, 3, 4).reshape(chunks, -1, heads, HEAD_SIZE)
        lse_local = jax.nn.logsumexp(lse_parts, 0)
        o_local = jnp.sum(o_parts * jnp.exp(lse_parts - lse_local)[..., None], 0)
        pay = jnp.concatenate(
            [o_local.reshape(-1, depth).astype(bf16), split_three(lse_local)], 1
        ).reshape(frame_size, share, depth + 3 * heads)
        pay = to_frames(pay)
        lse_each = join_three(pay[..., depth:])
        o_each = pay[..., :depth].astype(f32).reshape(frame_size, share, heads, HEAD_SIZE)
        top = jnp.max(lse_each, 0)
        weight = jnp.exp(lse_each - top)
        total = jnp.sum(weight, 0)
        o_tok = jnp.sum(o_each * weight[..., None], 0) / total[..., None]
        lse_tok = top + jnp.log(total)
        o_heads = o_tok.reshape(share, head_size, cols).transpose(1, 0, 2).astype(bf16)
        l_heads = split_three(lse_tok.reshape(share, head_size, heads_dev).transpose(1, 0, 2))
        pay = lax.all_to_all(jnp.concatenate([o_heads, l_heads], 2), "head", 0, 0, tiled=True)
        lse_tok = join_three(pay[..., cols:])
        o_tok = pay[..., :cols].astype(f32).reshape(head_size, share, heads_dev, HEAD_SIZE)
        first_row = lax.rem(f * share, lat_count)
        q_rows = lax.dynamic_slice_in_dim(query, first_row, share, 0).reshape(
            share, heads_dev, HEAD_SIZE
        )
        lat_scores = (
            jnp.einsum("rnd,jnd->rnj", q_rows, lat_key, preferred_element_type=f32) * scale
        )
        lse = jnp.logaddexp(lse_tok, jax.nn.logsumexp(lat_scores, -1)[None])
        lat_prob = jnp.exp(lat_scores[None] - lse[..., None])
        attn = o_tok * jnp.exp(lse_tok - lse)[..., None] + jnp.einsum(
            "srnj,jnd->srnd", lat_prob, lat_value.astype(f32), precision=HIGH_ACCURACY
        )
        rows = head_size * share
        attn_low = attn.reshape(rows, cols).astype(bf16)

    with jax.named_scope("latent_forward"):
        lat_rows = jnp.tile(lax.dynamic_slice_in_dim(latents, first_row, share, 0), (head_size, 1))
        z_one = lat_rows + sum_head(nt(attn_low, w_outt))
        z1hat, z1rstd = normalize_rows(z_one)
        ffn_in = (z1hat * gains[2]).astype(bf16)
        pre = nn(ffn_in, w_up)
        hidden = jax.nn.gelu(pre).astype(bf16)
        z_two = z_one + sum_head(nt(hidden, w_downt))
        z2hat, z2rstd = normalize_rows(z_two)
        final = (z2hat * gains[3]).astype(bf16)
        dec = jnp.concatenate([nn(final, w_query), nn(final, w_dec)], 1).astype(bf16)

    def to_tokens(x):
        x = lax.all_to_all(x.reshape(head_size, share, -1), "head", 0, 0, tiled=True)
        x = x.transpose(1, 0, 2)
        x = jnp.broadcast_to(x[None], (frame_size,) + x.shape)
        x = lax.all_to_all(x, "frame", 0, 0, tiled=True)
        return x.reshape(videos_dev * lat_count, head_size, -1)

    with jax.named_scope("decode"):
        dec_all = to_tokens(dec)
        dq_all = dec_all[..., :cols].reshape(videos_dev * lat_count, depth)
        dv_all = dec_all[..., cols:].reshape(videos_dev * lat_count, depth)
        own_mask = lax.dynamic_slice_in_dim(loss_mask, h * videos_dev, videos_dev, 0).astype(f32)
        counts = own_mask.reshape(videos_dev * tokens_video, 1)
        decoded = [
            decode_pass(j, xn_all, ft_all, counts, dq_all, dv_all, w_key, scale, videos_dev)
            for j in range(videos_dev)
        ]
        loss_part = sum(jnp.sum(d[4]) for d in decoded)
        count_part = jnp.sum(own_mask)
        dec_side = sum(d[3] for d in decoded)

    with jax.named_scope("latent_backward"):
        ddec = jnp.concatenate(
            [
                jnp.concatenate([d[n] for d in decoded], 0).reshape(frame_size, share, head_size, cols)
                for n in (0, 1)
            ],
            3,
        ).astype(bf16)
        ddec = to_frames(ddec.reshape(frame_size, share, -1)).astype(f32)
        ddec = jnp.sum(ddec, 0).astype(bf16).reshape(share, head_size, 2 * cols).transpose(1, 0, 2)
        ddec = lax.all_to_all(ddec, "head", 0, 0, tiled=True).reshape(rows, 2 * cols)
        ddq_low, ddv_low = (ddec[:, :cols], ddec[:, cols:])
        dfinal = sum_head(nt(ddq_low, w_query) + nt(ddv_low, w_dec))
        dz_two = norm_reverse(dfinal, z2hat, z2rstd, gains[3])
        dz2_low = dz_two.astype(bf16)
        _, gelu_back = jax.vjp(jax.nn.gelu, pre)
        dpre = gelu_back(nn(dz2_low, w_downt))[0].astype(bf16)
        dffn_in = sum_head(nt(dpre, w_up))
        dz_one = dz_two + norm_reverse(dffn_in, z1hat, z1rstd, gains[2])
        dz1_low = dz_one.astype(bf16)
        dattn = nn(dz1_low, w_outt).astype(bf16)
        dattn_heads = dattn.astype(f32).reshape(head_size, share, heads_dev, HEAD_SIZE)
        delta = jnp.sum(dattn_heads * attn, -1)
        pay = jnp.concatenate(
            [
                dattn,
                split_three(lse.reshape(rows, heads_dev)),
                split_three(delta.reshape(rows, heads_dev)),
            ],
            1,
        )
        pay = to_tokens(pay)
        do_all = pay[..., :cols].reshape(videos_dev * lat_count, depth)

        both = join_three(pay[..., cols:].reshape(-1, head_size, 2, 3 * heads_dev))
        both = both.transpose(0, 2, 1, 3).reshape(videos_dev * lat_count, 2 * heads)
        ld = jnp.pad(both, ((0, 0), (0, 128 - 2 * heads)))

    with jax.named_scope("latent_pairs"):
        lat_value_f = lat_value.astype(f32)
        lat_dprob = jnp.einsum("srnd,jnd->srnj", dattn_heads, lat_value_f, precision=HIGH_ACCURACY)
        lat_dscore = lat_prob * (lat_dprob - delta[..., None]) * scale
        dq_lat = jnp.einsum(
            "srnj,jnd->rnd", lat_dscore, lat_key.astype(f32), precision=HIGH_ACCURACY
        ).reshape(share, cols)
        dk_lat = jnp.einsum(
            "srnj,rnd->jnd", lat_dscore, q_rows.astype(f32), precision=HIGH_ACCURACY
        ).reshape(lat_count, cols)
        dv_lat = jnp.einsum(
            "srnj,srnd->jnd", lat_prob, dattn_heads, precision=HIGH_ACCURACY
        ).reshape(lat_count, cols)
        dk_lat_low = dk_lat.astype(bf16)
        dv_lat_low = dv_lat.astype(bf16)
        pairs = jnp.concatenate([dk_lat, dv_lat], 0)
        lat_part = jnp.concatenate(
            [
                jnp.sum(dz_one.reshape(head_size, share, depth), 0),
                jnp.sum(dffn_in * z1hat, 0)[None],
                jnp.sum(dfinal * z2hat, 0)[None],
                jnp.zeros((6, depth), f32),
            ],
            0,
        )
        lat_parts = lax.all_gather(lat_part, "frame")
        lat_direct = jnp.sum(
            lat_parts[:, :share].reshape(videos_dev, lat_count, depth), 0
        )
        gain_rows = jnp.sum(lat_parts[:, share : share + 2], 0)

    with jax.named_scope("row_gradients"):
        wide_a = lax.all_gather(
            jnp.concatenate([hidden, attn_low], 1), "frame", axis=0, tiled=True
        )
        wide_b = lax.all_gather(
            jnp.concatenate([dpre, ddq_low, ddv_low], 1), "frame", axis=0, tiled=True
        )

        own_cols = jnp.stack(
            [a.reshape(rows, frame_size, rows_dev) for a in (ffn_in, final, dz2_low, dz1_low)]
        ).transpose(2, 0, 1, 3)
        own_cols = lax.all_to_all(own_cols, "frame", 0, 0, tiled=True)

    with jax.named_scope("value"):
        ow, dwv_own, dwv_other, value_side = value_pass(do_all, w_value, px_all, st_all, ld, h, videos_dev)
        side = dec_side + jnp.concatenate(
            [value_side[:TAIL], jnp.zeros((TAIL, depth), f32), value_side[TAIL:]], 0
        )

    half = head_size // 2
    back = functools.partial(
        back_pass, e_all=e_all, ld=ld, ow=ow, qw=qw, q_all=q_all, wk=w_key, dq_all=dq_all,
        dxs=[d[2] for d in decoded], scale=scale, h=h, videos_dev=videos_dev,
    )

    with jax.named_scope("value_gradient"):
        dwv = dwv_own.astype(f32) + swap(dwv_other, "head", 1).astype(f32)
        dwv_pay = dwv[1].astype(bf16)
        dwv_far = swap(dwv_pay, "head", 2)

    with jax.named_scope("back"):
        xn_all = gate(xn_all, dwv_pay)
        far_dq, far_near, far_away, far_side = back(
            True, xn_all, st_all=st_all, sides=None, gain=None
        )

    with jax.named_scope("value_gradient"):
        dwv = dwv[0] + dwv_far.astype(f32) + tn(dv_lat_low, normed_lat)
        dwv = dwv.T.reshape(frame_size // 2, 2, rows_dev, cols)
        dwv_away = lax.dynamic_index_in_dim(dwv, 1 - (f & 1), 1, False).astype(bf16)
        dwv_near = lax.dynamic_index_in_dim(dwv, f & 1, 1, False)
        dwv_x = swap(dwv_away, "frame", 1)

    with jax.named_scope("key_gradient"):
        far_sum = far_near.astype(f32) + swap(far_away, "head", 1).astype(f32)
        dq_sum = far_dq[0] + swap(far_dq[1], "head", 1)
        dwk_pay = far_sum.astype(bf16)
        dwk_far = swap(dwk_pay, "head", 2)
        dq_far = swap(dq_sum, "head", 2)

    with jax.named_scope("back"):
        xn_all = gate(xn_all, dwk_pay, dq_sum, dwv_away)
        own_dq, own_near, own_away, pack = back(
            False, xn_all, st_all=st_all, sides=[side, far_side],
            gain=gains[0:1],
        )

    with jax.named_scope("value_gradient"):
        grad_value = scatter_deep(dwv_near + dwv_x.astype(f32))

    with jax.named_scope("key_gradient"):
        key_sum = own_near.astype(f32) + swap(own_away, "head", 1).astype(f32)
        key_sum = key_sum + dwk_far.astype(f32) + tn(dk_lat_low, normed_lat)
        key_sum = key_sum.T.reshape(frame_size // 2, 2, rows_dev, cols)
        key_away = lax.dynamic_index_in_dim(key_sum, 1 - (f & 1), 1, False).astype(bf16)
        key_near = lax.dynamic_index_in_dim(key_sum, f & 1, 1, False)
        key_half = key_near + swap(key_away, "frame", 1).astype(f32)

    with jax.named_scope("patch_gradients"):
        dq_pad = lax.dynamic_update_slice_in_dim(
            jnp.zeros((lat_count, cols), f32), dq_lat, first_row, 0
        )
        dquery = own_dq[0] + swap(own_dq[1], "head", 1) + dq_far + dq_pad
        dquery = jnp.concatenate([dquery + zero_of(key_away).astype(f32), pairs], 0)
        dquery = sum_rounded(dquery, "frame").astype(bf16)
        dquery, dk_sum, dv_sum = (
            dquery[n * lat_count : (n + 1) * lat_count] for n in range(3)
        )

    with jax.named_scope("key_gradient"):
        grad_key = scatter_deep(key_half)

    with jax.named_scope("patch_gradients"):
        pack = sum_near(pack[:half], pack[half:])
        time_own = pack[:frames_dev]
        gain0_own = sum_over(jnp.sum(pack[TAIL:], 0)[None], "frame")[0]
        dzn = sum_head(nt(dquery, w_query) + nt(dk_sum, w_key_own) + nt(dv_sum, w_value_own))
        grad_gain1 = jnp.sum(dzn * zhat_zero, 0)
        lat_grad = lat_direct + norm_reverse(dzn, zhat_zero, zrstd_zero, gains[1])
        gain_rest = jnp.concatenate([grad_gain1[None], gain_rows], 0)
        gain_grad = jnp.concatenate(
            [gain0_own[None], lax.dynamic_slice_in_dim(gain_rest, h * cols, cols, 1)], 0
        )

    with jax.named_scope("update"):
        own_cols = gate(own_cols, key_away)
        sq = functools.partial(turn, rows=rows_dev, cols=cols, left=left, right=right_sq)
        ffn = functools.partial(turn, rows=rows_dev, cols=hid, left=left, right=right_ffn)
        turned, totals = zip(
            sq(0, 0, (own_cols, 1, wide_b, hid, normed_own, dquery)),
            sq(1, 1, (grad_key,)),
            sq(2, 2, (grad_value,)),
            sq(3, 3, (own_cols, 3, wide_a, hid)),
            sq(4, 4, (own_cols, 1, wide_b, hid + cols)),
            ffn(5, 0, (own_cols, 0, wide_b, 0)),
            ffn(6, 1, (own_cols, 2, wide_a, 0)),
        )
        squares = (
            jnp.sum(sum(totals))
            + jnp.sum(time_own * time_own)
            + first_frame * first_head * jnp.sum(lat_grad * lat_grad)
            + first_frame * jnp.sum(gain_grad * gain_grad)
        )
        sums = jnp.pad(jnp.stack([loss_part, count_part, squares])[None], ((0, 7), (0, 125)))
        sums = sum_over(sum_over(sums, "head"), "frame")
        loss_sum, masked_count, squares = (sums[0, 0], sums[0, 1], sums[0, 2])
        grad_norm = jnp.sqrt(squares) / masked_count
        factor = jnp.minimum(1.0, clip_max / grad_norm) / masked_count
        out_rate = ((FRAMES * PATCH + LATENTS) / 64.0) ** 0.5
        ffn_out = update(
            factor[None], ffn_weight, ffn_first, ffn_second, 5, left, right_ffn, turned[5:],
            (0.02, 0.02),
        )
        sq_out = update(
            factor[None], sq_weight, sq_first, sq_second, 0, left, right_sq, turned[:5],
            (0.02, 0.02, 0.02, 0.02 * out_rate, 0.02),
        )
        lat_out = adamw_update(latents, lat_grad * factor, lat_first, lat_second, 0.01)
        time_out = adamw_update(time_embed, time_own * factor, time_first, time_second, 0.01)
        gain_own = lax.dynamic_slice_in_dim(gains, h * cols, cols, 1)
        gain_out = adamw_update(gain_own, gain_grad * factor, gain_first, gain_second, 0.0)
    return (loss_sum, masked_count, grad_norm, *sq_out, *ffn_out, *lat_out, *time_out, *gain_out)


def solution(mesh):
    matrix = P(None, "frame", "head")
    frame_rows = P("frame", "head")
    by_head = P(None, "head")
    placed = (
        P(None, "frame", None, "head"),
        P(None, "frame"),
        P(None, "frame", None),
        matrix, matrix, matrix, matrix, matrix, matrix,
        P(None, "frame", None, None),
        P(None, "head", None, None),
        P(None, "head", None, None),
        P(), P(), P(),
        frame_rows, frame_rows, frame_rows,
        P(), by_head, by_head,
    )
    outs = (
        P(), P(), P(),
        matrix, matrix, matrix, matrix, matrix, matrix, matrix, matrix,
        P(), P(), P(),
        frame_rows, frame_rows, frame_rows,
        by_head, by_head, by_head,
    )
    return jax.shard_map(per_device, mesh=mesh, in_specs=placed, out_specs=outs, check_vma=False)
```

```python
import functools

import jax
import jax.numpy as jnp
from jax import lax
from jax.experimental import pallas as pl
from jax.experimental.pallas import tpu as pltpu
from jax.sharding import PartitionSpec as P

HEAD_SIZE = 96
LATENTS = 64
PATCH = 256
FRAMES = 96
STEP = 5
GROUP = 4
EXTRA = 128
TAIL = 16
VMEM_BYTES = 62 * 1024 * 1024

HIGH_ACCURACY = lax.Precision.HIGHEST
clip_max = 0.05
beta_one = 0.5
beta_two = 0.6
adam_eps = 1e-08
BRIEF = pl.CostEstimate(flops=1, bytes_accessed=1, transcendentals=0)
f32 = jnp.float32
bf16 = jnp.bfloat16


def nn(a, b):
    return lax.dot_general(a, b, (((1,), (0,)), ((), ())), preferred_element_type=f32)


def nt(a, b):
    return lax.dot_general(a, b, (((1,), (1,)), ((), ())), preferred_element_type=f32)


def tn(a, b):
    return lax.dot_general(a, b, (((0,), (0,)), ((), ())), preferred_element_type=f32)


def normalize_rows(v):
    cent = v - jnp.mean(v, -1, keepdims=True)
    rstd = lax.rsqrt(jnp.mean(cent * cent, -1, keepdims=True) + 1e-05)
    return (cent * rstd, rstd)


def norm_reverse(dy, xhat, rstd, gain):
    scaled = dy * gain
    first = jnp.mean(scaled, -1, keepdims=True)
    second = jnp.mean(scaled * xhat, -1, keepdims=True)
    return rstd * (scaled - first - xhat * second)


def adam_moments(grad, one, two):
    one = beta_one * one + (1.0 - beta_one) * grad
    two = beta_two * two + (1.0 - beta_two) * grad * grad
    step = one / (1.0 - beta_one**STEP) / (jnp.sqrt(two / (1.0 - beta_two**STEP)) + adam_eps)
    return (one, two, step)


def adamw_update(weight, grad, one, two, decay):
    one, two, step = adam_moments(grad, one, two)
    return (weight - 0.3 * (step + decay * weight), one, two)


def swap(x, axis, bit):
    size = lax.axis_size(axis)
    return lax.ppermute(x, axis, [(i, i ^ bit) for i in range(size)])


def sum_over(x, axis):
    bit = 1
    while bit < lax.axis_size(axis):
        x = x + swap(x, axis, bit)
        bit *= 2
    return x


def sum_rounded(x, axis):
    bit = 1
    while bit < lax.axis_size(axis):
        x = lax.reduce_precision(x, 8, 7)
        x = x + swap(x.astype(bf16), axis, bit).astype(f32)
        bit *= 2
    return x


def sum_head(x):
    x = x + swap(x, "head", 1)
    x = lax.reduce_precision(x, 8, 7)
    return x + swap(x.astype(bf16), "head", 2).astype(f32)


def gather_head(x, axis):
    me = lax.axis_index("head")
    bit = 1
    while bit < lax.axis_size("head"):
        away = swap(x, "head", bit)
        mine_first = (me & bit) == 0
        x = jnp.concatenate(
            [jnp.where(mine_first, x, away), jnp.where(mine_first, away, x)], axis
        )
        bit *= 2
    return x


def zero_of(x):
    return (x[(0,) * x.ndim].astype(f32) * 0.0).astype(jnp.int32)


def after(x, *deps):
    return lax.optimization_barrier((x, *deps))[0]


def split_three(x):
    high = lax.reduce_precision(x, 8, 7)
    rest = x - high
    mid = lax.reduce_precision(rest, 8, 7)
    return jnp.concatenate([high, mid, rest - mid], -1).astype(bf16)


def join_three(x):
    n = x.shape[-1] // 3
    x = x.astype(f32)
    return x[..., :n] + x[..., n : 2 * n] + x[..., 2 * n :]


def head_of_lane(rows, cols):
    return lax.broadcasted_iota(jnp.int32, (rows, cols), 1) // HEAD_SIZE


def spread(x):
    owner = head_of_lane(*x.shape)
    x = x.astype(f32)
    return jnp.concatenate([jnp.where(owner == j, x, 0.0) for j in range(GROUP)], 0).astype(bf16)


def collect(r):
    rows = r.shape[0] // GROUP
    owner = head_of_lane(rows, r.shape[1])
    out = jnp.where(owner == 0, r[:rows], 0.0)
    for j in range(1, GROUP):
        out = out + jnp.where(owner == j, r[j * rows : (j + 1) * rows], 0.0)
    return out


def whole(shape):
    return pl.BlockSpec(shape, lambda *_: (0,) * len(shape), pipeline_mode=pl.Buffered(1))


def kernel_absorb(scale, x_ref, w_ref, out_ref):
    out_ref[...] = (nt(spread(x_ref[...]), w_ref[...]) * scale).astype(bf16)


def absorb(x, w, scale):
    depth, width = w.shape
    cols = GROUP * HEAD_SIZE
    groups = width // cols
    rows = GROUP * LATENTS
    return pl.pallas_call(
        functools.partial(kernel_absorb, scale),
        grid=(groups,),
        in_specs=[
            pl.BlockSpec((LATENTS, cols), lambda g: (0, g)),
            pl.BlockSpec((depth, cols), lambda g: (0, g)),
        ],
        out_specs=pl.BlockSpec((rows, depth), lambda g: (g, 0)),
        out_shape=jax.ShapeDtypeStruct((groups * rows, depth), bf16),
        compiler_params=pltpu.CompilerParams(vmem_limit_bytes=VMEM_BYTES),
        cost_estimate=BRIEF,
        name="absorb",
    )(x, w)


def kernel_pick(place, a, b, c, far_o, near_o):
    del place
    far_o[0] = a[...]
    far_o[1] = b[...]
    near_o[...] = c[...]


def pick(feat, place, j, c, videos_dev):
    count, tokens_video, cols = feat.shape
    frames_dev = tokens_video // PATCH
    cuts, nf = chunks_of(frames_dev)
    step = nf * PATCH
    blocks = cuts[c] // nf
    start = (j * frames_dev + sum(cuts[:c])) // nf
    tokens = cuts[c] * PATCH
    feat2 = feat.reshape(count * tokens_video, cols)

    def spot(k):
        return lambda i, p: ((p[0] ^ k) * (videos_dev * frames_dev // nf) + start + i, 0)

    return pl.pallas_call(
        kernel_pick,
        grid_spec=pltpu.PrefetchScalarGridSpec(
            num_scalar_prefetch=1,
            grid=(blocks,),
            in_specs=[pl.BlockSpec((step, cols), spot(k)) for k in (2, 3, 1)],
            out_specs=[
                pl.BlockSpec((2, step, cols), lambda i, p: (0, i, 0)),
                pl.BlockSpec((step, cols), lambda i, p: (i, 0)),
            ],
        ),
        out_shape=[
            jax.ShapeDtypeStruct((2, tokens, cols), bf16),
            jax.ShapeDtypeStruct((tokens, cols), bf16),
        ],
        compiler_params=pltpu.CompilerParams(vmem_limit_bytes=VMEM_BYTES),
        cost_estimate=BRIEF,
        name="pick",
    )(place[None], feat2, feat2, feat2)


def kernel_gate(*refs):
    del refs


def gate(x, *deps):
    anyspec = pl.BlockSpec(memory_space=pl.ANY)
    return pl.pallas_call(
        kernel_gate,
        in_specs=[anyspec] * (1 + len(deps)),
        out_specs=anyspec,
        out_shape=jax.ShapeDtypeStruct(x.shape, x.dtype),
        input_output_aliases={0: 0},
        cost_estimate=BRIEF,
        name="gate",
    )(x, *deps)


def frames_a_block(frames):
    return 2 if frames % 2 == 0 else 1


def chunks_of(frames):
    if frames % 6 == 0:
        return (frames // 3 * 2, frames // 3), frames // 3
    return (frames,), 1


def kernel_read(
    nf, first, carry, final, place, own, ra, rb, rc, time_ref, g0, qw, wv, xn_in, ft_in, e_in, px_in, st_in, o_in, dep,
    xn_o, ft_o, e_o, px_o, st_o, o_o, token_o, xs, acc, run,
):
    del xn_in, ft_in, e_in, o_in, dep
    i = pl.program_id(0)
    tokens, depth = xs.shape
    cols = own.shape[1]
    heads_rows = GROUP * LATENTS
    groups = qw.shape[0] // heads_rows

    @pl.when(i == 0)
    def _():
        if carry:
            acc[...] = px_in[...].astype(f32)
            run[0] = jnp.broadcast_to(st_in[:, 126:127], run.shape[1:])
            run[1] = jnp.broadcast_to(st_in[:, 127:128], run.shape[1:])
            st_o[...] = st_in[...]
        else:
            acc[...] = jnp.zeros_like(acc)
            run[0] = jnp.full(run.shape[1:], -1e30, f32)
            run[1] = jnp.zeros(run.shape[1:], f32)
            st_o[...] = jnp.zeros_like(st_o)

    for k, part in enumerate((own, ra, rb, rc)):
        off = pl.multiple_of((place[0] ^ k) * cols, 128)
        for f in range(nf):
            rows = slice(f * PATCH, (f + 1) * PATCH)
            raw = part[rows, :]
            ft_o[rows, pl.ds(off, cols)] = raw
            row = first + i * nf + f
            moved = raw.astype(f32) + time_ref[pl.ds(row, 1), pl.ds(off, cols)]
            xs[rows, pl.ds(off, cols)] = moved.astype(bf16)
    x = xs[...].astype(f32)
    cent = x - jnp.sum(x, -1, keepdims=True) * (1.0 / depth)
    rstd = lax.rsqrt(jnp.sum(cent * cent, -1, keepdims=True) * (1.0 / depth) + 1e-05)
    xn_o[:, :depth] = (cent * rstd * g0[...]).astype(bf16)
    lane = lax.broadcasted_iota(jnp.int32, (tokens, EXTRA), 1)
    frame = lax.broadcasted_iota(jnp.int32, (tokens, EXTRA), 0) // PATCH + first + i * nf
    xn_o[:, depth:] = jnp.where(lane == frame, rstd, 0.0).astype(bf16)
    key = lax.broadcasted_iota(jnp.int32, (1, tokens), 1)
    limit = place[1 + first + i * nf]
    for f in range(1, nf):
        limit = jnp.where(key >= f * PATCH, f * PATCH + place[1 + first + i * nf + f], limit)
    valid = key < limit
    block = lax.broadcasted_iota(jnp.int32, (heads_rows, 128), 1)
    last = i == pl.num_programs(0) - 1
    for g in range(groups):
        rows = slice(g * heads_rows, (g + 1) * heads_rows)
        scores = jnp.where(valid, nt(qw[rows, :], xn_o[:, :depth]), -1e30)
        old = run[0, rows, :]
        new = jnp.maximum(old, jnp.max(scores, -1, keepdims=True))
        expo = jnp.exp(scores - new[:, :1])
        shrink = jnp.exp(old - new)
        total = run[1, rows, :] * shrink + jnp.sum(expo, -1, keepdims=True)
        run[0, rows, :] = new
        run[1, rows, :] = total
        low = expo.astype(bf16)
        e_o[rows, :] = low
        stats = jnp.where(block == first // nf + i, new, st_o[rows, :])
        stats = jnp.where(last & (block == 126), new, stats)
        st_o[rows, :] = jnp.where(last & (block == 127), total, stats)
        acc[rows, :] = acc[rows, :] * shrink[:, :1] + nn(low, xn_o[...])

    @pl.when(last)
    def _():
        for g in range(groups):
            rows = slice(g * heads_rows, (g + 1) * heads_rows)
            wide = slice(g * cols, (g + 1) * cols)
            held = acc[rows, :].astype(bf16)
            px_o[rows, :] = held
            if final:
                mixed = nn(held[:, :depth], wv[:, wide]) * (1.0 / run[1, rows, :1])
                o_o[:, wide] = collect(mixed)
        if not final:
            o_o[...] = jnp.zeros_like(o_o)
        token_o[...] = run[1, 0:8, :]


def read_pass(j, c, prev, feat, got, time_full, gain, lens, qw, wv, dep, h, videos_dev):
    count, tokens_video, cols = feat.shape
    depth = wv.shape[0]
    frames_dev = tokens_video // PATCH
    cuts, nf = chunks_of(frames_dev)
    chunks = len(cuts)
    frames = cuts[c]
    before = sum(cuts[:c])
    tokens = nf * PATCH
    blocks = frames // nf
    start = (j * frames_dev + before) // nf
    rows = qw.shape[0]
    place = jnp.concatenate([h[None], lens]).astype(jnp.int32)
    feat2 = feat.reshape(count * tokens_video, cols)
    shapes = (
        jax.ShapeDtypeStruct((videos_dev * tokens_video, depth + EXTRA), bf16),
        jax.ShapeDtypeStruct((videos_dev * tokens_video, depth), bf16),
        jax.ShapeDtypeStruct((videos_dev * rows, tokens_video), bf16),
        jax.ShapeDtypeStruct((videos_dev * rows, depth + EXTRA), bf16),
        jax.ShapeDtypeStruct((videos_dev * rows, 128), f32),
        jax.ShapeDtypeStruct((videos_dev * LATENTS, depth), f32),
    )
    aliases = {}
    if prev is None:
        prev = [jnp.zeros((16, 128), s.dtype) for s in shapes]
    else:
        aliases = {9 + n: n for n in range(6)}
    anyspec = pl.BlockSpec(memory_space=pl.ANY)
    one = pl.Buffered(1)
    return pl.pallas_call(
        functools.partial(kernel_read, nf, before, c > 0, c == chunks - 1),
        grid_spec=pltpu.PrefetchScalarGridSpec(
            num_scalar_prefetch=1,
            grid=(blocks,),
            in_specs=[
                pl.BlockSpec(
                    (tokens, cols),
                    lambda i, p: (p[0] * (videos_dev * frames_dev // nf) + start + i, 0),
                ),
                pl.BlockSpec((tokens, cols), lambda i, p: (i, 0)),
                pl.BlockSpec((tokens, cols), lambda i, p: (i, 0)),
                pl.BlockSpec((tokens, cols), lambda i, p: (i, 0)),
                whole(time_full.shape),
                whole(gain.shape),
                whole(qw.shape),
                whole(wv.shape),
            ]
            + [anyspec] * 3
            + (
                [
                    pl.BlockSpec((rows, depth + EXTRA), lambda i, p: (j, 0), pipeline_mode=one),
                    pl.BlockSpec((rows, 128), lambda i, p: (j, 0), pipeline_mode=one),
                ]
                if c
                else [anyspec] * 2
            )
            + [anyspec] * 2,
            out_specs=[
                pl.BlockSpec((tokens, depth + EXTRA), lambda i, p: (start + i, 0)),
                pl.BlockSpec((tokens, depth), lambda i, p: (start + i, 0)),
                pl.BlockSpec((rows, tokens), lambda i, p: (j, before // nf + i)),
                pl.BlockSpec((rows, depth + EXTRA), lambda i, p: (j, 0), pipeline_mode=one),
                pl.BlockSpec((rows, 128), lambda i, p: (j, 0), pipeline_mode=one),
                pl.BlockSpec((LATENTS, depth), lambda i, p: (j, 0), pipeline_mode=one),
                whole((8, 128)),
            ],
            scratch_shapes=[
                pltpu.VMEM((tokens, depth), bf16),
                pltpu.VMEM((rows, depth + EXTRA), f32),
                pltpu.VMEM((2, rows, 128), f32),
            ],
        ),
        out_shape=(*shapes, jax.ShapeDtypeStruct((8, 128), f32)),
        input_output_aliases=aliases,
        compiler_params=pltpu.CompilerParams(vmem_limit_bytes=VMEM_BYTES),
        cost_estimate=pl.CostEstimate(
            flops=rows * frames * PATCH * depth // 2,
            bytes_accessed=frames * PATCH * depth,
            transcendentals=rows * frames * PATCH,
        ),
        name="read_pass",
    )(place, feat2, *got, time_full, gain, qw, wv, *prev, dep)


def kernel_decode(
    nf, scale, xn, feat, msk, dq, dv, wk,
    ddq_o, ddv_o, dx_o, side_o, loss_o, dqw, dvd, sc, zs, acc, dacc, loss,
):
    i = pl.program_id(1)
    tokens = xn.shape[0]
    depth = wk.shape[0]
    heads_rows = GROUP * LATENTS
    total_rows = dqw.shape[0]
    groups = total_rows // heads_rows
    cols = depth // groups

    @pl.when(i == 0)
    def _():
        acc[...] = jnp.zeros_like(acc)
        dacc[...] = jnp.zeros_like(dacc)
        loss[...] = jnp.zeros_like(loss)
        for g in range(groups):
            rows = slice(g * heads_rows, (g + 1) * heads_rows)
            wide = slice(g * cols, (g + 1) * cols)
            dqw[rows, :] = (nt(spread(dq[:, wide]), wk[:, wide]) * scale).astype(bf16)
            dvd[g] = spread(dv[:, wide])

    sc[...] = nt(dqw[...], xn[:, :depth])
    counts = msk[...]
    second = jnp.zeros((1, tokens), f32)
    for g in range(groups):
        rows = slice(g * heads_rows, (g + 1) * heads_rows)
        wide = slice(g * cols, (g + 1) * cols)
        s = sc[rows, :].reshape(GROUP, LATENTS, tokens)
        a = jnp.exp(s - jnp.max(s, 1, keepdims=True))
        a = a * (1.0 / jnp.sum(a, 1, keepdims=True))
        low = a.reshape(heads_rows, tokens).astype(bf16)
        error = tn(low, dvd[g]) - feat[:, wide].astype(f32)
        kept = counts * error
        loss[...] += jnp.sum((kept * error).reshape(tokens // 8, 8, cols), 0)
        dp = (2.0 * kept).astype(bf16)
        dacc[g] += nn(low, dp)
        da = nt(dvd[g], dp).reshape(GROUP, LATENTS, tokens)
        z = a * (da - jnp.sum(a * da, 1, keepdims=True))
        second = second + jnp.sum((z * s).reshape(heads_rows, tokens), 0, keepdims=True)
        zs[rows, :] = z.reshape(heads_rows, tokens).astype(bf16)
    zs[total_rows:, :] = tail_rows(nf, i, second, xn, depth)
    acc[...] += nn(zs[...], xn[...])

    @pl.when(i == pl.num_programs(1) - 1)
    def _():
        gain = jnp.zeros((8, depth), f32)
        for g in range(groups):
            rows = slice(g * heads_rows, (g + 1) * heads_rows)
            wide = slice(g * cols, (g + 1) * cols)
            held = acc[rows, :depth]
            low = held.astype(bf16)
            dx_o[rows, :] = low
            ddq_o[:, wide] = collect(nn(low, wk[:, wide])) * scale
            ddv_o[:, wide] = collect(dacc[g])
            gain = gain + jnp.sum(
                (held * dqw[rows, :].astype(f32)).reshape(heads_rows // 8, 8, depth), 0
            )
        side_o[0, 0:TAIL, :] = tn(acc[:total_rows, depth:].astype(bf16), dqw[...])[:TAIL]
        side_o[0, TAIL : 2 * TAIL, :] = acc[total_rows:, :depth]
        side_o[0, 2 * TAIL :, :] = gain
        loss_o[0] = loss[...]


def tail_rows(nf, i, second, xn, depth):
    tokens = xn.shape[0]
    rstd = nt(jnp.ones((TAIL, EXTRA), bf16), xn[:, depth:])
    row = lax.broadcasted_iota(jnp.int32, (TAIL, tokens), 0)
    frame = lax.broadcasted_iota(jnp.int32, (TAIL, tokens), 1) // PATCH + i * nf
    return jnp.where(row == frame, rstd * second * (1.0 / depth), 0.0).astype(bf16)


def decode_pass(xn_all, ft_all, counts, dq_all, dv_all, wk, scale, videos_dev):
    depth = wk.shape[0]
    tokens_video = xn_all.shape[0] // videos_dev
    cols = GROUP * HEAD_SIZE
    frames_dev = tokens_video // PATCH
    nf = frames_a_block(frames_dev)
    tokens = nf * PATCH
    blocks = frames_dev // nf
    groups = depth // cols
    heads_rows = GROUP * LATENTS
    rows = groups * heads_rows
    one = pl.Buffered(1)
    return pl.pallas_call(
        functools.partial(kernel_decode, nf, scale),
        grid=(videos_dev, blocks),
        in_specs=[
            pl.BlockSpec((tokens, depth + EXTRA), lambda j, i: (j * blocks + i, 0)),
            pl.BlockSpec((tokens, depth), lambda j, i: (j * blocks + i, 0)),
            pl.BlockSpec((tokens, 1), lambda j, i: (j * blocks + i, 0)),
            pl.BlockSpec((LATENTS, depth), lambda j, i: (j, 0), pipeline_mode=one),
            pl.BlockSpec((LATENTS, depth), lambda j, i: (j, 0), pipeline_mode=one),
            whole(wk.shape),
        ],
        out_specs=[
            pl.BlockSpec((LATENTS, depth), lambda j, i: (j, 0), pipeline_mode=one),
            pl.BlockSpec((LATENTS, depth), lambda j, i: (j, 0), pipeline_mode=one),
            pl.BlockSpec((rows, depth), lambda j, i: (j, 0), pipeline_mode=one),
            pl.BlockSpec((1, 2 * TAIL + 8, depth), lambda j, i: (j, 0, 0), pipeline_mode=one),
            pl.BlockSpec((1, 8, cols), lambda j, i: (j, 0, 0), pipeline_mode=one),
        ],
        scratch_shapes=[
            pltpu.VMEM((rows, depth), bf16),
            pltpu.VMEM((groups, heads_rows, cols), bf16),
            pltpu.VMEM((rows, tokens), f32),
            pltpu.VMEM((rows + TAIL, tokens), bf16),
            pltpu.VMEM((rows + TAIL, depth + EXTRA), f32),
            pltpu.VMEM((groups, heads_rows, cols), f32),
            pltpu.VMEM((8, cols), f32),
        ],
        out_shape=(
            jax.ShapeDtypeStruct((videos_dev * LATENTS, depth), f32),
            jax.ShapeDtypeStruct((videos_dev * LATENTS, depth), f32),
            jax.ShapeDtypeStruct((videos_dev * rows, depth), bf16),
            jax.ShapeDtypeStruct((videos_dev, 2 * TAIL + 8, depth), f32),
            jax.ShapeDtypeStruct((videos_dev, 8, cols), f32),
        ),
        compiler_params=pltpu.CompilerParams(vmem_limit_bytes=VMEM_BYTES),
        cost_estimate=pl.CostEstimate(
            flops=6 * rows * tokens_video * depth,
            bytes_accessed=tokens_video * depth * 4,
            transcendentals=rows * tokens_video,
        ),
        name="decode_pass",
    )(xn_all, ft_all, counts, dq_all, dv_all, wk)


def head_column(ld, first):
    lane = lax.broadcasted_iota(jnp.int32, ld.shape, 1)
    return jnp.concatenate(
        [jnp.sum(jnp.where(lane == first + j, ld, 0.0), -1, keepdims=True) for j in range(GROUP)], 0
    )


def kernel_value(chunks, place, do, wv, ld, *rest):
    pxs = rest[:chunks]
    sts = rest[chunks : 2 * chunks]
    ow_o, near_o, away_o, side_o, acc = rest[2 * chunks :]
    k = pl.program_id(0)
    v = pl.program_id(1)
    depth = wv.shape[0]

    @pl.when((k == 0) & (v == 0))
    def _():
        side_o[...] = jnp.zeros_like(side_o)

    diag = spread(do[...])
    ow = nt(diag, wv[...]).astype(bf16)
    ow_o[...] = ow
    norm = 0.0
    lse = head_column(ld[...], (place[0] ^ k) * GROUP)
    for px, st in zip(pxs, sts):
        norm = norm + px[...].astype(f32) * jnp.exp(st[:, 126:127] - lse)
    low = norm.astype(bf16)
    part = tn(diag, low[:, :depth])

    @pl.when(v == 0)
    def _():
        acc[...] = part

    @pl.when(v > 0)
    def _():
        acc[...] += part

    @pl.when(k & 1 == 0)
    def _():
        near_o[0] = acc[...].astype(bf16)

    @pl.when(k & 1 == 1)
    def _():
        away_o[0] = acc[...].astype(bf16)

    side_o[0:TAIL, :] += tn(low[:, depth:], ow)[:TAIL]
    rows = ow.shape[0]
    side_o[TAIL:, :] += jnp.sum((ow.astype(f32) * norm[:, :depth]).reshape(rows // 8, 8, depth), 0)


def value_pass(do_all, wv, px_all, st_all, ld, h, videos_dev):
    depth = wv.shape[0]
    cols = GROUP * HEAD_SIZE
    groups = depth // cols
    rows = GROUP * LATENTS
    chunks = px_all.shape[0] // (videos_dev * groups * rows)

    def spot(c):
        return lambda k, v, p: ((v * chunks + c) * groups + (p[0] ^ k), 0)

    return pl.pallas_call(
        functools.partial(kernel_value, chunks),
        grid_spec=pltpu.PrefetchScalarGridSpec(
            num_scalar_prefetch=1,
            grid=(groups, videos_dev),
            in_specs=[
                pl.BlockSpec((LATENTS, cols), lambda k, v, p: (v, p[0] ^ k)),
                pl.BlockSpec((depth, cols), lambda k, v, p: (0, p[0] ^ k)),
                pl.BlockSpec((LATENTS, 128), lambda k, v, p: (v, 0)),
            ]
            + [pl.BlockSpec((rows, depth + EXTRA), spot(c)) for c in range(chunks)]
            + [pl.BlockSpec((rows, 128), spot(c)) for c in range(chunks)],
            out_specs=[
                pl.BlockSpec((rows, depth), lambda k, v, p: (v * groups + (p[0] ^ k), 0)),
                pl.BlockSpec((1, cols, depth), lambda k, v, p: (k >> 1, 0, 0)),
                pl.BlockSpec((1, cols, depth), lambda k, v, p: (k >> 1, 0, 0)),
                pl.BlockSpec((TAIL + 8, depth), lambda k, v, p: (0, 0)),
            ],
            scratch_shapes=[pltpu.VMEM((cols, depth), f32)],
        ),
        out_shape=(
            jax.ShapeDtypeStruct((videos_dev * groups * rows, depth), bf16),
            jax.ShapeDtypeStruct((groups // 2, cols, depth), bf16),
            jax.ShapeDtypeStruct((groups // 2, cols, depth), bf16),
            jax.ShapeDtypeStruct((TAIL + 8, depth), f32),
        ),
        compiler_params=pltpu.CompilerParams(vmem_limit_bytes=VMEM_BYTES),
        cost_estimate=BRIEF,
        name="value_pass",
    )(jnp.full((1,), h, jnp.int32), do_all, wv, ld, *[px_all] * chunks, *[st_all] * chunks)


def kernel_back(
    nf, per_read, scale, videos_dev, final, place, xn, e, st, ld, ow, qw, q, wk, *rest
):
    dqs = rest[:videos_dev]
    dxs = rest[videos_dev : 2 * videos_dev]
    rest = rest[2 * videos_dev :]
    if final:
        g0, side_a, side_b, dq_o, near_o, away_o, pack_o, zs, acc, pack = rest
    else:
        dq_o, near_o, away_o, side_o, zs, acc = rest
    v = pl.program_id(0)
    i = pl.program_id(1)
    tokens = xn.shape[0]
    depth = wk.shape[0]
    heads_rows = GROUP * LATENTS
    total_rows = qw.shape[0]
    groups = total_rows // heads_rows
    cols = GROUP * HEAD_SIZE

    @pl.when((v == 0) & (i == 0))
    def _():
        acc[...] = jnp.zeros_like(acc)

    second = jnp.zeros((1, tokens), f32)
    block = lax.broadcasted_iota(jnp.int32, (heads_rows, 128), 1)
    heads_total = depth // HEAD_SIZE
    base = (place[0] >> 1 if final else (place[0] >> 1) ^ 1) * groups
    for g in range(groups):
        rows = slice(g * heads_rows, (g + 1) * heads_rows)
        spot = i // per_read
        peak = jnp.sum(jnp.where(block == spot, st[rows, :], 0.0), -1, keepdims=True)
        lse = head_column(ld[...], (base + g) * GROUP)
        delta = head_column(ld[...], (heads_total // GROUP + base + g) * GROUP)
        dp = nt(ow[rows, :], xn[:, :depth])
        expo = e[rows, :].astype(f32)
        prob = expo * jnp.exp(peak - lse)
        z = prob * (dp - delta)
        score = jnp.log(jnp.maximum(expo, 1e-37)) + peak
        second = second + jnp.sum(z * score + prob * dp, 0, keepdims=True)
        zs[rows, :] = z.astype(bf16)
    zs[total_rows:, :] = tail_rows(nf, i, second, xn, depth)
    acc[...] += nn(zs[...], xn[...])

    @pl.when((v == videos_dev - 1) & (i == pl.num_programs(1) - 1))
    def _():
        gain = jnp.zeros((8, depth), f32)
        for k in range(groups):
            g = (place[0] & 1) ^ k
            rows = pl.ds(pl.multiple_of(g * heads_rows, heads_rows), heads_rows)
            wide = pl.ds(pl.multiple_of(g * cols, 128), cols)
            low = acc[rows, :depth].astype(bf16)
            dq_o[k] = collect(nn(low, wk[:, wide])) * scale
            grad = tn(spread(q[:, wide]), low)
            for one, dx in zip(dqs, dxs):
                grad = grad + tn(spread(one[:, wide]), dx[rows, :])
            target = away_o if k & 1 else near_o
            target[...] = (grad * scale).astype(bf16)
        for g in range(groups):
            rows = slice(g * heads_rows, (g + 1) * heads_rows)
            gain = gain + jnp.sum(
                (acc[rows, :depth] * qw[rows, :].astype(f32)).reshape(heads_rows // 8, 8, depth), 0
            )
        pulled = tn(acc[:total_rows, depth:].astype(bf16), qw[...])[:TAIL]
        moved = acc[total_rows:, :depth]
        if final:
            pulled = (pulled + side_a[0:TAIL, :] + side_b[0:TAIL, :]) * g0[...]
            moved = moved + side_a[TAIL : 2 * TAIL, :] + side_b[TAIL : 2 * TAIL, :]
            moved = moved * (1.0 / g0[...])
            gain = gain + side_a[2 * TAIL :, :] + side_b[2 * TAIL :, :]
            mean = jnp.sum(pulled, -1, keepdims=True) * (1.0 / depth)
            pack[0:TAIL, :] = pulled - mean - moved
            pack[TAIL:, :] = gain * (1.0 / g0[...])
            for k in range(pack_o.shape[0]):
                wide = pl.ds(pl.multiple_of((place[0] ^ k) * cols, 128), cols)
                pack_o[(k & 1) * 2 + (k >> 1)] = pack[:, wide]
        else:
            side_o[0:TAIL, :] = pulled
            side_o[TAIL : 2 * TAIL, :] = moved
            side_o[2 * TAIL :, :] = gain


def back_pass(
    far, xn_all, e_all, st_all, ld, ow, qw, q_all, wk, dq_all, dx_all, sides, gain, scale, h, videos_dev
):
    depth = wk.shape[0]
    tokens_video = e_all.shape[1]
    frames_dev = tokens_video // PATCH
    _, read_nf = chunks_of(frames_dev)
    nf = frames_a_block(read_nf)
    tokens = nf * PATCH
    blocks = frames_dev // nf
    rows = qw.shape[0] // 2
    cols = GROUP * HEAD_SIZE
    groups = depth // cols
    packed = TAIL + 8
    final = not far
    one = pl.Buffered(1)

    def y(p):
        return (p[0] >> 1) ^ 1 if far else p[0] >> 1

    outs = [
        jax.ShapeDtypeStruct((2, LATENTS, cols), f32),
        jax.ShapeDtypeStruct((cols, depth), bf16),
        jax.ShapeDtypeStruct((cols, depth), bf16),
    ]
    scratch = [
        pltpu.VMEM((rows + TAIL, tokens), bf16),
        pltpu.VMEM((rows + TAIL, depth + EXTRA), f32),
    ]
    extra = []
    if final:
        extra = [gain, *sides]
        outs.append(jax.ShapeDtypeStruct((groups, packed, cols), f32))
        scratch.append(pltpu.VMEM((packed, depth), f32))
    else:
        outs.append(jax.ShapeDtypeStruct((2 * TAIL + 8, depth), f32))
    return pl.pallas_call(
        functools.partial(
            kernel_back, nf, read_nf // nf, scale, videos_dev, final
        ),
        grid_spec=pltpu.PrefetchScalarGridSpec(
            num_scalar_prefetch=1,
            grid=(videos_dev, blocks),
            in_specs=[
                pl.BlockSpec((tokens, depth + EXTRA), lambda v, i, p: (v * blocks + i, 0)),
                pl.BlockSpec((rows, tokens), lambda v, i, p: (v * 2 + y(p), i)),
                pl.BlockSpec((rows, 128), lambda v, i, p: (v * 2 + y(p), 0)),
                pl.BlockSpec((LATENTS, 128), lambda v, i, p: (v, 0)),
                pl.BlockSpec((rows, depth), lambda v, i, p: (v * 2 + y(p), 0)),
                pl.BlockSpec((rows, depth), lambda v, i, p: (y(p), 0), pipeline_mode=one),
                pl.BlockSpec((LATENTS, 2 * cols), lambda v, i, p: (0, y(p)), pipeline_mode=one),
                pl.BlockSpec((depth, 2 * cols), lambda v, i, p: (0, y(p)), pipeline_mode=one),
            ]
            + [
                pl.BlockSpec((LATENTS, 2 * cols), lambda v, i, p, n=n: (n, y(p)), pipeline_mode=one)
                for n in range(videos_dev)
            ]
            + [
                pl.BlockSpec((rows, depth), lambda v, i, p, n=n: (n * 2 + y(p), 0), pipeline_mode=one)
                for n in range(videos_dev)
            ]
            + [whole(a.shape) for a in extra],
            out_specs=[whole(a.shape) for a in outs],
            scratch_shapes=scratch,
        ),
        out_shape=outs,
        compiler_params=pltpu.CompilerParams(vmem_limit_bytes=VMEM_BYTES),
        cost_estimate=pl.CostEstimate(
            flops=4 * videos_dev * rows * tokens_video * depth,
            bytes_accessed=videos_dev * tokens_video * depth * 4,
            transcendentals=videos_dev * rows * tokens_video,
        ),
        name="back_far" if far else "back_near",
    )(
        jnp.full((1,), h, jnp.int32), xn_all, e_all, st_all, ld, ow, qw, q_all, wk,
        *[dq_all] * videos_dev, *[dx_all] * videos_dev, *extra,
    )


def halves(x):
    high = x.astype(bf16)
    return high, (x - high.astype(f32)).astype(bf16)


def precise(a, b, dims):
    dims = ((dims[0], dims[1]), ((), ()))
    ah, al = halves(a)
    bh, bl = halves(b)
    out = lax.dot_general(ah, bh, dims, preferred_element_type=f32)
    out = out + lax.dot_general(ah, bl, dims, preferred_element_type=f32)
    return out + lax.dot_general(al, bh, dims, preferred_element_type=f32)


def turn_body(g, left, right, out, total):
    @pl.when(pl.program_id(0) == 0)
    def _():
        total[...] = jnp.zeros_like(total)

    rows, cols = g.shape
    square = g * g
    part = square[:, :128]
    for c in range(1, cols // 128):
        part = part + square[:, c * 128 : (c + 1) * 128]
    total[...] += jnp.sum(part.reshape(rows // 8, 8, 128), 0)
    turned = precise(left[0], g, ((0,), (0,)))
    for c in range(cols // 128):
        wide = slice(c * 128, (c + 1) * 128)
        out[:, wide] = precise(turned[:, wide], right[0, c], ((1,), (0,)))


def kernel_turn(grad, left, right, out, total):
    turn_body(grad[...].astype(f32), left, right, out, total)


def kernel_turn_product(a, b, left, right, out, total):
    frames, _, rows, own = a.shape
    turn_body(tn(a[...].reshape(frames * rows, own), b[...]), left, right, out, total)


def kernel_turn_sum(a, b, c, d, left, right, out, total):
    frames, _, rows, own = a.shape
    grad = tn(a[...].reshape(frames * rows, own), b[...]) + tn(c[...], d[...])
    turn_body(grad, left, right, out, total)


def turn(slab, slot, operands, rows, cols, left, right):
    step = 3 * 128
    if len(operands) == 1:
        body = kernel_turn
        specs = [pl.BlockSpec((rows, step), lambda i: (0, i))]
        arrays = operands
    else:
        a, which, b, first = operands[:4]
        body = kernel_turn_product
        specs = [
            pl.BlockSpec((a.shape[0], 1) + a.shape[2:], lambda i: (0, which, 0, 0)),
            pl.BlockSpec((b.shape[0], step), lambda i: (0, first // step + i)),
        ]
        arrays = [a, b]
        if len(operands) > 4:
            body = kernel_turn_sum
            c, d = operands[4:]
            specs += [
                pl.BlockSpec(c.shape, lambda i: (0, 0)),
                pl.BlockSpec((d.shape[0], step), lambda i: (0, i)),
            ]
            arrays += [c, d]
    return pl.pallas_call(
        body,
        grid=(cols // step,),
        in_specs=specs
        + [
            pl.BlockSpec((1, rows, rows), lambda i: (slab, 0, 0)),
            pl.BlockSpec((1, 3, 128, 128), lambda i: (slot, i, 0, 0)),
        ],
        out_specs=[
            pl.BlockSpec((rows, step), lambda i: (0, i)),
            pl.BlockSpec((8, 128), lambda i: (0, 0)),
        ],
        out_shape=(
            jax.ShapeDtypeStruct((rows, cols), f32),
            jax.ShapeDtypeStruct((8, 128), f32),
        ),
        compiler_params=pltpu.CompilerParams(vmem_limit_bytes=VMEM_BYTES),
        cost_estimate=BRIEF,
        name="turn",
    )(*arrays, left, right)


def kernel_update(rates, factor, weight, one, two, left, right, *rest):
    turned = rest[: len(rates)]
    new_o, one_o, two_o, low_o = rest[len(rates) :]
    slab = pl.program_id(0)
    g = turned[0][...]
    rate = jnp.float32(rates[0])
    for n in range(1, len(rates)):
        g = jnp.where(slab == n, turned[n][...], g)
        rate = jnp.where(slab == n, jnp.float32(rates[n]), rate)
    first, second, step = adam_moments(g * factor[0], one[0], two[0])
    one_o[0] = first
    two_o[0] = second
    cols = step.shape[1]
    back = jnp.concatenate(
        [
            precise(step[:, c * 128 : (c + 1) * 128], right[0, c], ((1,), (1,)))
            for c in range(cols // 128)
        ],
        1,
    )
    back = precise(left[0], back, ((1,), (0,)))
    held = weight[0]
    new = held - rate * (back + 0.01 * held)
    new_o[0] = new
    low_o[0] = new.astype(bf16)


def update(factor, weight, one, two, first_slab, left, right, turned, rates):
    slabs, rows, cols = weight.shape
    step = 6 * 128 if cols % (6 * 128) == 0 else 3 * 128
    tile = pl.BlockSpec((1, rows, step), lambda s, i: (s, 0, i))
    own = [
        pl.BlockSpec((rows, step), lambda s, i, n=n: (0, jnp.where(s == n, i, 0)))
        for n in range(slabs)
    ]
    return pl.pallas_call(
        functools.partial(kernel_update, rates),
        grid=(slabs, cols // step),
        in_specs=[
            pl.BlockSpec(memory_space=pltpu.SMEM),
            tile,
            tile,
            tile,
            pl.BlockSpec((1, rows, rows), lambda s, i: (first_slab + s, 0, 0)),
            pl.BlockSpec((1, step // 128, 128, 128), lambda s, i: (s, i, 0, 0)),
        ]
        + own,
        out_specs=[tile] * 4,
        out_shape=[jax.ShapeDtypeStruct(weight.shape, f32)] * 3
        + [jax.ShapeDtypeStruct(weight.shape, bf16)],
        compiler_params=pltpu.CompilerParams(vmem_limit_bytes=VMEM_BYTES),
        cost_estimate=BRIEF,
        name="update",
    )(factor, weight, one, two, left, right, *turned)


def sum_near(near, away):
    near = near.astype(f32) + swap(away, "head", 1).astype(f32)
    return near[0] + swap(near[1].astype(bf16), "head", 2).astype(f32)


def to_frames(x):
    f = lax.axis_index("frame")
    out = []
    for d in range(x.shape[0]):
        piece = lax.dynamic_index_in_dim(x, f ^ d, 0, False)
        out.append(swap(piece, "frame", d) if d else piece)
    return jnp.stack(out)


def scatter_deep(x):
    mine = lax.axis_index("frame") >> 1
    total = lax.dynamic_index_in_dim(x, mine, 0, False)
    low = x.astype(bf16)
    for d in range(1, x.shape[0]):
        send = lax.dynamic_index_in_dim(low, mine ^ d, 0, False)
        total = total + swap(send, "frame", 2 * d).astype(f32)
    return total


def per_device(
    features, lengths, loss_mask, sq_weight, sq_first, sq_second, ffn_weight, ffn_first,
    ffn_second, left_bases, right_sq, right_ffn, latents, lat_first, lat_second, time_embed,
    time_first, time_second, gains, gain_first, gain_second,
):
    videos, frames_dev, patches, cols = features.shape
    lat_count, depth = latents.shape
    heads_dev = cols // HEAD_SIZE
    head_size = lax.axis_size("head")
    frame_size = lax.axis_size("frame")
    videos_dev = videos // head_size
    rows_dev = sq_weight.shape[1]
    scale = HEAD_SIZE ** (-0.5)
    f = lax.axis_index("frame")
    h = lax.axis_index("head")
    first_frame = (f == 0).astype(f32)
    first_head = (h == 0).astype(f32)
    share = videos_dev * lat_count // frame_size
    tokens_video = frames_dev * patches

    chunks = len(chunks_of(frames_dev)[0])
    feat = features.reshape(videos, tokens_video, cols)

    with jax.named_scope("weights"):
        sq_low = sq_weight.astype(bf16)
        ffn_low = ffn_weight.astype(bf16)
        zhat_zero, zrstd_zero = normalize_rows(latents)
        normed_lat = (zhat_zero * gains[1]).astype(bf16)
        normed_own = lax.dynamic_slice_in_dim(normed_lat, f * rows_dev, rows_dev, 1)
        kv_own = jnp.concatenate([sq_low[1], sq_low[2]], 1)
        kv_far = swap(kv_own, "head", 2)
        low_side = (h & 2) == 0
        kv_rows = jnp.concatenate(
            [jnp.where(low_side, kv_own, kv_far), jnp.where(low_side, kv_far, kv_own)], 1
        )
        away, near = zip(
            *[pick(feat, h, j, c, videos_dev) for j in range(videos_dev) for c in range(chunks)]
        )
        slabs, blocks_dev, bl, _ = left_bases.shape
        left = (
            left_bases[:, :, :, None, :] * jnp.eye(blocks_dev, dtype=f32)[None, :, None, :, None]
        ).reshape(slabs, rows_dev, rows_dev)
        opening = gate(away[0], kv_far)
        query = nn(normed_own, sq_low[0])
        bit = 1
        while bit < frame_size:
            query = query + swap(query, "frame", bit)
            if bit == 1:
                held = sum((zero_of(n) for n in near[1:]), zero_of(opening))
                query = query + held.astype(f32)
            bit *= 2
        query = query.astype(bf16)
        even_core = (h & 1) == 0
        q_all = gather_head(query, 1)
        time_full = gather_head(time_embed, 1)

    with jax.named_scope("exchange"):
        crossed = [swap(opening, "head", 2)]
        waiting = [opening] + [gate(n, crossed[0], q_all, time_full) for n in away[1:2]]

    with jax.named_scope("weights"):
        kv_half = lax.all_gather(kv_rows, "frame", axis=0, tiled=True)
        kv_half = kv_half + (zero_of(waiting[-1]) + zero_of(left)).astype(bf16)
        kv_away = swap(kv_half, "head", 1)
        even = jnp.where(even_core, kv_half, kv_away)
        odd = jnp.where(even_core, kv_away, kv_half)
        w_key, w_value = (
            jnp.concatenate(
                [
                    side[:, at : at + cols]
                    for at in (n * cols, (n + 2) * cols)
                    for side in (even, odd)
                ],
                1,
            )
            for n in (0, 1)
        )
        rest = lax.all_gather(
            after(
                jnp.concatenate([sq_low[0], sq_low[3], sq_low[4], ffn_low[0], ffn_low[1]], 1), kv_half
            ),
            "frame",
            axis=0,
            tiled=True,
        )
        w_query, w_outt, w_dec = (rest[:, n * cols : (n + 1) * cols] for n in range(3))
        hid = ffn_low.shape[2]
        w_up = rest[:, 3 * cols : 3 * cols + hid]
        w_downt = rest[:, 3 * cols + hid :]
        w_key_own = jnp.where(low_side, kv_half[:, :cols], kv_half[:, 2 * cols : 3 * cols])
        w_value_own = jnp.where(low_side, kv_half[:, cols : 2 * cols], kv_half[:, 3 * cols :])

    with jax.named_scope("latent_keys"):
        lat_key = nn(normed_lat, w_key_own).astype(bf16).reshape(lat_count, heads_dev, HEAD_SIZE)
        lat_value = nn(normed_lat, w_value_own).astype(bf16).reshape(lat_count, heads_dev, HEAD_SIZE)
        qw = absorb(q_all, w_key, scale)

    with jax.named_scope("read"):
        own_lens = lax.dynamic_slice_in_dim(lengths, h * videos_dev, videos_dev, 0)
        state = None
        parts = videos_dev * chunks
        token = qw
        for n in range(parts):
            j, c = divmod(n, chunks)
            passed = crossed[n][1] if n < 2 else gate(crossed[n][1], token)
            got = [swap(near[n], "head", 1), crossed[n].reshape(-1, cols), swap(passed, "head", 1)]
            if n + 1 < parts:
                crossed.append(swap(waiting[n + 1], "head", 2))
            if n + 2 < parts and n % 2 == 0:
                waiting.append(gate(away[n + 2], crossed[n + 1], token))
            *state, token = read_pass(
                j, c, state, feat, got, time_full, gains[0:1], own_lens[j], qw, w_value,
                waiting[-1], h, videos_dev,
            )
            if n + 2 < parts and n % 2 == 1:
                waiting.append(gate(away[n + 2], crossed[n + 1], token))
        xn_all, ft_all, e_all, px_all, st_all, o_all = state

    with jax.named_scope("combine"):
        heads = depth // HEAD_SIZE
        lse_local = (
            (st_all[:, 126] + jnp.log(st_all[:, 127]))
            .reshape(videos_dev, heads, lat_count)
            .transpose(0, 2, 1)
            .reshape(videos_dev * lat_count, heads)
        )
        pay = jnp.concatenate(
            [o_all.astype(bf16), split_three(lse_local)], 1
        ).reshape(frame_size, share, depth + 3 * heads)
        pay = to_frames(pay)
        lse_each = join_three(pay[..., depth:])
        o_each = pay[..., :depth].astype(f32).reshape(frame_size, share, heads, HEAD_SIZE)
        top = jnp.max(lse_each, 0)
        weight = jnp.exp(lse_each - top)
        total = jnp.sum(weight, 0)
        o_tok = jnp.sum(o_each * weight[..., None], 0) / total[..., None]
        lse_tok = top + jnp.log(total)
        o_heads = o_tok.reshape(share, head_size, cols).transpose(1, 0, 2).astype(bf16)
        l_heads = split_three(lse_tok.reshape(share, head_size, heads_dev).transpose(1, 0, 2))
        pay = lax.all_to_all(jnp.concatenate([o_heads, l_heads], 2), "head", 0, 0, tiled=True)
        lse_tok = join_three(pay[..., cols:])
        o_tok = pay[..., :cols].astype(f32).reshape(head_size, share, heads_dev, HEAD_SIZE)
        first_row = lax.rem(f * share, lat_count)
        q_rows = lax.dynamic_slice_in_dim(query, first_row, share, 0).reshape(
            share, heads_dev, HEAD_SIZE
        )
        lat_scores = (
            jnp.einsum("rnd,jnd->rnj", q_rows, lat_key, preferred_element_type=f32) * scale
        )
        lse = jnp.logaddexp(lse_tok, jax.nn.logsumexp(lat_scores, -1)[None])
        lat_prob = jnp.exp(lat_scores[None] - lse[..., None])
        attn = o_tok * jnp.exp(lse_tok - lse)[..., None] + jnp.einsum(
            "srnj,jnd->srnd", lat_prob, lat_value.astype(f32), precision=HIGH_ACCURACY
        )
        rows = head_size * share
        attn_low = attn.reshape(rows, cols).astype(bf16)

    with jax.named_scope("latent_forward"):
        lat_rows = jnp.tile(lax.dynamic_slice_in_dim(latents, first_row, share, 0), (head_size, 1))
        z_one = lat_rows + sum_head(nt(attn_low, w_outt))
        z1hat, z1rstd = normalize_rows(z_one)
        ffn_in = (z1hat * gains[2]).astype(bf16)
        pre = nn(ffn_in, w_up)
        hidden = jax.nn.gelu(pre).astype(bf16)
        z_two = z_one + sum_head(nt(hidden, w_downt))
        z2hat, z2rstd = normalize_rows(z_two)
        final = (z2hat * gains[3]).astype(bf16)
        dec = jnp.concatenate([nn(final, w_query), nn(final, w_dec)], 1).astype(bf16)

    def to_tokens(x):
        x = lax.all_to_all(x.reshape(head_size, share, -1), "head", 0, 0, tiled=True)
        x = x.transpose(1, 0, 2)
        x = jnp.broadcast_to(x[None], (frame_size,) + x.shape)
        x = lax.all_to_all(x, "frame", 0, 0, tiled=True)
        return x.reshape(videos_dev * lat_count, head_size, -1)

    with jax.named_scope("decode"):
        dec_all = to_tokens(dec)
        dq_all = dec_all[..., :cols].reshape(videos_dev * lat_count, depth)
        dv_all = dec_all[..., cols:].reshape(videos_dev * lat_count, depth)
        own_mask = lax.dynamic_slice_in_dim(loss_mask, h * videos_dev, videos_dev, 0).astype(f32)
        counts = own_mask.reshape(videos_dev * tokens_video, 1)
        decoded = decode_pass(xn_all, ft_all, counts, dq_all, dv_all, w_key, scale, videos_dev)
        loss_part = jnp.sum(decoded[4])
        count_part = jnp.sum(own_mask)
        dec_side = jnp.sum(decoded[3], 0)

    with jax.named_scope("latent_backward"):
        ddec = jnp.concatenate(
            [
                decoded[n].reshape(frame_size, share, head_size, cols)
                for n in (0, 1)
            ],
            3,
        ).astype(bf16)
        ddec = to_frames(ddec.reshape(frame_size, share, -1)).astype(f32)
        ddec = jnp.sum(ddec, 0).astype(bf16).reshape(share, head_size, 2 * cols).transpose(1, 0, 2)
        ddec = lax.all_to_all(ddec, "head", 0, 0, tiled=True).reshape(rows, 2 * cols)
        ddq_low, ddv_low = (ddec[:, :cols], ddec[:, cols:])
        dfinal = sum_head(nt(ddq_low, w_query) + nt(ddv_low, w_dec))
        dz_two = norm_reverse(dfinal, z2hat, z2rstd, gains[3])
        dz2_low = dz_two.astype(bf16)
        _, gelu_back = jax.vjp(jax.nn.gelu, pre)
        dpre = gelu_back(nn(dz2_low, w_downt))[0].astype(bf16)
        dffn_in = sum_head(nt(dpre, w_up))
        dz_one = dz_two + norm_reverse(dffn_in, z1hat, z1rstd, gains[2])
        dz1_low = dz_one.astype(bf16)
        dattn = nn(dz1_low, w_outt).astype(bf16)
        dattn_heads = dattn.astype(f32).reshape(head_size, share, heads_dev, HEAD_SIZE)
        delta = jnp.sum(dattn_heads * attn, -1)
        pay = jnp.concatenate(
            [
                dattn,
                split_three(lse.reshape(rows, heads_dev)),
                split_three(delta.reshape(rows, heads_dev)),
            ],
            1,
        )
        pay = to_tokens(pay)
        do_all = pay[..., :cols].reshape(videos_dev * lat_count, depth)

        both = join_three(pay[..., cols:].reshape(-1, head_size, 2, 3 * heads_dev))
        both = both.transpose(0, 2, 1, 3).reshape(videos_dev * lat_count, 2 * heads)
        ld = jnp.pad(both, ((0, 0), (0, 128 - 2 * heads)))

    with jax.named_scope("latent_pairs"):
        lat_value_f = lat_value.astype(f32)
        lat_dprob = jnp.einsum("srnd,jnd->srnj", dattn_heads, lat_value_f, precision=HIGH_ACCURACY)
        lat_dscore = lat_prob * (lat_dprob - delta[..., None]) * scale
        dq_lat = jnp.einsum(
            "srnj,jnd->rnd", lat_dscore, lat_key.astype(f32), precision=HIGH_ACCURACY
        ).reshape(share, cols)
        dk_lat = jnp.einsum(
            "srnj,rnd->jnd", lat_dscore, q_rows.astype(f32), precision=HIGH_ACCURACY
        ).reshape(lat_count, cols)
        dv_lat = jnp.einsum(
            "srnj,srnd->jnd", lat_prob, dattn_heads, precision=HIGH_ACCURACY
        ).reshape(lat_count, cols)
        dk_lat_low = dk_lat.astype(bf16)
        dv_lat_low = dv_lat.astype(bf16)
        pairs = jnp.concatenate([dk_lat, dv_lat], 0)
        lat_part = jnp.concatenate(
            [
                jnp.sum(dz_one.reshape(head_size, share, depth), 0),
                jnp.sum(dffn_in * z1hat, 0)[None],
                jnp.sum(dfinal * z2hat, 0)[None],
                jnp.zeros((6, depth), f32),
            ],
            0,
        )
        lat_parts = lax.all_gather(lat_part, "frame")
        lat_direct = jnp.sum(
            lat_parts[:, :share].reshape(videos_dev, lat_count, depth), 0
        )
        gain_rows = jnp.sum(lat_parts[:, share : share + 2], 0)

    with jax.named_scope("row_gradients"):
        wide_a = lax.all_gather(
            jnp.concatenate([hidden, attn_low], 1), "frame", axis=0, tiled=True
        )
        wide_b = lax.all_gather(
            jnp.concatenate([dpre, ddq_low, ddv_low], 1), "frame", axis=0, tiled=True
        )

        own_cols = jnp.stack(
            [a.reshape(rows, frame_size, rows_dev) for a in (ffn_in, final, dz2_low, dz1_low)]
        ).transpose(2, 0, 1, 3)
        own_cols = lax.all_to_all(own_cols, "frame", 0, 0, tiled=True)

    with jax.named_scope("value"):
        ow, dwv_own, dwv_other, value_side = value_pass(do_all, w_value, px_all, st_all, ld, h, videos_dev)
        side = dec_side + jnp.concatenate(
            [value_side[:TAIL], jnp.zeros((TAIL, depth), f32), value_side[TAIL:]], 0
        )

    half = head_size // 2
    back = functools.partial(
        back_pass, e_all=e_all, ld=ld, ow=ow, qw=qw, q_all=q_all, wk=w_key, dq_all=dq_all,
        dx_all=decoded[2], scale=scale, h=h, videos_dev=videos_dev,
    )

    with jax.named_scope("value_gradient"):
        dwv = dwv_own.astype(f32) + swap(dwv_other, "head", 1).astype(f32)
        dwv_pay = dwv[1].astype(bf16)
        dwv_far = swap(dwv_pay, "head", 2)

    with jax.named_scope("back"):
        xn_all = gate(xn_all, dwv_pay)
        far_dq, far_near, far_away, far_side = back(
            True, xn_all, st_all=st_all, sides=None, gain=None
        )

    with jax.named_scope("value_gradient"):
        dwv = dwv[0] + dwv_far.astype(f32) + tn(dv_lat_low, normed_lat)
        dwv = dwv.T.reshape(frame_size // 2, 2, rows_dev, cols)
        dwv_away = lax.dynamic_index_in_dim(dwv, 1 - (f & 1), 1, False).astype(bf16)
        dwv_near = lax.dynamic_index_in_dim(dwv, f & 1, 1, False)
        dwv_x = swap(dwv_away, "frame", 1)

    with jax.named_scope("key_gradient"):
        far_sum = far_near.astype(f32) + swap(far_away, "head", 1).astype(f32)
        dq_sum = far_dq[0] + swap(far_dq[1], "head", 1)
        dwk_pay = far_sum.astype(bf16)
        dwk_far = swap(dwk_pay, "head", 2)
        dq_far = swap(dq_sum, "head", 2)

    with jax.named_scope("back"):
        xn_all = gate(xn_all, dwk_pay, dq_sum, dwv_away)
        own_dq, own_near, own_away, pack = back(
            False, xn_all, st_all=st_all, sides=[side, far_side],
            gain=gains[0:1],
        )

    with jax.named_scope("value_gradient"):
        grad_value = scatter_deep(dwv_near + dwv_x.astype(f32))

    with jax.named_scope("key_gradient"):
        key_sum = own_near.astype(f32) + swap(own_away, "head", 1).astype(f32)
        key_sum = key_sum + dwk_far.astype(f32) + tn(dk_lat_low, normed_lat)
        key_sum = key_sum.T.reshape(frame_size // 2, 2, rows_dev, cols)
        key_away = lax.dynamic_index_in_dim(key_sum, 1 - (f & 1), 1, False).astype(bf16)
        key_near = lax.dynamic_index_in_dim(key_sum, f & 1, 1, False)
        key_away = gate(key_away, grad_value)
        own_cols = gate(own_cols, key_away)
        sq = functools.partial(turn, rows=rows_dev, cols=cols, left=left, right=right_sq)
        ffn = functools.partial(turn, rows=rows_dev, cols=hid, left=left, right=right_ffn)
        turned_up = ffn(5, 0, (own_cols, 0, wide_b, 0))
        turned_down = ffn(6, 1, (own_cols, 2, wide_a, 0))
        key_half = key_near + swap(key_away, "frame", 1).astype(f32)
        key_half = gate(key_half, turned_up[1], turned_down[1])

    with jax.named_scope("patch_gradients"):
        dq_pad = lax.dynamic_update_slice_in_dim(
            jnp.zeros((lat_count, cols), f32), dq_lat, first_row, 0
        )
        dquery = own_dq[0] + swap(own_dq[1], "head", 1) + dq_far + dq_pad
        dquery = jnp.concatenate([dquery + zero_of(key_away).astype(f32), pairs], 0)
        dquery = gate(sum_rounded(dquery, "frame").astype(bf16), key_half)
        dquery, dk_sum, dv_sum = (
            dquery[n * lat_count : (n + 1) * lat_count] for n in range(3)
        )

    with jax.named_scope("key_gradient"):
        grad_key = scatter_deep(key_half)

    with jax.named_scope("patch_gradients"):
        pack = sum_near(pack[:half], pack[half:])
        time_own = pack[:frames_dev]
        gain0_own = sum_over(jnp.sum(pack[TAIL:], 0)[None], "frame")[0]
        dzn = sum_head(nt(dquery, w_query) + nt(dk_sum, w_key_own) + nt(dv_sum, w_value_own))
        grad_gain1 = jnp.sum(dzn * zhat_zero, 0)
        lat_grad = lat_direct + norm_reverse(dzn, zhat_zero, zrstd_zero, gains[1])
        gain_rest = jnp.concatenate([grad_gain1[None], gain_rows], 0)
        gain_grad = jnp.concatenate(
            [gain0_own[None], lax.dynamic_slice_in_dim(gain_rest, h * cols, cols, 1)], 0
        )

    with jax.named_scope("update"):
        turned, totals = zip(
            sq(0, 0, (own_cols, 1, wide_b, hid, normed_own, dquery)),
            sq(1, 1, (grad_key,)),
            sq(2, 2, (grad_value,)),
            sq(3, 3, (own_cols, 3, wide_a, hid)),
            sq(4, 4, (own_cols, 1, wide_b, hid + cols)),
            turned_up,
            turned_down,
        )
        squares = (
            jnp.sum(sum(totals))
            + jnp.sum(time_own * time_own)
            + first_frame * first_head * jnp.sum(lat_grad * lat_grad)
            + first_frame * jnp.sum(gain_grad * gain_grad)
        )
        sums = jnp.pad(jnp.stack([loss_part, count_part, squares])[None], ((0, 7), (0, 125)))
        sums = sum_over(sum_over(sums, "head"), "frame")
        loss_sum, masked_count, squares = (sums[0, 0], sums[0, 1], sums[0, 2])
        grad_norm = jnp.sqrt(squares) / masked_count
        factor = jnp.minimum(1.0, clip_max / grad_norm) / masked_count
        out_rate = ((FRAMES * PATCH + LATENTS) / 64.0) ** 0.5
        ffn_out = update(
            factor[None], ffn_weight, ffn_first, ffn_second, 5, left, right_ffn, turned[5:],
            (0.02, 0.02),
        )
        sq_out = update(
            factor[None], sq_weight, sq_first, sq_second, 0, left, right_sq, turned[:5],
            (0.02, 0.02, 0.02, 0.02 * out_rate, 0.02),
        )
        lat_out = adamw_update(latents, lat_grad * factor, lat_first, lat_second, 0.01)
        time_out = adamw_update(time_embed, time_own * factor, time_first, time_second, 0.01)
        gain_own = lax.dynamic_slice_in_dim(gains, h * cols, cols, 1)
        gain_out = adamw_update(gain_own, gain_grad * factor, gain_first, gain_second, 0.0)
    return (loss_sum, masked_count, grad_norm, *sq_out, *ffn_out, *lat_out, *time_out, *gain_out)


def solution(mesh):
    matrix = P(None, "frame", "head")
    frame_rows = P("frame", "head")
    by_head = P(None, "head")
    placed = (
        P(None, "frame", None, "head"),
        P(None, "frame"),
        P(None, "frame", None),
        matrix, matrix, matrix, matrix, matrix, matrix,
        P(None, "frame", None, None),
        P(None, "head", None, None),
        P(None, "head", None, None),
        P(), P(), P(),
        frame_rows, frame_rows, frame_rows,
        P(), by_head, by_head,
    )
    outs = (
        P(), P(), P(),
        matrix, matrix, matrix, matrix, matrix, matrix, matrix, matrix,
        P(), P(), P(),
        frame_rows, frame_rows, frame_rows,
        by_head, by_head, by_head,
    )
    return jax.shard_map(per_device, mesh=mesh, in_specs=placed, out_specs=outs, check_vma=False)
```

```python
import functools

import jax
import jax.numpy as jnp
from jax import lax
from jax.experimental import pallas as pl
from jax.experimental.pallas import tpu as pltpu
from jax.sharding import PartitionSpec as P

HEAD_SIZE = 96
LATENTS = 64
PATCH = 256
FRAMES = 96
STEP = 5
GROUP = 4
EXTRA = 128
TAIL = 16
VMEM_BYTES = 62 * 1024 * 1024

HIGH_ACCURACY = lax.Precision.HIGHEST
clip_max = 0.05
beta_one = 0.5
beta_two = 0.6
adam_eps = 1e-08
BRIEF = pl.CostEstimate(flops=1, bytes_accessed=1, transcendentals=0)
f32 = jnp.float32
bf16 = jnp.bfloat16


def nn(a, b):
    return lax.dot_general(a, b, (((1,), (0,)), ((), ())), preferred_element_type=f32)


def nt(a, b):
    return lax.dot_general(a, b, (((1,), (1,)), ((), ())), preferred_element_type=f32)


def tn(a, b):
    return lax.dot_general(a, b, (((0,), (0,)), ((), ())), preferred_element_type=f32)


def normalize_rows(v):
    cent = v - jnp.mean(v, -1, keepdims=True)
    rstd = lax.rsqrt(jnp.mean(cent * cent, -1, keepdims=True) + 1e-05)
    return (cent * rstd, rstd)


def norm_reverse(dy, xhat, rstd, gain):
    scaled = dy * gain
    first = jnp.mean(scaled, -1, keepdims=True)
    second = jnp.mean(scaled * xhat, -1, keepdims=True)
    return rstd * (scaled - first - xhat * second)


def adam_moments(grad, one, two):
    one = beta_one * one + (1.0 - beta_one) * grad
    two = beta_two * two + (1.0 - beta_two) * grad * grad
    step = one / (1.0 - beta_one**STEP) / (jnp.sqrt(two / (1.0 - beta_two**STEP)) + adam_eps)
    return (one, two, step)


def adamw_update(weight, grad, one, two, decay):
    one, two, step = adam_moments(grad, one, two)
    return (weight - 0.3 * (step + decay * weight), one, two)


def swap(x, axis, bit):
    size = lax.axis_size(axis)
    return lax.ppermute(x, axis, [(i, i ^ bit) for i in range(size)])


def sum_over(x, axis):
    bit = 1
    while bit < lax.axis_size(axis):
        x = x + swap(x, axis, bit)
        bit *= 2
    return x


def sum_rounded(x, axis):
    bit = 1
    while bit < lax.axis_size(axis):
        x = lax.reduce_precision(x, 8, 7)
        x = x + swap(x.astype(bf16), axis, bit).astype(f32)
        bit *= 2
    return x


def sum_head(x):
    x = x + swap(x, "head", 1)
    x = lax.reduce_precision(x, 8, 7)
    return x + swap(x.astype(bf16), "head", 2).astype(f32)


def gather_head(x, axis):
    me = lax.axis_index("head")
    bit = 1
    while bit < lax.axis_size("head"):
        away = swap(x, "head", bit)
        mine_first = (me & bit) == 0
        x = jnp.concatenate(
            [jnp.where(mine_first, x, away), jnp.where(mine_first, away, x)], axis
        )
        bit *= 2
    return x


def zero_of(x):
    return (x[(0,) * x.ndim].astype(f32) * 0.0).astype(jnp.int32)


def after(x, *deps):
    return lax.optimization_barrier((x, *deps))[0]


def split_three(x):
    high = lax.reduce_precision(x, 8, 7)
    rest = x - high
    mid = lax.reduce_precision(rest, 8, 7)
    return jnp.concatenate([high, mid, rest - mid], -1).astype(bf16)


def join_three(x):
    n = x.shape[-1] // 3
    x = x.astype(f32)
    return x[..., :n] + x[..., n : 2 * n] + x[..., 2 * n :]


def head_of_lane(rows, cols):
    return lax.broadcasted_iota(jnp.int32, (rows, cols), 1) // HEAD_SIZE


def spread(x):
    owner = head_of_lane(*x.shape)
    x = x.astype(f32)
    return jnp.concatenate([jnp.where(owner == j, x, 0.0) for j in range(GROUP)], 0).astype(bf16)


def collect(r):
    rows = r.shape[0] // GROUP
    owner = head_of_lane(rows, r.shape[1])
    out = jnp.where(owner == 0, r[:rows], 0.0)
    for j in range(1, GROUP):
        out = out + jnp.where(owner == j, r[j * rows : (j + 1) * rows], 0.0)
    return out


def whole(shape):
    return pl.BlockSpec(shape, lambda *_: (0,) * len(shape), pipeline_mode=pl.Buffered(1))


def kernel_absorb(scale, x_ref, w_ref, out_ref):
    out_ref[...] = (nt(spread(x_ref[...]), w_ref[...]) * scale).astype(bf16)


def absorb(x, w, scale):
    depth, width = w.shape
    cols = GROUP * HEAD_SIZE
    groups = width // cols
    rows = GROUP * LATENTS
    return pl.pallas_call(
        functools.partial(kernel_absorb, scale),
        grid=(groups,),
        in_specs=[
            pl.BlockSpec((LATENTS, cols), lambda g: (0, g)),
            pl.BlockSpec((depth, cols), lambda g: (0, g)),
        ],
        out_specs=pl.BlockSpec((rows, depth), lambda g: (g, 0)),
        out_shape=jax.ShapeDtypeStruct((groups * rows, depth), bf16),
        compiler_params=pltpu.CompilerParams(vmem_limit_bytes=VMEM_BYTES),
        cost_estimate=BRIEF,
        name="absorb",
    )(x, w)


def kernel_pick(place, a, b, c, far_o, near_o):
    del place
    far_o[0] = a[...]
    far_o[1] = b[...]
    near_o[...] = c[...]


def pick(feat, place, j, c, videos_dev):
    count, tokens_video, cols = feat.shape
    frames_dev = tokens_video // PATCH
    cuts, nf = chunks_of(frames_dev)
    step = nf * PATCH
    blocks = cuts[c] // nf
    start = (j * frames_dev + sum(cuts[:c])) // nf
    tokens = cuts[c] * PATCH
    feat2 = feat.reshape(count * tokens_video, cols)

    def spot(k):
        return lambda i, p: ((p[0] ^ k) * (videos_dev * frames_dev // nf) + start + i, 0)

    return pl.pallas_call(
        kernel_pick,
        grid_spec=pltpu.PrefetchScalarGridSpec(
            num_scalar_prefetch=1,
            grid=(blocks,),
            in_specs=[pl.BlockSpec((step, cols), spot(k)) for k in (2, 3, 1)],
            out_specs=[
                pl.BlockSpec((2, step, cols), lambda i, p: (0, i, 0)),
                pl.BlockSpec((step, cols), lambda i, p: (i, 0)),
            ],
        ),
        out_shape=[
            jax.ShapeDtypeStruct((2, tokens, cols), bf16),
            jax.ShapeDtypeStruct((tokens, cols), bf16),
        ],
        compiler_params=pltpu.CompilerParams(vmem_limit_bytes=VMEM_BYTES),
        cost_estimate=BRIEF,
        name="pick",
    )(place[None], feat2, feat2, feat2)


def kernel_gate(*refs):
    del refs


def gate(x, *deps):
    anyspec = pl.BlockSpec(memory_space=pl.ANY)
    return pl.pallas_call(
        kernel_gate,
        in_specs=[anyspec] * (1 + len(deps)),
        out_specs=anyspec,
        out_shape=jax.ShapeDtypeStruct(x.shape, x.dtype),
        input_output_aliases={0: 0},
        cost_estimate=BRIEF,
        name="gate",
    )(x, *deps)


def frames_a_block(frames):
    return 2 if frames % 2 == 0 else 1


def chunks_of(frames):
    if frames % 6 == 0:
        return (frames // 3 * 2, frames // 3), frames // 3
    return (frames,), 1


def kernel_read(
    nf, first, carry, final, place, own, ra, rb, rc, time_ref, g0, qw, wv, xn_in, ft_in, e_in, px_in, st_in, o_in, dep,
    xn_o, ft_o, e_o, px_o, st_o, o_o, token_o, xs, acc, run,
):
    del xn_in, ft_in, e_in, o_in, dep
    i = pl.program_id(0)
    tokens, depth = xs.shape
    cols = own.shape[1]
    heads_rows = GROUP * LATENTS
    groups = qw.shape[0] // heads_rows

    @pl.when(i == 0)
    def _():
        if carry:
            acc[...] = px_in[...].astype(f32)
            run[0] = jnp.broadcast_to(st_in[:, 126:127], run.shape[1:])
            run[1] = jnp.broadcast_to(st_in[:, 127:128], run.shape[1:])
            st_o[...] = st_in[...]
        else:
            acc[...] = jnp.zeros_like(acc)
            run[0] = jnp.full(run.shape[1:], -1e30, f32)
            run[1] = jnp.zeros(run.shape[1:], f32)
            st_o[...] = jnp.zeros_like(st_o)

    for k, part in enumerate((own, ra, rb, rc)):
        off = pl.multiple_of((place[0] ^ k) * cols, 128)
        for f in range(nf):
            rows = slice(f * PATCH, (f + 1) * PATCH)
            raw = part[rows, :]
            ft_o[rows, pl.ds(off, cols)] = raw
            row = first + i * nf + f
            moved = raw.astype(f32) + time_ref[pl.ds(row, 1), pl.ds(off, cols)]
            xs[rows, pl.ds(off, cols)] = moved.astype(bf16)
    x = xs[...].astype(f32)
    cent = x - jnp.sum(x, -1, keepdims=True) * (1.0 / depth)
    rstd = lax.rsqrt(jnp.sum(cent * cent, -1, keepdims=True) * (1.0 / depth) + 1e-05)
    xn_o[:, :depth] = (cent * rstd * g0[...]).astype(bf16)
    lane = lax.broadcasted_iota(jnp.int32, (tokens, EXTRA), 1)
    frame = lax.broadcasted_iota(jnp.int32, (tokens, EXTRA), 0) // PATCH + first + i * nf
    xn_o[:, depth:] = jnp.where(lane == frame, rstd, 0.0).astype(bf16)
    key = lax.broadcasted_iota(jnp.int32, (1, tokens), 1)
    limit = place[1 + first + i * nf]
    for f in range(1, nf):
        limit = jnp.where(key >= f * PATCH, f * PATCH + place[1 + first + i * nf + f], limit)
    valid = key < limit
    block = lax.broadcasted_iota(jnp.int32, (heads_rows, 128), 1)
    last = i == pl.num_programs(0) - 1
    for g in range(groups):
        rows = slice(g * heads_rows, (g + 1) * heads_rows)
        scores = jnp.where(valid, nt(qw[rows, :], xn_o[:, :depth]), -1e30)
        old = run[0, rows, :]
        new = jnp.maximum(old, jnp.max(scores, -1, keepdims=True))
        expo = jnp.exp(scores - new[:, :1])
        shrink = jnp.exp(old - new)
        total = run[1, rows, :] * shrink + jnp.sum(expo, -1, keepdims=True)
        run[0, rows, :] = new
        run[1, rows, :] = total
        low = expo.astype(bf16)
        e_o[rows, :] = low
        stats = jnp.where(block == first // nf + i, new, st_o[rows, :])
        stats = jnp.where(last & (block == 126), new, stats)
        st_o[rows, :] = jnp.where(last & (block == 127), total, stats)
        acc[rows, :] = acc[rows, :] * shrink[:, :1] + nn(low, xn_o[...])

    @pl.when(last)
    def _():
        for g in range(groups):
            rows = slice(g * heads_rows, (g + 1) * heads_rows)
            wide = slice(g * cols, (g + 1) * cols)
            held = acc[rows, :].astype(bf16)
            px_o[rows, :] = held
            if final:
                mixed = nn(held[:, :depth], wv[:, wide]) * (1.0 / run[1, rows, :1])
                o_o[:, wide] = collect(mixed)
        if not final:
            o_o[...] = jnp.zeros_like(o_o)
        token_o[...] = run[1, 0:8, :]


def read_pass(j, c, prev, feat, got, time_full, gain, lens, qw, wv, dep, h, videos_dev):
    count, tokens_video, cols = feat.shape
    depth = wv.shape[0]
    frames_dev = tokens_video // PATCH
    cuts, nf = chunks_of(frames_dev)
    chunks = len(cuts)
    frames = cuts[c]
    before = sum(cuts[:c])
    tokens = nf * PATCH
    blocks = frames // nf
    start = (j * frames_dev + before) // nf
    rows = qw.shape[0]
    place = jnp.concatenate([h[None], lens]).astype(jnp.int32)
    feat2 = feat.reshape(count * tokens_video, cols)
    shapes = (
        jax.ShapeDtypeStruct((videos_dev * tokens_video, depth + EXTRA), bf16),
        jax.ShapeDtypeStruct((videos_dev * tokens_video, depth), bf16),
        jax.ShapeDtypeStruct((videos_dev * rows, tokens_video), bf16),
        jax.ShapeDtypeStruct((videos_dev * rows, depth + EXTRA), bf16),
        jax.ShapeDtypeStruct((videos_dev * rows, 128), f32),
        jax.ShapeDtypeStruct((videos_dev * LATENTS, depth), f32),
    )
    aliases = {}
    if prev is None:
        prev = [jnp.zeros((16, 128), s.dtype) for s in shapes]
    else:
        aliases = {9 + n: n for n in range(6)}
    anyspec = pl.BlockSpec(memory_space=pl.ANY)
    one = pl.Buffered(1)
    return pl.pallas_call(
        functools.partial(kernel_read, nf, before, c > 0, c == chunks - 1),
        grid_spec=pltpu.PrefetchScalarGridSpec(
            num_scalar_prefetch=1,
            grid=(blocks,),
            in_specs=[
                pl.BlockSpec(
                    (tokens, cols),
                    lambda i, p: (p[0] * (videos_dev * frames_dev // nf) + start + i, 0),
                ),
                pl.BlockSpec((tokens, cols), lambda i, p: (i, 0)),
                pl.BlockSpec((tokens, cols), lambda i, p: (i, 0)),
                pl.BlockSpec((tokens, cols), lambda i, p: (i, 0)),
                whole(time_full.shape),
                whole(gain.shape),
                whole(qw.shape),
                whole(wv.shape),
            ]
            + [anyspec] * 3
            + (
                [
                    pl.BlockSpec((rows, depth + EXTRA), lambda i, p: (j, 0), pipeline_mode=one),
                    pl.BlockSpec((rows, 128), lambda i, p: (j, 0), pipeline_mode=one),
                ]
                if c
                else [anyspec] * 2
            )
            + [anyspec] * 2,
            out_specs=[
                pl.BlockSpec((tokens, depth + EXTRA), lambda i, p: (start + i, 0)),
                pl.BlockSpec((tokens, depth), lambda i, p: (start + i, 0)),
                pl.BlockSpec((rows, tokens), lambda i, p: (j, before // nf + i)),
                pl.BlockSpec((rows, depth + EXTRA), lambda i, p: (j, 0), pipeline_mode=one),
                pl.BlockSpec((rows, 128), lambda i, p: (j, 0), pipeline_mode=one),
                pl.BlockSpec((LATENTS, depth), lambda i, p: (j, 0), pipeline_mode=one),
                whole((8, 128)),
            ],
            scratch_shapes=[
                pltpu.VMEM((tokens, depth), bf16),
                pltpu.VMEM((rows, depth + EXTRA), f32),
                pltpu.VMEM((2, rows, 128), f32),
            ],
        ),
        out_shape=(*shapes, jax.ShapeDtypeStruct((8, 128), f32)),
        input_output_aliases=aliases,
        compiler_params=pltpu.CompilerParams(vmem_limit_bytes=VMEM_BYTES),
        cost_estimate=pl.CostEstimate(
            flops=rows * frames * PATCH * depth // 2,
            bytes_accessed=frames * PATCH * depth,
            transcendentals=rows * frames * PATCH,
        ),
        name="read_pass",
    )(place, feat2, *got, time_full, gain, qw, wv, *prev, dep)


def kernel_decode(
    nf, scale, xn, feat, msk, dq, dv, wk,
    ddq_o, ddv_o, dx_o, side_o, loss_o, dqw, dvd, sc, zs, acc, dacc, loss,
):
    i = pl.program_id(1)
    tokens = xn.shape[0]
    depth = wk.shape[0]
    heads_rows = GROUP * LATENTS
    total_rows = dqw.shape[0]
    groups = total_rows // heads_rows
    cols = depth // groups

    @pl.when(i == 0)
    def _():
        acc[...] = jnp.zeros_like(acc)
        dacc[...] = jnp.zeros_like(dacc)
        loss[...] = jnp.zeros_like(loss)
        for g in range(groups):
            rows = slice(g * heads_rows, (g + 1) * heads_rows)
            wide = slice(g * cols, (g + 1) * cols)
            dqw[rows, :] = (nt(spread(dq[:, wide]), wk[:, wide]) * scale).astype(bf16)
            dvd[g] = spread(dv[:, wide])

    sc[...] = nt(dqw[...], xn[:, :depth])
    counts = msk[...]
    second = jnp.zeros((1, tokens), f32)
    for g in range(groups):
        rows = slice(g * heads_rows, (g + 1) * heads_rows)
        wide = slice(g * cols, (g + 1) * cols)
        s = sc[rows, :].reshape(GROUP, LATENTS, tokens)
        a = jnp.exp(s - jnp.max(s, 1, keepdims=True))
        a = a * (1.0 / jnp.sum(a, 1, keepdims=True))
        low = a.reshape(heads_rows, tokens).astype(bf16)
        error = tn(low, dvd[g]) - feat[:, wide].astype(f32)
        kept = counts * error
        loss[...] += jnp.sum((kept * error).reshape(tokens // 8, 8, cols), 0)
        dp = (2.0 * kept).astype(bf16)
        dacc[g] += nn(low, dp)
        da = nt(dvd[g], dp).reshape(GROUP, LATENTS, tokens)
        z = a * (da - jnp.sum(a * da, 1, keepdims=True))
        second = second + jnp.sum((z * s).reshape(heads_rows, tokens), 0, keepdims=True)
        zs[rows, :] = z.reshape(heads_rows, tokens).astype(bf16)
    zs[total_rows:, :] = tail_rows(nf, i, second, xn, depth)
    acc[...] += nn(zs[...], xn[...])

    @pl.when(i == pl.num_programs(1) - 1)
    def _():
        gain = jnp.zeros((8, depth), f32)
        for g in range(groups):
            rows = slice(g * heads_rows, (g + 1) * heads_rows)
            wide = slice(g * cols, (g + 1) * cols)
            held = acc[rows, :depth]
            low = held.astype(bf16)
            dx_o[rows, :] = low
            ddq_o[:, wide] = collect(nn(low, wk[:, wide])) * scale
            ddv_o[:, wide] = collect(dacc[g])
            gain = gain + jnp.sum(
                (held * dqw[rows, :].astype(f32)).reshape(heads_rows // 8, 8, depth), 0
            )
        side_o[0, 0:TAIL, :] = tn(acc[:total_rows, depth:].astype(bf16), dqw[...])[:TAIL]
        side_o[0, TAIL : 2 * TAIL, :] = acc[total_rows:, :depth]
        side_o[0, 2 * TAIL :, :] = gain
        loss_o[0] = loss[...]


def tail_rows(nf, i, second, xn, depth):
    tokens = xn.shape[0]
    rstd = nt(jnp.ones((TAIL, EXTRA), bf16), xn[:, depth:])
    row = lax.broadcasted_iota(jnp.int32, (TAIL, tokens), 0)
    frame = lax.broadcasted_iota(jnp.int32, (TAIL, tokens), 1) // PATCH + i * nf
    return jnp.where(row == frame, rstd * second * (1.0 / depth), 0.0).astype(bf16)


def decode_pass(xn_all, ft_all, counts, dq_all, dv_all, wk, scale, videos_dev):
    depth = wk.shape[0]
    tokens_video = xn_all.shape[0] // videos_dev
    cols = GROUP * HEAD_SIZE
    frames_dev = tokens_video // PATCH
    nf = frames_a_block(frames_dev)
    tokens = nf * PATCH
    blocks = frames_dev // nf
    groups = depth // cols
    heads_rows = GROUP * LATENTS
    rows = groups * heads_rows
    one = pl.Buffered(1)
    return pl.pallas_call(
        functools.partial(kernel_decode, nf, scale),
        grid=(videos_dev, blocks),
        in_specs=[
            pl.BlockSpec((tokens, depth + EXTRA), lambda j, i: (j * blocks + i, 0)),
            pl.BlockSpec((tokens, depth), lambda j, i: (j * blocks + i, 0)),
            pl.BlockSpec((tokens, 1), lambda j, i: (j * blocks + i, 0)),
            pl.BlockSpec((LATENTS, depth), lambda j, i: (j, 0), pipeline_mode=one),
            pl.BlockSpec((LATENTS, depth), lambda j, i: (j, 0), pipeline_mode=one),
            whole(wk.shape),
        ],
        out_specs=[
            pl.BlockSpec((LATENTS, depth), lambda j, i: (j, 0), pipeline_mode=one),
            pl.BlockSpec((LATENTS, depth), lambda j, i: (j, 0), pipeline_mode=one),
            pl.BlockSpec((rows, depth), lambda j, i: (j, 0), pipeline_mode=one),
            pl.BlockSpec((1, 2 * TAIL + 8, depth), lambda j, i: (j, 0, 0), pipeline_mode=one),
            pl.BlockSpec((1, 8, cols), lambda j, i: (j, 0, 0), pipeline_mode=one),
        ],
        scratch_shapes=[
            pltpu.VMEM((rows, depth), bf16),
            pltpu.VMEM((groups, heads_rows, cols), bf16),
            pltpu.VMEM((rows, tokens), f32),
            pltpu.VMEM((rows + TAIL, tokens), bf16),
            pltpu.VMEM((rows + TAIL, depth + EXTRA), f32),
            pltpu.VMEM((groups, heads_rows, cols), f32),
            pltpu.VMEM((8, cols), f32),
        ],
        out_shape=(
            jax.ShapeDtypeStruct((videos_dev * LATENTS, depth), f32),
            jax.ShapeDtypeStruct((videos_dev * LATENTS, depth), f32),
            jax.ShapeDtypeStruct((videos_dev * rows, depth), bf16),
            jax.ShapeDtypeStruct((videos_dev, 2 * TAIL + 8, depth), f32),
            jax.ShapeDtypeStruct((videos_dev, 8, cols), f32),
        ),
        compiler_params=pltpu.CompilerParams(vmem_limit_bytes=VMEM_BYTES),
        cost_estimate=pl.CostEstimate(
            flops=6 * rows * tokens_video * depth,
            bytes_accessed=tokens_video * depth * 4,
            transcendentals=rows * tokens_video,
        ),
        name="decode_pass",
    )(xn_all, ft_all, counts, dq_all, dv_all, wk)


def head_column(ld, first):
    lane = lax.broadcasted_iota(jnp.int32, ld.shape, 1)
    return jnp.concatenate(
        [jnp.sum(jnp.where(lane == first + j, ld, 0.0), -1, keepdims=True) for j in range(GROUP)], 0
    )


def kernel_value(chunks, place, do, wv, ld, *rest):
    pxs = rest[:chunks]
    sts = rest[chunks : 2 * chunks]
    ow_o, near_o, away_o, side_o, acc = rest[2 * chunks :]
    k = pl.program_id(0)
    v = pl.program_id(1)
    depth = wv.shape[0]

    @pl.when((k == 0) & (v == 0))
    def _():
        side_o[...] = jnp.zeros_like(side_o)

    diag = spread(do[...])
    ow = nt(diag, wv[...]).astype(bf16)
    ow_o[...] = ow
    norm = 0.0
    lse = head_column(ld[...], (place[0] ^ k) * GROUP)
    for px, st in zip(pxs, sts):
        norm = norm + px[...].astype(f32) * jnp.exp(st[:, 126:127] - lse)
    low = norm.astype(bf16)
    part = tn(diag, low[:, :depth])

    @pl.when(v == 0)
    def _():
        acc[...] = part

    @pl.when(v > 0)
    def _():
        acc[...] += part

    @pl.when(k & 1 == 0)
    def _():
        near_o[0] = acc[...].astype(bf16)

    @pl.when(k & 1 == 1)
    def _():
        away_o[0] = acc[...].astype(bf16)

    side_o[0:TAIL, :] += tn(low[:, depth:], ow)[:TAIL]
    rows = ow.shape[0]
    side_o[TAIL:, :] += jnp.sum((ow.astype(f32) * norm[:, :depth]).reshape(rows // 8, 8, depth), 0)


def value_pass(do_all, wv, px_all, st_all, ld, h, videos_dev):
    depth = wv.shape[0]
    cols = GROUP * HEAD_SIZE
    groups = depth // cols
    rows = GROUP * LATENTS
    chunks = px_all.shape[0] // (videos_dev * groups * rows)

    def spot(c):
        return lambda k, v, p: ((v * chunks + c) * groups + (p[0] ^ k), 0)

    return pl.pallas_call(
        functools.partial(kernel_value, chunks),
        grid_spec=pltpu.PrefetchScalarGridSpec(
            num_scalar_prefetch=1,
            grid=(groups, videos_dev),
            in_specs=[
                pl.BlockSpec((LATENTS, cols), lambda k, v, p: (v, p[0] ^ k)),
                pl.BlockSpec((depth, cols), lambda k, v, p: (0, p[0] ^ k)),
                pl.BlockSpec((LATENTS, 128), lambda k, v, p: (v, 0)),
            ]
            + [pl.BlockSpec((rows, depth + EXTRA), spot(c)) for c in range(chunks)]
            + [pl.BlockSpec((rows, 128), spot(c)) for c in range(chunks)],
            out_specs=[
                pl.BlockSpec((rows, depth), lambda k, v, p: (v * groups + (p[0] ^ k), 0)),
                pl.BlockSpec((1, cols, depth), lambda k, v, p: (k >> 1, 0, 0)),
                pl.BlockSpec((1, cols, depth), lambda k, v, p: (k >> 1, 0, 0)),
                pl.BlockSpec((TAIL + 8, depth), lambda k, v, p: (0, 0)),
            ],
            scratch_shapes=[pltpu.VMEM((cols, depth), f32)],
        ),
        out_shape=(
            jax.ShapeDtypeStruct((videos_dev * groups * rows, depth), bf16),
            jax.ShapeDtypeStruct((groups // 2, cols, depth), bf16),
            jax.ShapeDtypeStruct((groups // 2, cols, depth), bf16),
            jax.ShapeDtypeStruct((TAIL + 8, depth), f32),
        ),
        compiler_params=pltpu.CompilerParams(vmem_limit_bytes=VMEM_BYTES),
        cost_estimate=BRIEF,
        name="value_pass",
    )(jnp.full((1,), h, jnp.int32), do_all, wv, ld, *[px_all] * chunks, *[st_all] * chunks)


def kernel_back(
    nf, per_read, scale, videos_dev, final, place, xn, e, st, ld, ow, qw, q, wk, *rest
):
    dqs = rest[:videos_dev]
    dxs = rest[videos_dev : 2 * videos_dev]
    rest = rest[2 * videos_dev :]
    if final:
        g0, side_a, side_b, dq_o, near_o, away_o, pack_o, zs, acc, pack = rest
    else:
        dq_o, near_o, away_o, side_o, zs, acc = rest
    v = pl.program_id(0)
    i = pl.program_id(1)
    tokens = xn.shape[0]
    depth = wk.shape[0]
    heads_rows = GROUP * LATENTS
    total_rows = qw.shape[0]
    groups = total_rows // heads_rows
    cols = GROUP * HEAD_SIZE

    @pl.when((v == 0) & (i == 0))
    def _():
        acc[...] = jnp.zeros_like(acc)

    second = jnp.zeros((1, tokens), f32)
    block = lax.broadcasted_iota(jnp.int32, (heads_rows, 128), 1)
    heads_total = depth // HEAD_SIZE
    base = (place[0] >> 1 if final else (place[0] >> 1) ^ 1) * groups
    for g in range(groups):
        rows = slice(g * heads_rows, (g + 1) * heads_rows)
        spot = i // per_read
        peak = jnp.sum(jnp.where(block == spot, st[rows, :], 0.0), -1, keepdims=True)
        lse = head_column(ld[...], (base + g) * GROUP)
        delta = head_column(ld[...], (heads_total // GROUP + base + g) * GROUP)
        dp = nt(ow[rows, :], xn[:, :depth])
        expo = e[rows, :].astype(f32)
        prob = expo * jnp.exp(peak - lse)
        z = prob * (dp - delta)
        score = jnp.log(jnp.maximum(expo, 1e-37)) + peak
        second = second + jnp.sum(z * score + prob * dp, 0, keepdims=True)
        zs[rows, :] = z.astype(bf16)
    zs[total_rows:, :] = tail_rows(nf, i, second, xn, depth)
    acc[...] += nn(zs[...], xn[...])

    @pl.when((v == videos_dev - 1) & (i == pl.num_programs(1) - 1))
    def _():
        gain = jnp.zeros((8, depth), f32)
        for k in range(groups):
            g = (place[0] & 1) ^ k
            rows = pl.ds(pl.multiple_of(g * heads_rows, heads_rows), heads_rows)
            wide = pl.ds(pl.multiple_of(g * cols, 128), cols)
            low = acc[rows, :depth].astype(bf16)
            dq_o[k] = collect(nn(low, wk[:, wide])) * scale
            grad = tn(spread(q[:, wide]), low)
            for one, dx in zip(dqs, dxs):
                grad = grad + tn(spread(one[:, wide]), dx[rows, :])
            target = away_o if k & 1 else near_o
            target[...] = (grad * scale).astype(bf16)
        for g in range(groups):
            rows = slice(g * heads_rows, (g + 1) * heads_rows)
            gain = gain + jnp.sum(
                (acc[rows, :depth] * qw[rows, :].astype(f32)).reshape(heads_rows // 8, 8, depth), 0
            )
        pulled = tn(acc[:total_rows, depth:].astype(bf16), qw[...])[:TAIL]
        moved = acc[total_rows:, :depth]
        if final:
            pulled = (pulled + side_a[0:TAIL, :] + side_b[0:TAIL, :]) * g0[...]
            moved = moved + side_a[TAIL : 2 * TAIL, :] + side_b[TAIL : 2 * TAIL, :]
            moved = moved * (1.0 / g0[...])
            gain = gain + side_a[2 * TAIL :, :] + side_b[2 * TAIL :, :]
            mean = jnp.sum(pulled, -1, keepdims=True) * (1.0 / depth)
            pack[0:TAIL, :] = pulled - mean - moved
            pack[TAIL:, :] = gain * (1.0 / g0[...])
            for k in range(pack_o.shape[0]):
                wide = pl.ds(pl.multiple_of((place[0] ^ k) * cols, 128), cols)
                pack_o[(k & 1) * 2 + (k >> 1)] = pack[:, wide]
        else:
            side_o[0:TAIL, :] = pulled
            side_o[TAIL : 2 * TAIL, :] = moved
            side_o[2 * TAIL :, :] = gain


def back_pass(
    far, xn_all, e_all, st_all, ld, ow, qw, q_all, wk, dq_all, dx_all, sides, gain, scale, h, videos_dev
):
    depth = wk.shape[0]
    tokens_video = e_all.shape[1]
    frames_dev = tokens_video // PATCH
    _, read_nf = chunks_of(frames_dev)
    nf = frames_a_block(read_nf)
    tokens = nf * PATCH
    blocks = frames_dev // nf
    rows = qw.shape[0] // 2
    cols = GROUP * HEAD_SIZE
    groups = depth // cols
    packed = TAIL + 8
    final = not far
    one = pl.Buffered(1)

    def y(p):
        return (p[0] >> 1) ^ 1 if far else p[0] >> 1

    outs = [
        jax.ShapeDtypeStruct((2, LATENTS, cols), f32),
        jax.ShapeDtypeStruct((cols, depth), bf16),
        jax.ShapeDtypeStruct((cols, depth), bf16),
    ]
    scratch = [
        pltpu.VMEM((rows + TAIL, tokens), bf16),
        pltpu.VMEM((rows + TAIL, depth + EXTRA), f32),
    ]
    extra = []
    if final:
        extra = [gain, *sides]
        outs.append(jax.ShapeDtypeStruct((groups, packed, cols), f32))
        scratch.append(pltpu.VMEM((packed, depth), f32))
    else:
        outs.append(jax.ShapeDtypeStruct((2 * TAIL + 8, depth), f32))
    return pl.pallas_call(
        functools.partial(
            kernel_back, nf, read_nf // nf, scale, videos_dev, final
        ),
        grid_spec=pltpu.PrefetchScalarGridSpec(
            num_scalar_prefetch=1,
            grid=(videos_dev, blocks),
            in_specs=[
                pl.BlockSpec((tokens, depth + EXTRA), lambda v, i, p: (v * blocks + i, 0)),
                pl.BlockSpec((rows, tokens), lambda v, i, p: (v * 2 + y(p), i)),
                pl.BlockSpec((rows, 128), lambda v, i, p: (v * 2 + y(p), 0)),
                pl.BlockSpec((LATENTS, 128), lambda v, i, p: (v, 0)),
                pl.BlockSpec((rows, depth), lambda v, i, p: (v * 2 + y(p), 0)),
                pl.BlockSpec((rows, depth), lambda v, i, p: (y(p), 0), pipeline_mode=one),
                pl.BlockSpec((LATENTS, 2 * cols), lambda v, i, p: (0, y(p)), pipeline_mode=one),
                pl.BlockSpec((depth, 2 * cols), lambda v, i, p: (0, y(p)), pipeline_mode=one),
            ]
            + [
                pl.BlockSpec((LATENTS, 2 * cols), lambda v, i, p, n=n: (n, y(p)), pipeline_mode=one)
                for n in range(videos_dev)
            ]
            + [
                pl.BlockSpec((rows, depth), lambda v, i, p, n=n: (n * 2 + y(p), 0), pipeline_mode=one)
                for n in range(videos_dev)
            ]
            + [whole(a.shape) for a in extra],
            out_specs=[whole(a.shape) for a in outs],
            scratch_shapes=scratch,
        ),
        out_shape=outs,
        compiler_params=pltpu.CompilerParams(vmem_limit_bytes=VMEM_BYTES),
        cost_estimate=pl.CostEstimate(
            flops=4 * videos_dev * rows * tokens_video * depth,
            bytes_accessed=videos_dev * tokens_video * depth * 4,
            transcendentals=videos_dev * rows * tokens_video,
        ),
        name="back_far" if far else "back_near",
    )(
        jnp.full((1,), h, jnp.int32), xn_all, e_all, st_all, ld, ow, qw, q_all, wk,
        *[dq_all] * videos_dev, *[dx_all] * videos_dev, *extra,
    )


def halves(x):
    high = x.astype(bf16)
    return high, (x - high.astype(f32)).astype(bf16)


def precise(a, b, dims):
    dims = ((dims[0], dims[1]), ((), ()))
    ah, al = halves(a)
    bh, bl = halves(b)
    out = lax.dot_general(ah, bh, dims, preferred_element_type=f32)
    out = out + lax.dot_general(ah, bl, dims, preferred_element_type=f32)
    return out + lax.dot_general(al, bh, dims, preferred_element_type=f32)


def turn_body(g, left, right, out, total):
    @pl.when(pl.program_id(0) == 0)
    def _():
        total[...] = jnp.zeros_like(total)

    rows, cols = g.shape
    square = g * g
    part = square[:, :128]
    for c in range(1, cols // 128):
        part = part + square[:, c * 128 : (c + 1) * 128]
    total[...] += jnp.sum(part.reshape(rows // 8, 8, 128), 0)
    turned = precise(left[0], g, ((0,), (0,)))
    for c in range(cols // 128):
        wide = slice(c * 128, (c + 1) * 128)
        out[:, wide] = precise(turned[:, wide], right[0, c], ((1,), (0,)))


def kernel_turn(grad, left, right, out, total):
    turn_body(grad[...].astype(f32), left, right, out, total)


def kernel_turn_product(a, b, left, right, out, total):
    frames, _, rows, own = a.shape
    turn_body(tn(a[...].reshape(frames * rows, own), b[...]), left, right, out, total)


def kernel_turn_sum(a, b, c, d, left, right, out, total):
    frames, _, rows, own = a.shape
    grad = tn(a[...].reshape(frames * rows, own), b[...]) + tn(c[...], d[...])
    turn_body(grad, left, right, out, total)


def turn(slab, slot, operands, rows, cols, left, right):
    step = 3 * 128
    if len(operands) == 1:
        body = kernel_turn
        specs = [pl.BlockSpec((rows, step), lambda i: (0, i))]
        arrays = operands
    else:
        a, which, b, first = operands[:4]
        body = kernel_turn_product
        specs = [
            pl.BlockSpec((a.shape[0], 1) + a.shape[2:], lambda i: (0, which, 0, 0)),
            pl.BlockSpec((b.shape[0], step), lambda i: (0, first // step + i)),
        ]
        arrays = [a, b]
        if len(operands) > 4:
            body = kernel_turn_sum
            c, d = operands[4:]
            specs += [
                pl.BlockSpec(c.shape, lambda i: (0, 0)),
                pl.BlockSpec((d.shape[0], step), lambda i: (0, i)),
            ]
            arrays += [c, d]
    return pl.pallas_call(
        body,
        grid=(cols // step,),
        in_specs=specs
        + [
            pl.BlockSpec((1, rows, rows), lambda i: (slab, 0, 0)),
            pl.BlockSpec((1, 3, 128, 128), lambda i: (slot, i, 0, 0)),
        ],
        out_specs=[
            pl.BlockSpec((rows, step), lambda i: (0, i)),
            pl.BlockSpec((8, 128), lambda i: (0, 0)),
        ],
        out_shape=(
            jax.ShapeDtypeStruct((rows, cols), f32),
            jax.ShapeDtypeStruct((8, 128), f32),
        ),
        compiler_params=pltpu.CompilerParams(vmem_limit_bytes=VMEM_BYTES),
        cost_estimate=BRIEF,
        name="turn",
    )(*arrays, left, right)


def kernel_update(rates, factor, weight, one, two, left, right, *rest):
    turned = rest[: len(rates)]
    new_o, one_o, two_o, low_o = rest[len(rates) :]
    slab = pl.program_id(0)
    g = turned[0][...]
    rate = jnp.float32(rates[0])
    for n in range(1, len(rates)):
        g = jnp.where(slab == n, turned[n][...], g)
        rate = jnp.where(slab == n, jnp.float32(rates[n]), rate)
    first, second, step = adam_moments(g * factor[0], one[0], two[0])
    one_o[0] = first
    two_o[0] = second
    cols = step.shape[1]
    back = jnp.concatenate(
        [
            precise(step[:, c * 128 : (c + 1) * 128], right[0, c], ((1,), (1,)))
            for c in range(cols // 128)
        ],
        1,
    )
    back = precise(left[0], back, ((1,), (0,)))
    held = weight[0]
    new = held - rate * (back + 0.01 * held)
    new_o[0] = new
    low_o[0] = new.astype(bf16)


def update(factor, weight, one, two, first_slab, left, right, turned, rates):
    slabs, rows, cols = weight.shape
    step = 6 * 128 if cols % (6 * 128) == 0 else 3 * 128
    tile = pl.BlockSpec((1, rows, step), lambda s, i: (s, 0, i))
    own = [
        pl.BlockSpec((rows, step), lambda s, i, n=n: (0, jnp.where(s == n, i, 0)))
        for n in range(slabs)
    ]
    return pl.pallas_call(
        functools.partial(kernel_update, rates),
        grid=(slabs, cols // step),
        in_specs=[
            pl.BlockSpec(memory_space=pltpu.SMEM),
            tile,
            tile,
            tile,
            pl.BlockSpec((1, rows, rows), lambda s, i: (first_slab + s, 0, 0)),
            pl.BlockSpec((1, step // 128, 128, 128), lambda s, i: (s, i, 0, 0)),
        ]
        + own,
        out_specs=[tile] * 4,
        out_shape=[jax.ShapeDtypeStruct(weight.shape, f32)] * 3
        + [jax.ShapeDtypeStruct(weight.shape, bf16)],
        compiler_params=pltpu.CompilerParams(vmem_limit_bytes=VMEM_BYTES),
        cost_estimate=BRIEF,
        name="update",
    )(factor, weight, one, two, left, right, *turned)


def sum_near(near, away):
    near = near.astype(f32) + swap(away, "head", 1).astype(f32)
    return near[0] + swap(near[1].astype(bf16), "head", 2).astype(f32)


def to_frames(x):
    f = lax.axis_index("frame")
    out = []
    for d in range(x.shape[0]):
        piece = lax.dynamic_index_in_dim(x, f ^ d, 0, False)
        out.append(swap(piece, "frame", d) if d else piece)
    return jnp.stack(out)


def scatter_deep(x):
    mine = lax.axis_index("frame") >> 1
    total = lax.dynamic_index_in_dim(x, mine, 0, False)
    low = x.astype(bf16)
    for d in range(1, x.shape[0]):
        send = lax.dynamic_index_in_dim(low, mine ^ d, 0, False)
        total = total + swap(send, "frame", 2 * d).astype(f32)
    return total


def per_device(
    features, lengths, loss_mask, sq_weight, sq_first, sq_second, ffn_weight, ffn_first,
    ffn_second, left_bases, right_sq, right_ffn, latents, lat_first, lat_second, time_embed,
    time_first, time_second, gains, gain_first, gain_second,
):
    videos, frames_dev, patches, cols = features.shape
    lat_count, depth = latents.shape
    heads_dev = cols // HEAD_SIZE
    head_size = lax.axis_size("head")
    frame_size = lax.axis_size("frame")
    videos_dev = videos // head_size
    rows_dev = sq_weight.shape[1]
    scale = HEAD_SIZE ** (-0.5)
    f = lax.axis_index("frame")
    h = lax.axis_index("head")
    first_frame = (f == 0).astype(f32)
    first_head = (h == 0).astype(f32)
    share = videos_dev * lat_count // frame_size
    tokens_video = frames_dev * patches

    chunks = len(chunks_of(frames_dev)[0])
    feat = features.reshape(videos, tokens_video, cols)

    with jax.named_scope("weights"):
        sq_low = sq_weight.astype(bf16)
        ffn_low = ffn_weight.astype(bf16)
        zhat_zero, zrstd_zero = normalize_rows(latents)
        normed_lat = (zhat_zero * gains[1]).astype(bf16)
        normed_own = lax.dynamic_slice_in_dim(normed_lat, f * rows_dev, rows_dev, 1)
        kv_own = jnp.concatenate([sq_low[1], sq_low[2]], 1)
        kv_far = swap(kv_own, "head", 2)
        low_side = (h & 2) == 0
        kv_rows = jnp.concatenate(
            [jnp.where(low_side, kv_own, kv_far), jnp.where(low_side, kv_far, kv_own)], 1
        )
        away, near = zip(
            *[pick(feat, h, j, c, videos_dev) for j in range(videos_dev) for c in range(chunks)]
        )
        slabs, blocks_dev, bl, _ = left_bases.shape
        left = (
            left_bases[:, :, :, None, :] * jnp.eye(blocks_dev, dtype=f32)[None, :, None, :, None]
        ).reshape(slabs, rows_dev, rows_dev)
        opening = gate(away[0], kv_far)
        query = nn(normed_own, sq_low[0])
        bit = 1
        while bit < frame_size:
            query = query + swap(query, "frame", bit)
            if bit == 1:
                held = sum((zero_of(n) for n in near[1:]), zero_of(opening))
                query = query + held.astype(f32)
            bit *= 2
        query = query.astype(bf16)
        even_core = (h & 1) == 0
        q_all = gather_head(query, 1)
        time_full = gather_head(time_embed, 1)

    with jax.named_scope("exchange"):
        crossed = [swap(opening, "head", 2)]
        waiting = [opening] + [gate(n, crossed[0], q_all, time_full) for n in away[1:2]]

    with jax.named_scope("weights"):
        kv_half = lax.all_gather(kv_rows, "frame", axis=0, tiled=True)
        kv_half = kv_half + (zero_of(waiting[-1]) + zero_of(left)).astype(bf16)
        kv_away = swap(kv_half, "head", 1)
        even = jnp.where(even_core, kv_half, kv_away)
        odd = jnp.where(even_core, kv_away, kv_half)
        w_key, w_value = (
            jnp.concatenate(
                [
                    side[:, at : at + cols]
                    for at in (n * cols, (n + 2) * cols)
                    for side in (even, odd)
                ],
                1,
            )
            for n in (0, 1)
        )
        rest = lax.all_gather(
            after(
                jnp.concatenate([sq_low[0], sq_low[3], sq_low[4], ffn_low[0], ffn_low[1]], 1), kv_half
            ),
            "frame",
            axis=0,
            tiled=True,
        )
        w_query, w_outt, w_dec = (rest[:, n * cols : (n + 1) * cols] for n in range(3))
        hid = ffn_low.shape[2]
        w_up = rest[:, 3 * cols : 3 * cols + hid]
        w_downt = rest[:, 3 * cols + hid :]
        w_key_own = jnp.where(low_side, kv_half[:, :cols], kv_half[:, 2 * cols : 3 * cols])
        w_value_own = jnp.where(low_side, kv_half[:, cols : 2 * cols], kv_half[:, 3 * cols :])

    with jax.named_scope("latent_keys"):
        lat_key = nn(normed_lat, w_key_own).astype(bf16).reshape(lat_count, heads_dev, HEAD_SIZE)
        lat_value = nn(normed_lat, w_value_own).astype(bf16).reshape(lat_count, heads_dev, HEAD_SIZE)
        qw = absorb(q_all, w_key, scale)

    with jax.named_scope("read"):
        own_lens = lax.dynamic_slice_in_dim(lengths, h * videos_dev, videos_dev, 0)
        state = None
        parts = videos_dev * chunks
        token = qw
        for n in range(parts):
            j, c = divmod(n, chunks)
            passed = crossed[n][1] if n < 2 else gate(crossed[n][1], token)
            got = [swap(near[n], "head", 1), crossed[n].reshape(-1, cols), swap(passed, "head", 1)]
            if n + 1 < parts:
                crossed.append(swap(waiting[n + 1], "head", 2))
            if n + 2 < parts and n % 2 == 0:
                waiting.append(gate(away[n + 2], crossed[n + 1], token))
            *state, token = read_pass(
                j, c, state, feat, got, time_full, gains[0:1], own_lens[j], qw, w_value,
                waiting[-1], h, videos_dev,
            )
            if n + 2 < parts and n % 2 == 1:
                waiting.append(gate(away[n + 2], crossed[n + 1], token))
        xn_all, ft_all, e_all, px_all, st_all, o_all = state

    with jax.named_scope("combine"):
        heads = depth // HEAD_SIZE
        lse_local = (
            (st_all[:, 126] + jnp.log(st_all[:, 127]))
            .reshape(videos_dev, heads, lat_count)
            .transpose(0, 2, 1)
            .reshape(videos_dev * lat_count, heads)
        )
        pay = jnp.concatenate(
            [o_all.astype(bf16), split_three(lse_local)], 1
        ).reshape(frame_size, share, depth + 3 * heads)
        pay = to_frames(pay)
        lse_each = join_three(pay[..., depth:])
        o_each = pay[..., :depth].astype(f32).reshape(frame_size, share, heads, HEAD_SIZE)
        top = jnp.max(lse_each, 0)
        weight = jnp.exp(lse_each - top)
        total = jnp.sum(weight, 0)
        o_tok = jnp.sum(o_each * weight[..., None], 0) / total[..., None]
        lse_tok = top + jnp.log(total)
        o_heads = o_tok.reshape(share, head_size, cols).transpose(1, 0, 2).astype(bf16)
        l_heads = split_three(lse_tok.reshape(share, head_size, heads_dev).transpose(1, 0, 2))
        pay = lax.all_to_all(jnp.concatenate([o_heads, l_heads], 2), "head", 0, 0, tiled=True)
        lse_tok = join_three(pay[..., cols:])
        o_tok = pay[..., :cols].astype(f32).reshape(head_size, share, heads_dev, HEAD_SIZE)
        first_row = lax.rem(f * share, lat_count)
        q_rows = lax.dynamic_slice_in_dim(query, first_row, share, 0).reshape(
            share, heads_dev, HEAD_SIZE
        )
        lat_scores = (
            jnp.einsum("rnd,jnd->rnj", q_rows, lat_key, preferred_element_type=f32) * scale
        )
        lse = jnp.logaddexp(lse_tok, jax.nn.logsumexp(lat_scores, -1)[None])
        lat_prob = jnp.exp(lat_scores[None] - lse[..., None])
        attn = o_tok * jnp.exp(lse_tok - lse)[..., None] + jnp.einsum(
            "srnj,jnd->srnd", lat_prob, lat_value.astype(f32), precision=HIGH_ACCURACY
        )
        rows = head_size * share
        attn_low = attn.reshape(rows, cols).astype(bf16)

    with jax.named_scope("latent_forward"):
        lat_rows = jnp.tile(lax.dynamic_slice_in_dim(latents, first_row, share, 0), (head_size, 1))
        z_one = lat_rows + sum_head(nt(attn_low, w_outt))
        z1hat, z1rstd = normalize_rows(z_one)
        ffn_in = (z1hat * gains[2]).astype(bf16)
        pre = nn(ffn_in, w_up)
        hidden = jax.nn.gelu(pre).astype(bf16)
        z_two = z_one + sum_head(nt(hidden, w_downt))
        z2hat, z2rstd = normalize_rows(z_two)
        final = (z2hat * gains[3]).astype(bf16)
        dec = jnp.concatenate([nn(final, w_query), nn(final, w_dec)], 1).astype(bf16)

    def to_tokens(x):
        x = lax.all_to_all(x.reshape(head_size, share, -1), "head", 0, 0, tiled=True)
        x = x.transpose(1, 0, 2)
        x = jnp.broadcast_to(x[None], (frame_size,) + x.shape)
        x = lax.all_to_all(x, "frame", 0, 0, tiled=True)
        return x.reshape(videos_dev * lat_count, head_size, -1)

    with jax.named_scope("decode"):
        dec_all = to_tokens(dec)
        dq_all = dec_all[..., :cols].reshape(videos_dev * lat_count, depth)
        dv_all = dec_all[..., cols:].reshape(videos_dev * lat_count, depth)
        own_mask = lax.dynamic_slice_in_dim(loss_mask, h * videos_dev, videos_dev, 0).astype(f32)
        counts = own_mask.reshape(videos_dev * tokens_video, 1)
        decoded = decode_pass(xn_all, ft_all, counts, dq_all, dv_all, w_key, scale, videos_dev)
        loss_part = jnp.sum(decoded[4])
        count_part = jnp.sum(own_mask)
        dec_side = jnp.sum(decoded[3], 0)

    with jax.named_scope("latent_backward"):
        ddec = jnp.concatenate(
            [
                decoded[n].reshape(frame_size, share, head_size, cols)
                for n in (0, 1)
            ],
            3,
        ).astype(bf16)
        ddec = to_frames(ddec.reshape(frame_size, share, -1)).astype(f32)
        ddec = jnp.sum(ddec, 0).astype(bf16).reshape(share, head_size, 2 * cols).transpose(1, 0, 2)
        ddec = lax.all_to_all(ddec, "head", 0, 0, tiled=True).reshape(rows, 2 * cols)
        ddq_low, ddv_low = (ddec[:, :cols], ddec[:, cols:])
        dfinal = sum_head(nt(ddq_low, w_query) + nt(ddv_low, w_dec))
        dz_two = norm_reverse(dfinal, z2hat, z2rstd, gains[3])
        dz2_low = dz_two.astype(bf16)
        _, gelu_back = jax.vjp(jax.nn.gelu, pre)
        dpre = gelu_back(nn(dz2_low, w_downt))[0].astype(bf16)
        dffn_in = sum_head(nt(dpre, w_up))
        dz_one = dz_two + norm_reverse(dffn_in, z1hat, z1rstd, gains[2])
        dz1_low = dz_one.astype(bf16)
        dattn = nn(dz1_low, w_outt).astype(bf16)
        dattn_heads = dattn.astype(f32).reshape(head_size, share, heads_dev, HEAD_SIZE)
        delta = jnp.sum(dattn_heads * attn, -1)
        pay = jnp.concatenate(
            [
                dattn,
                split_three(lse.reshape(rows, heads_dev)),
                split_three(delta.reshape(rows, heads_dev)),
            ],
            1,
        )
        pay = to_tokens(pay)
        do_all = pay[..., :cols].reshape(videos_dev * lat_count, depth)

        both = join_three(pay[..., cols:].reshape(-1, head_size, 2, 3 * heads_dev))
        both = both.transpose(0, 2, 1, 3).reshape(videos_dev * lat_count, 2 * heads)
        ld = jnp.pad(both, ((0, 0), (0, 128 - 2 * heads)))

    with jax.named_scope("latent_pairs"):
        lat_value_f = lat_value.astype(f32)
        lat_dprob = jnp.einsum("srnd,jnd->srnj", dattn_heads, lat_value_f, precision=HIGH_ACCURACY)
        lat_dscore = lat_prob * (lat_dprob - delta[..., None]) * scale
        dq_lat = jnp.einsum(
            "srnj,jnd->rnd", lat_dscore, lat_key.astype(f32), precision=HIGH_ACCURACY
        ).reshape(share, cols)
        dk_lat = jnp.einsum(
            "srnj,rnd->jnd", lat_dscore, q_rows.astype(f32), precision=HIGH_ACCURACY
        ).reshape(lat_count, cols)
        dv_lat = jnp.einsum(
            "srnj,srnd->jnd", lat_prob, dattn_heads, precision=HIGH_ACCURACY
        ).reshape(lat_count, cols)
        dk_lat_low = dk_lat.astype(bf16)
        dv_lat_low = dv_lat.astype(bf16)
        pairs = jnp.concatenate([dk_lat, dv_lat], 0)
        lat_part = jnp.concatenate(
            [
                jnp.sum(dz_one.reshape(head_size, share, depth), 0),
                jnp.sum(dffn_in * z1hat, 0)[None],
                jnp.sum(dfinal * z2hat, 0)[None],
                jnp.zeros((6, depth), f32),
            ],
            0,
        )
        lat_parts = lax.all_gather(lat_part, "frame")
        lat_direct = jnp.sum(
            lat_parts[:, :share].reshape(videos_dev, lat_count, depth), 0
        )
        gain_rows = jnp.sum(lat_parts[:, share : share + 2], 0)

    with jax.named_scope("row_gradients"):
        wide_a = lax.all_gather(
            jnp.concatenate([hidden, attn_low], 1), "frame", axis=0, tiled=True
        )
        wide_b = lax.all_gather(
            jnp.concatenate([dpre, ddq_low, ddv_low], 1), "frame", axis=0, tiled=True
        )

        own_cols = jnp.stack(
            [a.reshape(rows, frame_size, rows_dev) for a in (ffn_in, final, dz2_low, dz1_low)]
        ).transpose(2, 0, 1, 3)
        own_cols = lax.all_to_all(own_cols, "frame", 0, 0, tiled=True)

    with jax.named_scope("value"):
        ow, dwv_own, dwv_other, value_side = value_pass(do_all, w_value, px_all, st_all, ld, h, videos_dev)
        side = dec_side + jnp.concatenate(
            [value_side[:TAIL], jnp.zeros((TAIL, depth), f32), value_side[TAIL:]], 0
        )

    half = head_size // 2
    back = functools.partial(
        back_pass, e_all=e_all, ld=ld, ow=ow, qw=qw, q_all=q_all, wk=w_key, dq_all=dq_all,
        dx_all=decoded[2], scale=scale, h=h, videos_dev=videos_dev,
    )

    with jax.named_scope("value_gradient"):
        dwv = dwv_own.astype(f32) + swap(dwv_other, "head", 1).astype(f32)
        dwv_pay = dwv[1].astype(bf16)
        dwv_far = swap(dwv_pay, "head", 2)

    with jax.named_scope("back"):
        xn_all = gate(xn_all, dwv_pay)
        far_dq, far_near, far_away, far_side = back(
            True, xn_all, st_all=st_all, sides=None, gain=None
        )

    with jax.named_scope("value_gradient"):
        dwv = dwv[0] + dwv_far.astype(f32) + tn(dv_lat_low, normed_lat)
        dwv = dwv.T.reshape(frame_size // 2, 2, rows_dev, cols)
        dwv_away = lax.dynamic_index_in_dim(dwv, 1 - (f & 1), 1, False).astype(bf16)
        dwv_near = lax.dynamic_index_in_dim(dwv, f & 1, 1, False)
        dwv_x = swap(dwv_away, "frame", 1)

    with jax.named_scope("key_gradient"):
        far_sum = far_near.astype(f32) + swap(far_away, "head", 1).astype(f32)
        dq_sum = far_dq[0] + swap(far_dq[1], "head", 1)
        dwk_pay = far_sum.astype(bf16)
        dwk_far = swap(dwk_pay, "head", 2)
        dq_far = swap(dq_sum, "head", 2)

    with jax.named_scope("back"):
        xn_all = gate(xn_all, dwk_pay, dq_sum, dwv_away)
        own_dq, own_near, own_away, pack = back(
            False, xn_all, st_all=st_all, sides=[side, far_side],
            gain=gains[0:1],
        )

    with jax.named_scope("value_gradient"):
        grad_value = scatter_deep(dwv_near + dwv_x.astype(f32))

    with jax.named_scope("key_gradient"):
        key_sum = own_near.astype(f32) + swap(own_away, "head", 1).astype(f32)
        key_sum = key_sum + dwk_far.astype(f32) + tn(dk_lat_low, normed_lat)
        key_sum = key_sum.T.reshape(frame_size // 2, 2, rows_dev, cols)
        key_away = lax.dynamic_index_in_dim(key_sum, 1 - (f & 1), 1, False).astype(bf16)
        key_near = lax.dynamic_index_in_dim(key_sum, f & 1, 1, False)
        key_away = gate(key_away, grad_value)
        own_cols = gate(own_cols, key_away)
        sq = functools.partial(turn, rows=rows_dev, cols=cols, left=left, right=right_sq)
        ffn = functools.partial(turn, rows=rows_dev, cols=hid, left=left, right=right_ffn)
        turned_up = ffn(5, 0, (own_cols, 0, wide_b, 0))
        turned_down = ffn(6, 1, (own_cols, 2, wide_a, 0))
        key_half = key_near + swap(key_away, "frame", 1).astype(f32)
        key_half = gate(key_half, turned_up[1], turned_down[1])
        key_low = key_half.astype(bf16)
        key_sends = [
            lax.dynamic_index_in_dim(key_low, (f >> 1) ^ d, 0, False)
            for d in range(1, frame_size // 2)
        ]

    with jax.named_scope("patch_gradients"):
        dq_pad = lax.dynamic_update_slice_in_dim(
            jnp.zeros((lat_count, cols), f32), dq_lat, first_row, 0
        )
        dquery = own_dq[0] + swap(own_dq[1], "head", 1) + dq_far + dq_pad
        dquery = jnp.concatenate([dquery + zero_of(key_away).astype(f32), pairs], 0)
        dquery = gate(sum_rounded(dquery, "frame").astype(bf16), *key_sends)
        dquery, dk_sum, dv_sum = (
            dquery[n * lat_count : (n + 1) * lat_count] for n in range(3)
        )

    with jax.named_scope("key_gradient"):
        grad_key = lax.dynamic_index_in_dim(key_half, f >> 1, 0, False)
        for d, send in enumerate(key_sends):
            grad_key = grad_key + swap(send, "frame", 2 * (d + 1)).astype(f32)

    with jax.named_scope("patch_gradients"):
        pack = sum_near(pack[:half], pack[half:])
        time_own = pack[:frames_dev]
        gain0_own = sum_over(jnp.sum(pack[TAIL:], 0)[None], "frame")[0]
        dzn = sum_head(nt(dquery, w_query) + nt(dk_sum, w_key_own) + nt(dv_sum, w_value_own))
        grad_gain1 = jnp.sum(dzn * zhat_zero, 0)
        lat_grad = lat_direct + norm_reverse(dzn, zhat_zero, zrstd_zero, gains[1])
        gain_rest = jnp.concatenate([grad_gain1[None], gain_rows], 0)
        gain_grad = jnp.concatenate(
            [gain0_own[None], lax.dynamic_slice_in_dim(gain_rest, h * cols, cols, 1)], 0
        )

    with jax.named_scope("update"):
        turned, totals = zip(
            sq(0, 0, (own_cols, 1, wide_b, hid, normed_own, dquery)),
            sq(1, 1, (grad_key,)),
            sq(2, 2, (grad_value,)),
            sq(3, 3, (own_cols, 3, wide_a, hid)),
            sq(4, 4, (own_cols, 1, wide_b, hid + cols)),
            turned_up,
            turned_down,
        )
        squares = (
            jnp.sum(sum(totals))
            + jnp.sum(time_own * time_own)
            + first_frame * first_head * jnp.sum(lat_grad * lat_grad)
            + first_frame * jnp.sum(gain_grad * gain_grad)
        )
        sums = jnp.pad(jnp.stack([loss_part, count_part, squares])[None], ((0, 7), (0, 125)))
        sums = sum_over(sum_over(sums, "head"), "frame")
        loss_sum, masked_count, squares = (sums[0, 0], sums[0, 1], sums[0, 2])
        grad_norm = jnp.sqrt(squares) / masked_count
        factor = jnp.minimum(1.0, clip_max / grad_norm) / masked_count
        out_rate = ((FRAMES * PATCH + LATENTS) / 64.0) ** 0.5
        ffn_out = update(
            factor[None], ffn_weight, ffn_first, ffn_second, 5, left, right_ffn, turned[5:],
            (0.02, 0.02),
        )
        sq_out = update(
            factor[None], sq_weight, sq_first, sq_second, 0, left, right_sq, turned[:5],
            (0.02, 0.02, 0.02, 0.02 * out_rate, 0.02),
        )
        lat_out = adamw_update(latents, lat_grad * factor, lat_first, lat_second, 0.01)
        time_out = adamw_update(time_embed, time_own * factor, time_first, time_second, 0.01)
        gain_own = lax.dynamic_slice_in_dim(gains, h * cols, cols, 1)
        gain_out = adamw_update(gain_own, gain_grad * factor, gain_first, gain_second, 0.0)
    return (loss_sum, masked_count, grad_norm, *sq_out, *ffn_out, *lat_out, *time_out, *gain_out)


def solution(mesh):
    matrix = P(None, "frame", "head")
    frame_rows = P("frame", "head")
    by_head = P(None, "head")
    placed = (
        P(None, "frame", None, "head"),
        P(None, "frame"),
        P(None, "frame", None),
        matrix, matrix, matrix, matrix, matrix, matrix,
        P(None, "frame", None, None),
        P(None, "head", None, None),
        P(None, "head", None, None),
        P(), P(), P(),
        frame_rows, frame_rows, frame_rows,
        P(), by_head, by_head,
    )
    outs = (
        P(), P(), P(),
        matrix, matrix, matrix, matrix, matrix, matrix, matrix, matrix,
        P(), P(), P(),
        frame_rows, frame_rows, frame_rows,
        by_head, by_head, by_head,
    )
    return jax.shard_map(per_device, mesh=mesh, in_specs=placed, out_specs=outs, check_vma=False)
```
